32 devices in a mesh: batch: 8 (over z, y), expert: 4 (over x, core).
Axes of the slice: x: 2, y: 2, z: 4, core: 2. Of those that a mesh axis runs over, the one named last changes fastest.
Arguments:
- tokens: bfloat16 [4096, 768], P(('batch', 'expert')), may hold values from -6 to 6
- cond: bfloat16 [32, 768], P(('batch', 'expert')), may hold values from -6 to 6
- lengths: int32 [32], P(('batch', 'expert')), may hold values from 32 to 128, as said below
- routes: int32 [4096, 2], P(('batch', 'expert')), may hold values from 0 to 3, all different within a row
- gate_weights: float32 [4096, 2], P(('batch', 'expert')), may hold values from 0.2 to 1
- ada_weight: bfloat16 [768, 4608], P(('batch', 'expert')), may hold values from -0.21875 to 0.21875
- ada_bias: bfloat16 [4608], P(('batch', 'expert')), may hold values from -3 to 3
- qkv_weight: bfloat16 [768, 2304], P(('batch', 'expert')), may hold values from -0.21875 to 0.21875
- out_weight: bfloat16 [768, 768], P(('batch', 'expert')), may hold values from -0.875 to 0.875
- shared_up: bfloat16 [768, 3072], P(('batch', 'expert')), may hold values from -0.21875 to 0.21875
- shared_down: bfloat16 [3072, 768], P(('batch', 'expert')), may hold values from -0.109375 to 0.109375
- expert_up: bfloat16 [4, 768, 3072], P('expert', 'batch'), may hold values from -0.21875 to 0.21875
- expert_down: bfloat16 [4, 3072, 768], P('expert', 'batch'), may hold values from -0.109375 to 0.109375
- cotangent: bfloat16 [4096, 768], P(('batch', 'expert')), may hold values from -6 to 6
Outputs:
- block_out: float32 [4096, 768], P(('batch', 'expert'))
- grad_tokens: float32 [4096, 768], P(('batch', 'expert'))
- grad_cond: float32 [32, 768], P(('batch', 'expert'))
- grad_gate_weights: float32 [4096, 2], P(('batch', 'expert'))
- grad_ada_weight: float32 [768, 4608], P('batch', 'expert')
- grad_ada_bias: float32 [4608], replicated
- grad_qkv_weight: float32 [768, 2304], P('batch', 'expert')
- grad_out_weight: float32 [768, 768], P('batch', 'expert')
- grad_shared_up: float32 [768, 3072], P('batch', 'expert')
- grad_shared_down: float32 [3072, 768], P('batch', 'expert')
- grad_expert_up: float32 [4, 768, 3072], P('expert', 'batch')
- grad_expert_down: float32 [4, 3072, 768], P('expert', 'batch')
- expert_load: float32 [4], replicated
The draws below stay inside these ranges and needn't reach their ends.
Inputs may be any that keep to these rules, and one draw needn't show every extreme that they name: `lengths`: every item holds 128 or 32 valid patches at its start; both occur in every draw. `routes`: the two experts of a patch slot differ.
All inputs are finite; a program needn't handle non-finite values.
Results may differ from the reference program's by a relative error of at most 0.017.
The reference program's roundings to bfloat16 on the way count: a program that leaves them out, or rounds other values in their place, can miss the bound.
Values may be sent and summed in bfloat16 or wider, within the bound.
No kernel may reach another device: no remote copies, remote signals or barrier semaphores. Data moves between devices by JAX's collectives and lax.ppermute only.
A program may use at most 128 MiB of HBM per device.

```python
import math
import jax
import jax.numpy as jnp
from jax import lax

D = 768
HEADS = 12
HEAD_DIM = 64
FF = 3072
TOP = 2
LEN = 128
EXPERTS = 4
ITEMS = 32
TOKENS = 4096
CAP = 80


def draw_lengths(key, part):
    key = jax.random.fold_in(key, 11)
    pick_key, place_key = jax.random.split(key)
    picks = jax.random.randint(pick_key, (ITEMS,), 0, 4)
    values = jnp.where(picks == 0, LEN // 4, LEN).astype(jnp.int32)
    order = jax.random.permutation(place_key, ITEMS)
    values = values.at[order[0]].set(LEN).at[order[1]].set(LEN // 4)
    return values.astype(jnp.int32)


def level_of(key, dims, cuts, low, largest):
    def one(axis_at, shards_of):
        steps = jax.random.uniform(jax.random.fold_in(jax.random.fold_in(key, 6), axis_at), (shards_of,), jnp.float32, low / len(cuts), largest / len(cuts))
        return jnp.repeat(jnp.exp(steps), dims[axis_at] // shards_of).reshape((-1,) + (1,) * (len(dims) - axis_at - 1))

    loudness = one(*cuts[0])
    for cut in cuts[1:]:
        loudness = loudness * one(*cut)
    return loudness


def choose_distinct(key, rows, count, top, lift):
    order = jax.random.permutation(jax.random.fold_in(key, 1), count)
    pull = order
    for power in range(3):
        pull = pull * pull // count
    pull = pull * lift // count
    chance = jax.random.randint(jax.random.fold_in(key, 2), (rows, count), 0, 4096) + pull
    fixed_rows = jax.random.permutation(jax.random.fold_in(key, 3), rows)[jnp.arange(count) % rows]
    chance = jnp.where(jnp.arange(rows)[:, None] == fixed_rows[None, :], 1 << 14, chance)
    priority = chance * count + jnp.arange(count)
    return lax.top_k(priority.astype(jnp.int32), top)[1].astype(jnp.int32)


def normal_values(stream_key, extent, scale, limit, shards=(), kind=jnp.bfloat16):
    gain = level_of(stream_key, extent, shards, -0.22, 0.18) if shards else 1.0
    entries = jax.random.normal(stream_key, extent, jnp.float32) * scale * gain
    return jnp.minimum(jnp.maximum(entries, -limit), limit).astype(kind)


def setup_inputs(seed: int = 0) -> dict:
    key_of = jax.random.split(jax.random.key(seed), 15)
    tokens = normal_values(key_of[0], (TOKENS, D), 1.0, 6.0, ((0, 32),))
    cond = normal_values(key_of[1], (ITEMS, D), 1.0, 6.0, ((0, 32),))
    lengths = draw_lengths(jax.random.fold_in(key_of[14], 71), 0)
    routes = choose_distinct(key_of[3], TOKENS, EXPERTS, TOP, 4096)
    gate_weights = jnp.clip(jnp.exp(math.log(1.0) - 1.609438 * jax.random.uniform(key_of[4], (TOKENS, TOP), jnp.float32) ** level_of(key_of[4], (TOKENS, TOP), ((0, 32),), -0.2, 0.2)), 0.2, 1.0)
    ada_weight = normal_values(key_of[5], (D, 6 * D), D ** -0.5, 0.21875, ((0, 32),))
    ada_bias = normal_values(key_of[6], (6 * D,), 0.5, 3.0, ((0, 32),))
    qkv_weight = normal_values(key_of[7], (D, 3 * D), D ** -0.5, 0.21875, ((0, 32),))
    out_weight = normal_values(key_of[8], (D, D), (D // 16) ** -0.5, 0.875, ((0, 32),))
    shared_up = normal_values(key_of[9], (D, FF), D ** -0.5, 0.21875, ((0, 32),))
    shared_down = normal_values(key_of[10], (FF, D), FF ** -0.5, 0.109375, ((0, 32),))
    expert_up = normal_values(key_of[11], (EXPERTS, D, FF), D ** -0.5, 0.21875, ((0, 4), (1, 8)))
    expert_down = normal_values(key_of[12], (EXPERTS, FF, D), FF ** -0.5, 0.109375, ((0, 4), (1, 8)))
    cotangent = normal_values(key_of[13], (TOKENS, D), 1.0, 6.0, ((0, 32),))
    return dict(tokens=tokens, cond=cond, lengths=lengths, routes=routes, gate_weights=gate_weights, ada_weight=ada_weight, ada_bias=ada_bias, qkv_weight=qkv_weight, out_weight=out_weight, shared_up=shared_up, shared_down=shared_down, expert_up=expert_up, expert_down=expert_down, cotangent=cotangent)


@jax.custom_vjp
def low(v):
    return lax.optimization_barrier(v.astype(jnp.bfloat16)).astype(jnp.float32)

@jax.custom_vjp
def low_back(v):
    return v

def low_keep(v):
    return (low(v), None)

def low_pass(kept, grad):
    return (grad,)

def back_keep(v):
    return (v, None)

def back_low(kept, grad):
    return (low(grad),)
low.defvjp(low_keep, low_pass)
low_back.defvjp(back_keep, back_low)

def normalize(values):
    center = values - lax.optimization_barrier(jnp.mean(values, axis=-1, keepdims=True))
    spread = lax.optimization_barrier(jnp.mean(center * center, axis=-1, keepdims=True))
    return center * lax.rsqrt(spread + 1e-06)

def modulate_norm(values, shift, scale):
    return normalize(values) * (1.0 + scale) + shift

def gelu_tanh(values):
    return jax.nn.gelu(values, approximate=True)

def slot_table(routes, length):
    live = jnp.arange(LEN).astype(jnp.int32) < length
    chosen = routes.reshape(-1).astype(jnp.int32)
    live_pairs = jnp.repeat(live, 2)
    hits = ((chosen[:, None] == jnp.arange(EXPERTS).astype(jnp.int32)[None, :]) & live_pairs[:, None]).astype(jnp.int32)
    before = (jnp.cumsum(hits, axis=0) - hits).astype(jnp.int32)
    slot = lax.optimization_barrier(jnp.sum(before * hits, axis=1)).astype(jnp.int32)
    kept = live_pairs & (slot < CAP)
    target = jnp.where(kept, chosen * CAP + slot, -1).astype(jnp.int32)
    return (target.reshape(LEN, 2), kept.reshape(LEN, 2))

def block(params, tok_rows, cond_row, gate_rows, route_rows, length):
    ada_w, ada_b, qkv_w, out_w, up_w, down_w, exp_up, exp_down = params
    highest = lax.Precision.HIGHEST
    cond_act = low(jax.nn.silu(cond_row))
    modulation = low_back(jnp.dot(cond_act, ada_w, precision=highest) + ada_b)
    shift1, scale1, gate1, shift2, scale2, gate2 = jnp.split(modulation, 6)
    first = low(modulate_norm(tok_rows, shift1, scale1))
    joined = low(low_back(jnp.dot(first, qkv_w, precision=highest)))
    queries = joined[:, :D].reshape(LEN, HEADS, HEAD_DIM)
    keys = joined[:, D:2 * D].reshape(LEN, HEADS, HEAD_DIM)
    values = joined[:, 2 * D:].reshape(LEN, HEADS, HEAD_DIM)
    scores = jnp.einsum('qhd,khd->hqk', queries, keys, precision=highest) * HEAD_DIM ** (-0.5)
    live_keys = jnp.arange(LEN).astype(jnp.int32) < length
    scores = low_back(jnp.where(live_keys[None, None, :], scores, -1e+30))
    top_score = lax.optimization_barrier(jnp.max(scores, axis=-1, keepdims=True))
    log_total = top_score + jnp.log(lax.optimization_barrier(jnp.sum(jnp.exp(scores - top_score), axis=-1, keepdims=True)))
    probs = low(jnp.exp(scores - log_total))
    attended = jnp.einsum('hqk,khd->qhd', probs, values, precision=highest).reshape(LEN, D)
    attended = low(low_back(attended))
    attn = low_back(jnp.dot(attended, out_w, precision=highest))
    middle = tok_rows + gate1 * attn
    second = low(modulate_norm(middle, shift2, scale2))
    shared_pre = low_back(jnp.dot(second, up_w, precision=highest))
    shared = low_back(jnp.dot(low(gelu_tanh(shared_pre)), down_w, precision=highest))
    target, kept = slot_table(route_rows, length)
    slot_ids = jnp.arange(EXPERTS * CAP).astype(jnp.int32)
    select = lax.optimization_barrier(jnp.sum((target[None, :, :] == slot_ids[:, None, None]).astype(jnp.float32), axis=2))
    dispatch = low_back(jnp.dot(select, second, precision=highest)).reshape(EXPERTS, CAP, D)
    expert_pre = low_back(jnp.einsum('ecd,edf->ecf', dispatch, exp_up, precision=highest))
    expert_hidden = low(gelu_tanh(expert_pre))
    expert_rows = low(low_back(jnp.einsum('ecf,efd->ecd', expert_hidden, exp_down, precision=highest)))
    expert_rows = expert_rows.reshape(EXPERTS * CAP, D)
    picked = jnp.take(expert_rows, jnp.clip(target, 0, EXPERTS * CAP - 1), axis=0)
    weights = gate_rows * kept.astype(jnp.float32)
    routed = weights[:, 0:1] * picked[:, 0] + weights[:, 1:2] * picked[:, 1]
    return middle + gate2 * (shared + routed)

def reference(tokens, cond, lengths, routes, gate_weights, ada_weight, ada_bias, qkv_weight, out_weight, shared_up, shared_down, expert_up, expert_down, cotangent):
    params = tuple((weight.astype(jnp.float32) for weight in (ada_weight, ada_bias, qkv_weight, out_weight, shared_up, shared_down, expert_up, expert_down)))
    tok_items = tokens.astype(jnp.float32).reshape(ITEMS, LEN, D)
    cond_items = cond.astype(jnp.float32)
    gate_items = gate_weights.astype(jnp.float32).reshape(ITEMS, LEN, 2)
    route_items = routes.reshape(ITEMS, LEN, 2)

    def forward(weights, tok_all, cond_all, gate_all):

        def single(entry):
            return block(weights, entry[0], entry[1], entry[2], entry[3], entry[4])
        return lax.map(jax.checkpoint(single), (tok_all, cond_all, gate_all, route_items, lengths))
    outputs, pullback = jax.vjp(forward, params, tok_items, cond_items, gate_items)
    grad_params, grad_tok, grad_cnd, grad_gate = pullback(cotangent.astype(jnp.float32).reshape(ITEMS, LEN, D))
    live = jnp.arange(LEN).astype(jnp.int32)[None, :] < lengths[:, None]
    hits = (route_items[:, :, :, None] == jnp.arange(EXPERTS).astype(jnp.int32)) & live[:, :, None, None]
    counts = lax.optimization_barrier(jnp.sum(hits.astype(jnp.float32), axis=(0, 1, 2)))
    expert_load = counts * EXPERTS / (2.0 * jnp.sum(lengths.astype(jnp.float32)))
    return (outputs.reshape(TOKENS, D), grad_tok.reshape(TOKENS, D), grad_cnd, grad_gate.reshape(TOKENS, 2), grad_params[0], grad_params[1], grad_params[2], grad_params[3], grad_params[4], grad_params[5], grad_params[6], grad_params[7], expert_load)
```

```python
import jax
import jax.numpy as jnp
from jax import lax
from jax.sharding import PartitionSpec as P

HEADS = 12
HEAD_DIM = 64
AXES = ("batch", "expert")
LOW = jnp.bfloat16
WIDE = jnp.float32


def dot(left, right):
    return jnp.dot(left, right, preferred_element_type=WIDE)


def dot_nt(left, right):
    return lax.dot_general(left, right, (((1,), (1,)), ((), ())), preferred_element_type=WIDE)


def dot_tn(left, right):
    return lax.dot_general(left, right, (((0,), (0,)), ((), ())), preferred_element_type=WIDE)


def bits_of(count):
    found = []
    step = 1
    while step < count:
        found.append(step)
        step *= 2
    assert step == count
    return found


def swap(values, mask):
    total = lax.axis_size("batch") * lax.axis_size("expert")
    return lax.ppermute(values, AXES, [(at, at ^ mask) for at in range(total)])


def spread(values, masks):
    for mask in masks:
        values = jnp.concatenate([values, swap(values, mask)], axis=0)
    return values


def order(masks):
    found = [0]
    for mask in masks:
        found = found + [at ^ mask for at in found]
    return found


def fold(values, masks):
    for mask in reversed(masks):
        half = values.shape[0] // 2
        got = swap(values[half:], mask)
        values = (values[:half].astype(WIDE) + got.astype(WIDE)).astype(values.dtype)
    return values


def normalize(values):
    center = values - jnp.mean(values, axis=-1, keepdims=True)
    spread_ = jnp.mean(center * center, axis=-1, keepdims=True)
    return center * lax.rsqrt(spread_ + 1e-06)


def modulate_norm(values, shift, scale):
    return normalize(values) * (1.0 + scale) + shift


def gelu_tanh(values):
    return jax.nn.gelu(values, approximate=True)


def slot_table(routes, length, experts, capacity):
    count = routes.shape[0]
    live = jnp.arange(count, dtype=jnp.int32) < length
    chosen = routes.reshape(-1)
    live_pairs = jnp.repeat(live, 2)
    hits = (
        (chosen[:, None] == jnp.arange(experts, dtype=jnp.int32)[None, :]) & live_pairs[:, None]
    ).astype(jnp.int32)
    before = jnp.cumsum(hits, axis=0) - hits
    slot = jnp.sum(before * hits, axis=1)
    kept = live_pairs & (slot < capacity)
    return kept.reshape(count, 2), jnp.sum(hits, axis=0)


def attention_scores(queries, keys, live_keys, factor):
    raw = jnp.einsum("qhd,khd->hqk", queries, keys, preferred_element_type=WIDE) * factor
    return jnp.where(live_keys[None, None, :], raw, -1e30)


def pad_lanes(values, width):
    return jnp.pad(values, ((0, 0),) * (values.ndim - 1) + ((0, width - values.shape[-1]),))


def shards(
    tokens,
    cond,
    lengths,
    routes,
    gate_weights,
    ada_weight,
    ada_bias,
    qkv_weight,
    out_weight,
    shared_up,
    shared_down,
    expert_up,
    expert_down,
    cotangent,
):
    count, width = tokens.shape
    experts = lax.axis_size("expert")
    groups = lax.axis_size("batch")
    total = experts * groups
    me = lax.axis_index(AXES)
    my_expert = lax.axis_index("expert")
    my_group = lax.axis_index("batch")
    capacity = 5 * 2 * count // (4 * experts)
    factor = HEAD_DIM ** (-0.5)
    length = lengths[0]
    piece = ada_weight.shape[0]

    expert_masks = bits_of(experts)
    group_masks = [experts * step for step in bits_of(groups)]
    near_masks, far_masks = group_masks[:2], group_masks[2:]
    all_masks = list(reversed(group_masks)) + list(reversed(expert_masks))
    team_masks = near_masks + list(reversed(expert_masks))
    team = 1
    for _ in team_masks:
        team *= 2

    kept, hits = slot_table(routes, length, experts, capacity)
    kept_wide = kept.astype(WIDE)
    weights = gate_weights * kept_wide
    chosen = (routes[:, :, None] == jnp.arange(experts, dtype=jnp.int32)).astype(WIDE)
    weight_of = jnp.sum(weights[:, :, None] * chosen, axis=1)
    weight_high = weight_of.astype(LOW)
    weight_low = (weight_of - weight_high.astype(WIDE)).astype(LOW)

    cond_row = cond.astype(WIDE)
    cond_act, silu_back = jax.vjp(jax.nn.silu, cond_row)
    side = jnp.concatenate([hits.astype(LOW), lengths.astype(LOW)])[None, :]
    cond_all = spread(jnp.concatenate([cond_act.astype(LOW), pad_lanes(side, 128)], axis=1), all_masks)
    tallies = jnp.sum(cond_all[:, width:].astype(WIDE), axis=0)
    expert_load = tallies[:experts] * experts / (2.0 * tallies[experts])
    cond_all = cond_all[:, :width]
    cond_mine = lax.dynamic_slice(cond_all, (0, me * piece), (total, piece))
    bias_mine = lax.dynamic_update_slice(
        jnp.zeros((ada_weight.shape[1],), WIDE), ada_bias.astype(WIDE), (me * ada_bias.shape[0],)
    )
    modulation = fold(dot(cond_mine, ada_weight) + bias_mine[None, :], all_masks)
    shift1, scale1, gate1, shift2, scale2, gate2 = jnp.split(modulation, 6, axis=1)

    attn_w = spread(jnp.concatenate([qkv_weight, out_weight], axis=1)[None], all_masks)
    attn_w = attn_w.reshape(width, 4 * width)
    rows = ((me ^ jnp.array(order(all_masks), jnp.int32))[:, None] * piece + jnp.arange(piece, dtype=jnp.int32)).reshape(-1)
    place = (jnp.arange(width, dtype=jnp.int32)[:, None] == rows[None, :]).astype(LOW)
    attn_w = dot(place, attn_w).astype(LOW)
    qkv_w, out_w = attn_w[:, : 3 * width], attn_w[:, 3 * width :]

    part_up = lax.all_to_all(expert_up[0], "batch", split_axis=1, concat_axis=0, tiled=True)
    part_shared_up = lax.all_to_all(shared_up, AXES, split_axis=1, concat_axis=0, tiled=True)
    units, shared_units = part_up.shape[1], part_shared_up.shape[1]
    wide = -(-(units + shared_units) // 128) * 128
    up_own = pad_lanes(jnp.concatenate([part_up, part_shared_up], axis=1), wide)
    down_own = jnp.concatenate([expert_down[0], shared_down], axis=0)
    down_own = jnp.pad(down_own, ((0, wide - units - shared_units), (0, 0)))
    both = spread(jnp.concatenate([up_own.reshape(-1, width), down_own], axis=0)[None], far_masks)
    replicas = both.shape[0]
    up_cat = both[:, : width * wide // width].reshape(replicas, width, wide)
    up_cat = jnp.concatenate([up_cat[at] for at in range(replicas)], axis=1)
    down_cat = both[:, width * wide // width :].reshape(replicas * wide, width)
    routed_unit = (jnp.arange(replicas * wide) % wide < units)[None, :]

    grad = cotangent.astype(WIDE)
    d_mlp = gate2 * grad
    d_mlp_all = spread(
        jnp.concatenate([d_mlp.astype(LOW), pad_lanes(jnp.concatenate([weight_high, weight_low], axis=1), 128)], axis=1)[None],
        team_masks,
    ).reshape(team * count, width + 128)
    side_all = d_mlp_all[:, width:].astype(WIDE)
    d_mlp_all = d_mlp_all[:, :width]
    lane = jnp.arange(128, dtype=jnp.int32)[None, :]
    mine = (lane == my_expert) | (lane == my_expert + experts)
    weight_all = jnp.sum(jnp.where(mine, side_all, 0.0), axis=1, keepdims=True)
    unit_weight = jnp.where(routed_unit, weight_all, 1.0)

    tok_rows = tokens.astype(WIDE)
    first, first_back = jax.vjp(modulate_norm, tok_rows, shift1, scale1)
    first_low = first.astype(LOW)
    joined = dot(first_low, qkv_w).astype(LOW)
    queries = joined[:, :width].reshape(count, HEADS, HEAD_DIM)
    keys = joined[:, width : 2 * width].reshape(count, HEADS, HEAD_DIM)
    values = joined[:, 2 * width :].reshape(count, HEADS, HEAD_DIM)
    live_keys = jnp.arange(count, dtype=jnp.int32) < length
    scores = attention_scores(queries, keys, live_keys, factor)
    top_score = jnp.max(scores, axis=-1, keepdims=True)
    log_total = top_score + jnp.log(jnp.sum(jnp.exp(scores - top_score), axis=-1, keepdims=True))
    probs_low = jnp.exp(scores - log_total).astype(LOW)
    attended = jnp.einsum("hqk,khd->qhd", probs_low, values, preferred_element_type=WIDE)
    attended_low = attended.reshape(count, width).astype(LOW)
    attn = dot(attended_low, out_w)
    middle = tok_rows + gate1 * attn
    second, second_back = jax.vjp(modulate_norm, middle, shift2, scale2)
    second_low = second.astype(LOW)

    second_all = spread(second_low[None], team_masks).reshape(team * count, width)
    d_act = dot_nt(d_mlp_all, down_cat)
    pre = dot(second_all, up_cat)
    act, gelu_back = jax.vjp(gelu_tanh, pre)
    act_low = act.astype(LOW)
    d_pre = (gelu_back(d_act)[0] * unit_weight).astype(LOW)
    d_second_part = dot_nt(d_pre, up_cat).astype(LOW)
    d_second = fold(d_second_part.reshape(team, count, width), team_masks)[0].astype(WIDE)
    act_weighted = (act_low.astype(WIDE) * unit_weight).astype(LOW)
    branch_part = dot(act_weighted, down_cat).astype(LOW)
    pair_part = jnp.sum(jnp.where(routed_unit, act_low.astype(WIDE) * d_act, 0.0), axis=1, keepdims=True)
    pair_part = jnp.where(lane == my_expert, pair_part, 0.0).astype(LOW)
    branch_all = fold(
        jnp.concatenate([branch_part, pair_part], axis=1).reshape(team, count, width + 128), team_masks
    )[0].astype(WIDE)
    branch = branch_all[:, :width]
    pair_grads = branch_all[:, width : width + experts]
    grad_up_part = dot_tn(second_all, d_pre).astype(LOW)
    grad_down_part = dot_tn(act_weighted, d_mlp_all).astype(LOW)
    grads_part = jnp.concatenate(
        [
            jnp.stack([grad_up_part[:, at * wide : (at + 1) * wide] for at in range(replicas)]).reshape(replicas, -1, width),
            grad_down_part.reshape(replicas, wide, width),
        ],
        axis=1,
    )
    for mask in reversed(far_masks):
        half = grads_part.shape[0] // 2
        grads_part = grads_part[:half].astype(WIDE) + swap(grads_part[half:], mask).astype(WIDE)
        if half > 1:
            grads_part = grads_part.astype(LOW)
    grads_own = grads_part[0].astype(WIDE)
    grad_up_own = grads_own[: width * wide // width].reshape(width, wide)
    grad_down_own = grads_own[width * wide // width :]
    grad_expert_down = grad_down_own[:units][None]
    grad_shared_down = lax.all_to_all(
        grad_down_own[units : units + shared_units].astype(LOW), "expert", split_axis=1, concat_axis=0, tiled=True
    ).astype(WIDE)
    grad_up_own = grad_up_own[:, : units + shared_units].astype(LOW).reshape(groups, width // groups, -1)
    grad_up_rows = lax.all_to_all(grad_up_own, "batch", split_axis=0, concat_axis=0, tiled=True)
    grad_expert_up = (
        grad_up_rows[:, :, :units].transpose(1, 0, 2).reshape(1, width // groups, groups * units).astype(WIDE)
    )
    shared_rows = grad_up_rows[:, :, units:].reshape(experts, groups // experts, width // groups, shared_units)
    shared_rows = lax.all_to_all(shared_rows, "expert", split_axis=0, concat_axis=0, tiled=True)
    grad_shared_up = (
        shared_rows.transpose(2, 1, 0, 3).reshape(width // groups, groups * shared_units).astype(WIDE)
    )

    block_out = middle + gate2 * branch
    d_gate2 = jnp.sum(grad * branch, axis=0, keepdims=True)
    grad_gate_weights = jnp.sum(chosen * pair_grads[:, None, :], axis=2) * kept_wide
    d_middle_norm, d_shift2, d_scale2 = second_back(d_second)
    d_middle = grad + d_middle_norm
    d_gate1 = jnp.sum(d_middle * attn, axis=0, keepdims=True)
    d_attn = (gate1 * d_middle).astype(LOW)
    d_attended = dot_nt(d_attn, out_w).astype(LOW).reshape(count, HEADS, HEAD_DIM)
    scores_again = attention_scores(queries, keys, live_keys, factor)
    probs_again = jnp.exp(scores_again - log_total)
    probs_again_low = probs_again.astype(LOW)
    d_probs = jnp.einsum("qhd,khd->hqk", d_attended, values, preferred_element_type=WIDE)
    d_values = jnp.einsum("hqk,qhd->khd", probs_again_low, d_attended, preferred_element_type=WIDE)
    d_scores = probs_again * (d_probs - jnp.sum(probs_again * d_probs, axis=-1, keepdims=True))
    d_scores_low = d_scores.astype(LOW)
    d_queries = jnp.einsum("hqk,khd->qhd", d_scores_low, keys, preferred_element_type=WIDE) * factor
    d_keys = jnp.einsum("hqk,qhd->khd", d_scores_low, queries, preferred_element_type=WIDE) * factor
    d_joined = jnp.concatenate(
        [d_queries.reshape(count, width), d_keys.reshape(count, width), d_values.reshape(count, width)],
        axis=1,
    ).astype(LOW)
    d_first = dot_nt(d_joined, qkv_w)
    d_tok_norm, d_shift1, d_scale1 = first_back(d_first)
    grad_tokens = d_middle + d_tok_norm
    d_modulation = jnp.concatenate([d_shift1, d_scale1, d_gate1, d_shift2, d_scale2, d_gate2], axis=1).astype(LOW)

    d_mod_all = spread(d_modulation, all_masks)
    grad_ada_bias = jnp.sum(d_mod_all.astype(WIDE), axis=0)
    columns = d_mod_all.shape[1] // experts
    grad_ada_weight = dot_tn(
        lax.dynamic_slice(cond_all, (0, my_group * (width // groups)), (total, width // groups)),
        lax.dynamic_slice(d_mod_all, (0, my_expert * columns), (total, columns)),
    )
    d_cond_part = dot_nt(d_mod_all, ada_weight)
    d_cond_part = jnp.sum(
        jnp.where(
            ((me ^ jnp.array(order(all_masks), jnp.int32))[None, :] == jnp.arange(total, dtype=jnp.int32)[:, None])[:, :, None],
            d_cond_part[None],
            0.0,
        ),
        axis=1,
    )
    d_cond_act = lax.all_to_all(d_cond_part, AXES, split_axis=0, concat_axis=0, tiled=True).reshape(1, width)
    grad_cond = silu_back(d_cond_act)[0]

    rows_group = lax.all_gather(jnp.concatenate([first_low, attended_low], axis=1), "expert", axis=0, tiled=True)
    d_cols = jnp.concatenate(
        [d_joined.reshape(count, experts, -1), d_attn.reshape(count, experts, -1)], axis=2
    )
    d_cols = lax.all_to_all(d_cols, "expert", split_axis=1, concat_axis=0, tiled=True).reshape(experts * count, -1)
    wide_cols = 3 * width // experts
    term_qkv = dot_tn(rows_group[:, :width], d_cols[:, :wide_cols])
    term_out = dot_tn(rows_group[:, width:], d_cols[:, wide_cols:])
    terms = jnp.concatenate([term_qkv, term_out], axis=1).astype(LOW).reshape(groups, width // groups, -1)
    terms = lax.all_to_all(terms, "batch", split_axis=0, concat_axis=0, tiled=True)
    terms = jnp.sum(terms.astype(WIDE), axis=0)
    grad_qkv, grad_out = terms[:, :wide_cols], terms[:, wide_cols:]

    return (
        block_out,
        grad_tokens,
        grad_cond,
        grad_gate_weights,
        grad_ada_weight,
        grad_ada_bias,
        grad_qkv,
        grad_out,
        grad_shared_up,
        grad_shared_down,
        grad_expert_up,
        grad_expert_down,
        expert_load,
    )


def solution(mesh):
    rows = P(AXES, None)
    line = P(AXES)
    tiles = P("batch", "expert")
    split = P("expert", "batch", None)
    in_specs = (rows, rows, line, rows, rows, rows, line, rows, rows, rows, rows, split, split, rows)
    out_specs = (rows, rows, rows, rows, tiles, P(), tiles, tiles, tiles, tiles, split, split, P())
    return jax.shard_map(shards, mesh=mesh, in_specs=in_specs, out_specs=out_specs, check_vma=False)
```

```python
import functools

import jax
import jax.numpy as jnp
from jax import lax
from jax.experimental import pallas as pl
from jax.experimental.pallas import tpu as pltpu
from jax.sharding import PartitionSpec as P

HEADS = 12
HEAD_DIM = 64
AXES = ("batch", "expert")
LOW = jnp.bfloat16
WIDE = jnp.float32
LANES = 128
SHARES = (1, 2, 3)
CURVE = 0.7978845608028654
CUBIC = 0.044715


def dot(left, right):
    return lax.dot_general(left, right, (((1,), (0,)), ((), ())), preferred_element_type=WIDE)


def dot_nt(left, right):
    return lax.dot_general(left, right, (((1,), (1,)), ((), ())), preferred_element_type=WIDE)


def dot_tn(left, right):
    return lax.dot_general(left, right, (((0,), (0,)), ((), ())), preferred_element_type=WIDE)


def up_to(value, step):
    return -(-value // step) * step


def call(body, outs, args, scratch=(), smem=(), limit=48):
    specs = [
        pl.BlockSpec(memory_space=pltpu.SMEM if at in smem else pltpu.VMEM) for at in range(len(args))
    ]
    return pl.pallas_call(
        body,
        out_shape=[jax.ShapeDtypeStruct(shape, kind) for shape, kind in outs],
        in_specs=specs,
        out_specs=[pl.BlockSpec(memory_space=pltpu.VMEM)] * len(outs),
        scratch_shapes=[pltpu.VMEM(shape, kind) for shape, kind in scratch],
        compiler_params=pltpu.CompilerParams(vmem_limit_bytes=limit * 1024 * 1024),
    )(*args)


def sweep(body, steps, table, ins, outs, scratch=(), limit=48):
    return pl.pallas_call(
        body,
        out_shape=[jax.ShapeDtypeStruct(shape, kind) for shape, kind, _, _ in outs],
        grid_spec=pltpu.PrefetchScalarGridSpec(
            num_scalar_prefetch=1,
            grid=(steps,),
            in_specs=[pl.BlockSpec(block, index) for _, block, index in ins],
            out_specs=[pl.BlockSpec(block, index) for _, _, block, index in outs],
            scratch_shapes=[pltpu.VMEM(shape, kind) for shape, kind in scratch],
        ),
        compiler_params=pltpu.CompilerParams(vmem_limit_bytes=limit * 1024 * 1024),
    )(table, *[array for array, _, _ in ins])


def bits_of(count):
    found = []
    step = 1
    while step < count:
        found.append(step)
        step *= 2
    assert step == count
    return found


def swap(values, mask):
    total = lax.axis_size("batch") * lax.axis_size("expert")
    return lax.ppermute(values, AXES, [(at, at ^ mask) for at in range(total)])


def spread(values, masks):
    for mask in masks:
        values = jnp.concatenate([values, swap(values, mask)], axis=0)
    return values


def order(masks):
    found = [0]
    for mask in masks:
        found = found + [at ^ mask for at in found]
    return found


def add_body(low, got, keep, send):
    half = keep.shape[0]
    keep[...] = (low[:half].astype(WIDE) + got[:half].astype(WIDE)).astype(keep.dtype)
    send[...] = (low[half:].astype(WIDE) + got[half:].astype(WIDE)).astype(send.dtype)


def fold(low, high, masks):
    for mask in reversed(masks[1:]):
        got = swap(high, mask)
        half = ((low.shape[0] // 2,) + low.shape[1:], low.dtype)
        low, high = call(add_body, [half, half], (low, got))
    return low[0], swap(high, masks[0])[0]


def center_of(values):
    center = values - jnp.mean(values, axis=-1, keepdims=True)
    scale = lax.rsqrt(jnp.mean(center * center, axis=-1, keepdims=True) + 1e-06)
    return center * scale, scale


def norm_back(grad, unit, scale):
    return scale * (
        grad
        - jnp.mean(grad, axis=-1, keepdims=True)
        - unit * jnp.mean(grad * unit, axis=-1, keepdims=True)
    )


def route_body(
    experts, capacity, groups, routes, gates, lengths, cond, cotangent, packed, kept, sent
):
    count, width = cotangent.shape
    lane = lax.broadcasted_iota(jnp.int32, (count, LANES), 1)
    row = lax.broadcasted_iota(jnp.int32, (count, LANES), 0)
    length = lengths[0]
    live = row < length
    first = (lane == routes[:, 0:1]) & live
    second = (lane == routes[:, 1:2]) & live
    hits = first.astype(WIDE) + second.astype(WIDE)
    below = (
        lax.broadcasted_iota(jnp.int32, (count, count), 1)
        < lax.broadcasted_iota(jnp.int32, (count, count), 0)
    ).astype(LOW)
    room = (dot(below, hits.astype(LOW)) < capacity).astype(WIDE)
    first = first.astype(WIDE) * room
    second = second.astype(WIDE) * room
    weight = first * gates[:, 0:1] + second * gates[:, 1:2]
    high = weight.astype(LOW).astype(WIDE)
    packed[:, :width] = cotangent[...]
    packed[:, width:] = (high + pltpu.roll(weight - high, experts, 1)).astype(LOW)
    kept[0] = first
    kept[1] = second
    tally = jnp.sum(hits, axis=0, keepdims=True)
    tally = jnp.where(lane[:1] == experts, length.astype(WIDE), tally)
    rows = width // groups
    tally = pltpu.roll(tally, rows, 1)
    value = cond[...].astype(WIDE)
    value = value / (1.0 + jnp.exp(-value))
    for group in range(groups):
        start = group * rows // LANES * LANES
        part = value[:, start : start + LANES]
        shift = group * rows - start
        if shift:
            tail = value[:, start + LANES : start + 2 * LANES] if start + 2 * LANES <= width else part
            part = jnp.where(
                lane[:1] < LANES - shift, pltpu.roll(part, LANES - shift, 1), pltpu.roll(tail, LANES - shift, 1)
            )
        part = jnp.where(lane[:1] < rows, part, tally).astype(LOW)
        for expert in range(experts):
            sent[group * experts + expert] = jnp.broadcast_to(part, sent.shape[1:])


def place_of(rows, width):
    return (lax.broadcasted_iota(jnp.int32, (width, width), 0) == rows[...]).astype(LOW)


def lines_of(values, out):
    for at in range(values.shape[-1] // LANES):
        out[:, at, :] = values[:, at * LANES : (at + 1) * LANES]


def terms_body(where, got, weight, bias, out, loads):
    me, expert = where[0], where[1]
    total, _, _ = got.shape
    piece, wide = weight.shape
    rows = got[:, 0, :]
    pick = (
        lax.broadcasted_iota(jnp.int32, (LANES, piece), 0)
        == lax.broadcasted_iota(jnp.int32, (LANES, piece), 1) + expert * piece
    ).astype(LOW)
    share = bias.shape[1]
    spot = (
        lax.broadcasted_iota(jnp.int32, (share, wide), 1)
        == lax.broadcasted_iota(jnp.int32, (share, wide), 0) + me * share
    ).astype(LOW)
    terms = dot(dot(rows, pick).astype(LOW), weight[...]) + dot(bias[...], spot)
    lines_of(terms.astype(LOW), out)
    load = jnp.sum(rows.astype(WIDE), axis=0, keepdims=True)
    loads[...] = load


def shift_body(terms, modulation, gates):
    lines = jnp.sum(terms[...].astype(WIDE), axis=0)
    count = lines.shape[0]
    for at in range(count):
        modulation[:, at * LANES : (at + 1) * LANES] = lines[at : at + 1]
    gate = count // 6
    gates[...] = jnp.zeros(gates.shape, WIDE)
    for at in range(gate):
        gates[:, at, :] = jnp.broadcast_to(lines[5 * gate + at : 5 * gate + at + 1], (gates.shape[0], LANES))


def head_pair(values, pair):
    both = values[:, pair * LANES : (pair + 1) * LANES]
    lane = lax.broadcasted_iota(jnp.int32, both.shape, 1)
    zero = jnp.zeros_like(both)
    return jnp.concatenate(
        [jnp.where(lane < HEAD_DIM, both, zero), jnp.where(lane < HEAD_DIM, zero, both)], axis=0
    )


def scores_of(queries, stacked, pair, length):
    count = queries.shape[0]
    raw = dot_nt(queries[:, pair * LANES : (pair + 1) * LANES], stacked) * HEAD_DIM ** (-0.5)
    lane = lax.broadcasted_iota(jnp.int32, raw.shape, 1)
    return jnp.where((lane & (count - 1)) < length, raw, -1e30)


def times(left, low, high, cols):
    half = low.shape[0]
    return dot(left[:, :half], low[:, cols]) + dot(left[:, half:], high[:, cols])


def times_back(left, low, high, cols):
    return jnp.concatenate([dot_nt(left, low[:, cols]), dot_nt(left, high[:, cols])], axis=1)


def forward_body(
    tokens, modulation, lengths, rows0, rows1, rows2, low0, high0, low1, high1, low2, high2,
    both, joined, totals, attn_out, middle_out, *parts,
):
    count, width = tokens.shape
    length = lengths[0]
    mod = modulation[...]
    tok = tokens[...].astype(WIDE)
    unit, _ = center_of(tok)
    first = (unit * (1.0 + mod[:, width : 2 * width]) + mod[:, :width]).astype(LOW)
    both[:, :width] = first
    start = 0
    for rows, low, high in ((rows0, low0, high0), (rows1, low1, high1), (rows2, low2, high2)):
        moved = dot(first, place_of(rows, width)).astype(LOW)
        size = min(low.shape[1], 3 * width - start)
        joined[:, start : start + size] = times(moved, low, high, slice(0, size)).astype(LOW)
        start += size
    queries, keys, values = joined[:, :width], joined[:, width : 2 * width], joined[:, 2 * width :]
    lane = lax.broadcasted_iota(jnp.int32, (count, LANES), 1)
    sums = jnp.zeros((count, LANES), WIDE)
    for pair in range(HEADS // 2):
        scores = scores_of(queries, head_pair(keys, pair), pair, length)
        probs = []
        for one in range(2):
            mine = scores[:, one * count : (one + 1) * count]
            top = jnp.max(mine, axis=-1, keepdims=True)
            total = top + jnp.log(jnp.sum(jnp.exp(mine - top), axis=-1, keepdims=True))
            sums = jnp.where(lane == 2 * pair + one, total, sums)
            probs.append(jnp.exp(mine - total).astype(LOW))
        both[:, width + pair * LANES : width + (pair + 1) * LANES] = dot(
            jnp.concatenate(probs, axis=1), head_pair(values, pair)
        ).astype(LOW)
    totals[...] = sums
    moved = dot(both[:, width:], place_of(rows2, width)).astype(LOW)
    attn = times(moved, low2, high2, slice(width, 2 * width))
    attn_out[...] = attn
    middle = tok + mod[:, 2 * width : 3 * width] * attn
    middle_out[...] = middle
    unit, _ = center_of(middle)
    second = (unit * (1.0 + mod[:, 4 * width : 5 * width]) + mod[:, 3 * width : 4 * width]).astype(LOW)
    start = 0
    for part in parts:
        part[...] = second[:, start : start + part.shape[1]]
        start += part.shape[1]


def backward_body(
    tokens, cotangent, modulation, lengths, rows0, rows1, rows2, low0, high0, low1, high1, low2, high2,
    joined, totals, attn_in, middle_in, near0, far0, near1, far1, near2, far2,
    grad_tokens, sent, d_mod, d_rows, d_cols,
):
    count, width = tokens.shape
    length = lengths[0]
    mod = modulation[...]
    start = 0
    for low, high in ((near0, far0), (near1, far1), (near2, far2)):
        size = low.shape[1]
        d_rows[:, start : start + size] = low[...].astype(WIDE) + high[...].astype(WIDE)
        start += size
    d_second = d_rows[...]
    attn = attn_in[...]
    unit, scale = center_of(middle_in[...])
    d_mod[:, 3 * width : 4 * width] = jnp.sum(d_second, axis=0, keepdims=True)
    d_mod[:, 4 * width : 5 * width] = jnp.sum(d_second * unit, axis=0, keepdims=True)
    d_middle = cotangent[...].astype(WIDE) + norm_back(
        d_second * (1.0 + mod[:, 4 * width : 5 * width]), unit, scale
    )
    d_mod[:, 2 * width : 3 * width] = jnp.sum(d_middle * attn, axis=0, keepdims=True)
    d_attn = (mod[:, 2 * width : 3 * width] * d_middle).astype(LOW)
    d_cols[:, 3 * width :] = d_attn
    d_attended = dot_nt(
        times_back(d_attn, low2, high2, slice(width, 2 * width)).astype(LOW), place_of(rows2, width)
    ).astype(LOW)
    queries, keys, values = joined[:, :width], joined[:, width : 2 * width], joined[:, 2 * width :]
    sums = totals[...]
    lane = lax.broadcasted_iota(jnp.int32, (count, LANES), 1)
    factor = HEAD_DIM ** (-0.5)
    for pair in range(HEADS // 2):
        at = slice(pair * LANES, (pair + 1) * LANES)
        k_pair, v_pair = head_pair(keys, pair), head_pair(values, pair)
        scores = scores_of(queries, k_pair, pair, length)
        d_probs = dot_nt(d_attended[:, at], v_pair)
        probs_low, d_scores_low = [], []
        for one in range(2):
            half = slice(one * count, (one + 1) * count)
            total = jnp.sum(jnp.where(lane == 2 * pair + one, sums, 0.0), axis=1, keepdims=True)
            probs = jnp.exp(scores[:, half] - total)
            back = d_probs[:, half]
            d_scores = probs * (back - jnp.sum(probs * back, axis=-1, keepdims=True))
            probs_low.append(probs.astype(LOW))
            d_scores_low.append(d_scores.astype(LOW))
        d_scores_both = jnp.concatenate(d_scores_low, axis=1)
        d_cols[:, at] = (dot(d_scores_both, k_pair) * factor).astype(LOW)
        q_pair, d_pair = queries[:, at], d_attended[:, at]
        d_k = dot_tn(d_scores_both, q_pair) * factor
        d_v = dot_tn(jnp.concatenate(probs_low, axis=1), d_pair)
        d_k = jnp.where(lane < HEAD_DIM, d_k[:count], d_k[count:])
        d_v = jnp.where(lane < HEAD_DIM, d_v[:count], d_v[count:])
        d_cols[:, width + pair * LANES : width + (pair + 1) * LANES] = d_k.astype(LOW)
        d_cols[:, 2 * width + pair * LANES : 2 * width + (pair + 1) * LANES] = d_v.astype(LOW)
    d_first = jnp.zeros((count, width), WIDE)
    start = 0
    for rows, low, high in ((rows0, low0, high0), (rows1, low1, high1), (rows2, low2, high2)):
        size = min(low.shape[1], 3 * width - start)
        part = times_back(d_cols[:, start : start + size], low, high, slice(0, size))
        start += size
        place = place_of(rows, width)
        top = part.astype(LOW)
        rest = (part - top.astype(WIDE)).astype(LOW)
        d_first += dot_nt(top, place) + dot_nt(rest, place)
    unit, scale = center_of(tokens[...].astype(WIDE))
    d_mod[:, :width] = jnp.sum(d_first, axis=0, keepdims=True)
    d_mod[:, width : 2 * width] = jnp.sum(d_first * unit, axis=0, keepdims=True)
    grad_tokens[...] = d_middle + norm_back(
        d_first * (1.0 + mod[:, width : 2 * width]), unit, scale
    )
    experts = sent.shape[0]
    cols, out_cols = 3 * width // experts, width // experts
    for expert in range(experts):
        sent[expert, :, :cols] = d_cols[:, expert * cols : (expert + 1) * cols]
        sent[expert, :, cols:] = d_cols[:, 3 * width + expert * out_cols : 3 * width + (expert + 1) * out_cols]


class Slots:
    def __init__(self, width, units, shared_units, replicas):
        self.width, self.replicas = width, replicas
        slot, shared_slot = up_to(units, LANES), up_to(shared_units, LANES)
        self.routed = replicas * slot
        self.hidden = self.routed + replicas * shared_slot
        self.places = [(at * slot, units, slot) for at in range(replicas)]
        self.places += [(self.routed + at * shared_slot, shared_units, shared_slot) for at in range(replicas)]

    def join_down(self, pieces, full):
        for (start, size, room), piece in zip(self.places, pieces):
            full[start : start + size] = piece[...]
            if room > size:
                full[start + size : start + room] = jnp.zeros((room - size, self.width), LOW)

    def join_up(self, pieces, full):
        for (start, size, room), piece in zip(self.places, pieces):
            full[:, start : start + size] = piece[...]
            if room > size:
                full[:, start + size : start + room] = jnp.zeros((self.width, room - size), LOW)


def d_act_body(slots, table, low, high, gate_low, gate_high, *refs):
    pieces, (d_act, d_mlp, down) = refs[: 2 * slots.replicas], refs[2 * slots.replicas :]
    count, width = low.shape[1], slots.width

    @pl.when(pl.program_id(0) == 0)
    def _():
        slots.join_down(pieces, down)

    for at, (rows, gate) in enumerate(((low, gate_low), (high, gate_high))):
        for line in range(width // LANES):
            cols = slice(line * LANES, (line + 1) * LANES)
            d_mlp[0, at * count : (at + 1) * count, cols] = (
                rows[0, :, cols].astype(WIDE) * gate[0, line : line + 1, :]
            ).astype(LOW)
    d_act[0] = dot_nt(d_mlp[0], down[...]).astype(LOW)


def hidden_body(slots, table, *refs):
    lows, highs, refs = refs[:3], refs[3:6], refs[6:]
    side_low, side_high, mine, d_act, refs = refs[0], refs[1], refs[2], refs[3], refs[4:]
    pieces, refs = refs[: 2 * slots.replicas], refs[2 * slots.replicas :]
    back_lows, back_highs, refs = refs[:3], refs[3:6], refs[6:]
    d_pre, act, pairs, rows, up = refs
    count = lows[0].shape[1]

    @pl.when(pl.program_id(0) == 0)
    def _():
        slots.join_up(pieces, up)

    start = 0
    for low, high in zip(lows, highs):
        size = low.shape[2]
        rows[0, :count, start : start + size] = low[0]
        rows[0, count:, start : start + size] = high[0]
        start += size
    for at, (side, backs) in enumerate(((side_low, back_lows), (side_high, back_highs))):
        here = slice(at * count, (at + 1) * count)
        weight = jnp.sum(side[0].astype(WIDE) * mine[...], axis=1, keepdims=True)
        pre = dot(rows[0, here], up[...])
        square = pre * pre
        bend = jnp.tanh(pre * (CURVE + (CURVE * CUBIC) * square))
        gate = 0.5 + 0.5 * bend
        hidden = pre * gate
        slope = gate + hidden * (1.0 - bend) * (CURVE + (3.0 * CURVE * CUBIC) * square)
        d_hidden = d_act[0, here].astype(WIDE)
        d_full = d_hidden * slope
        d_low = jnp.concatenate(
            [d_full[:, : slots.routed] * weight, d_full[:, slots.routed :]], axis=1
        ).astype(LOW)
        d_pre[0, here] = d_low
        act[0, here] = jnp.concatenate(
            [hidden[:, : slots.routed] * weight, hidden[:, slots.routed :]], axis=1
        ).astype(LOW)
        pair = jnp.sum(hidden[:, : slots.routed] * d_hidden[:, : slots.routed], axis=1, keepdims=True)
        pairs[0, here] = (pair * mine[...]).astype(LOW)
        back = dot_nt(d_low, up[...]).astype(LOW)
        start = 0
        for ref in backs:
            size = ref.shape[2]
            ref[0] = back[:, start : start + size]
            start += size


def branch_body(slots, table, act, pairs, *refs):
    pieces, refs = refs[: 2 * slots.replicas], refs[2 * slots.replicas :]
    lows, highs, (down,) = refs[:3], refs[3:6], refs[6:]
    count = lows[0].shape[1]

    @pl.when(pl.program_id(0) == 0)
    def _():
        slots.join_down(pieces, down)

    for at, parts in enumerate((lows, highs)):
        here = slice(at * count, (at + 1) * count)
        out = dot(act[0, here], down[...]).astype(LOW)
        start = 0
        for number, ref in enumerate(parts):
            size = ref.shape[2] - (LANES if number == 0 else 0)
            ref[0, :, :size] = out[:, start : start + size]
            if number == 0:
                ref[0, :, size:] = pairs[0, here]
            start += size


def finish_body(
    experts, cotangent, modulation, middle, kept, d_mod, near0, far0, near1, far1, near2, far2,
    block_out, grad_gates, sent, branch,
):
    count, width = cotangent.shape
    start = 0
    for number, (low, high) in enumerate(((near0, far0), (near1, far1), (near2, far2))):
        total = low[...].astype(WIDE) + high[...].astype(WIDE)
        if number == 0:
            pairs = total[:, -LANES:]
            total = total[:, :-LANES]
        branch[:, start : start + total.shape[1]] = total
        start += total.shape[1]
    block_out[...] = middle[...] + modulation[:, 5 * width :] * branch[...]
    for choice in range(2):
        grad_gates[:, choice : choice + 1] = jnp.sum(kept[choice] * pairs, axis=1, keepdims=True)
    d_gate = jnp.sum(cotangent[...].astype(WIDE) * branch[...], axis=0, keepdims=True)
    for at in range(sent.shape[1]):
        cols = slice(at * LANES, (at + 1) * LANES)
        if at * LANES < 5 * width:
            line = d_mod[:, cols]
        else:
            line = d_gate[:, at * LANES - 5 * width : (at + 1) * LANES - 5 * width]
        sent[:, at, :] = jnp.broadcast_to(line.astype(LOW), (sent.shape[0], LANES))


def ada_body(experts, where, got, cond, weight, grad_weight, grad_bias, sent, d_mod):
    expert = where[1]
    total, lines, _ = got.shape
    for at in range(lines):
        d_mod[:, at * LANES : (at + 1) * LANES] = got[:, at, :]
    grad_bias[...] = jnp.sum(d_mod[...].astype(WIDE), axis=0, keepdims=True)
    cols = grad_weight.shape[1]
    mine = d_mod[:, pl.ds(pl.multiple_of(expert * cols, LANES), cols)]
    grad_weight[...] = dot_tn(cond[:, 0, :], mine)[: grad_weight.shape[0]]
    piece = weight.shape[0]
    back = dot_nt(d_mod[...], weight[...])
    sent[...] = jnp.zeros(sent.shape, WIDE)
    sent[:, 0, :piece] = back


def attn_grads_body(both, d_cols, out):
    experts, count, cols = d_cols.shape
    width = both.shape[2] // 2
    groups, rows, _ = out.shape
    flat = d_cols[...].reshape(experts * count, cols)
    inputs = both[...].reshape(experts * count, 2 * width)
    cut = 3 * cols // 4
    out[...] = jnp.concatenate(
        [dot_tn(inputs[:, :width], flat[:, :cut]), dot_tn(inputs[:, width:], flat[:, cut:])], axis=1
    ).astype(LOW).reshape(groups, rows, cols)


def attn_sum_body(got, grad_qkv, grad_out):
    total = jnp.sum(got[...].astype(WIDE), axis=0)
    cut = grad_qkv.shape[1]
    grad_qkv[...] = total[:, :cut]
    grad_out[...] = total[:, cut:]


def up_out_body(units, got, grad_up):
    for group in range(got.shape[0]):
        grad_up[:, group * units : (group + 1) * units] = got[group, :, :units].astype(WIDE)


def gather_far(pieces, masks):
    found = [pieces]
    for mask in masks:
        found = found + [[swap(piece, mask) for piece in held] for held in found]
    return found


def shards(
    tokens,
    cond,
    lengths,
    routes,
    gate_weights,
    ada_weight,
    ada_bias,
    qkv_weight,
    out_weight,
    shared_up,
    shared_down,
    expert_up,
    expert_down,
    cotangent,
):
    count, width = tokens.shape
    experts = lax.axis_size("expert")
    groups = lax.axis_size("batch")
    total = experts * groups
    me = lax.axis_index(AXES)
    my_expert = lax.axis_index("expert")
    where = jnp.stack([me, my_expert]).astype(jnp.int32)
    capacity = 5 * 2 * count // (4 * experts)
    piece = ada_weight.shape[0]
    group_rows = width // groups
    shares = [width * share // sum(SHARES) for share in SHARES]

    expert_masks = bits_of(experts)
    group_masks = [experts * step for step in bits_of(groups)]
    near_bits = len(bits_of(min(groups, 32 // experts)))
    near, far = group_masks[:near_bits], group_masks[near_bits:]
    core, across = expert_masks[:1], expert_masks[1:]
    away = list(reversed(near[1:]))
    team_links = [across + near[:1] + away, near[:1] + away + across, away + across + near[:1]]
    far_away = list(reversed(far)) + away
    weight_links = [
        across + near[:1] + far_away,
        near[:1] + far_away + across,
        far_away + across + near[:1],
    ]
    masks = order(team_links[0])
    steps = len(masks)

    packed, kept, sent = call(
        functools.partial(route_body, experts, capacity, groups),
        [((count, width + LANES), LOW), ((2, count, LANES), WIDE), ((total, 16, LANES), LOW)],
        (routes, gate_weights, lengths, cond, cotangent),
        smem=(2,),
    )
    if far:
        team_all = spread(packed[None], team_links[0] + core)
        first_block = jnp.arange(steps, dtype=jnp.int32)
        second_block = first_block + steps
    else:
        team_all = lax.all_gather(packed, AXES, axis=0).reshape(total, count, width + LANES)
        first_block = me ^ jnp.array(masks, jnp.int32)
        second_block = first_block ^ core[0]
    spots = [jnp.array([order(links).index(mask) for mask in masks], jnp.int32) for links in team_links]
    gate_block = [(me ^ jnp.array(masks, jnp.int32)), (me ^ jnp.array(masks, jnp.int32)) ^ core[0]]
    table = jnp.stack([*spots, first_block, second_block, *gate_block])

    cond_all = lax.all_to_all(sent, AXES, split_axis=0, concat_axis=0, tiled=True)
    terms, loads = call(
        terms_body,
        [((total, 6 * width // LANES, LANES), LOW), ((1, LANES), WIDE)],
        (where, cond_all, ada_weight, ada_bias[None]),
        smem=(0,),
    )
    tallies = loads[0, group_rows : group_rows + experts + 1]
    expert_load = tallies[:experts] * experts / (2.0 * tallies[experts])
    terms = lax.all_to_all(terms, AXES, split_axis=0, concat_axis=0, tiled=True)
    modulation, gates = call(
        shift_body, [((1, 6 * width), WIDE), ((total, 8, LANES), WIDE)], (terms,)
    )
    gates = lax.all_to_all(gates, AXES, split_axis=0, concat_axis=0, tiled=True)

    wide_cut = 4 * width // sum(SHARES)
    own = [
        qkv_weight[:, :wide_cut],
        qkv_weight[:, wide_cut : 3 * wide_cut],
        jnp.concatenate([qkv_weight[:, 3 * wide_cut :], out_weight], axis=1),
    ]
    weights = []
    rows_at = []
    for part, links in zip(own, weight_links):
        low = spread(part[None], links)
        high = swap(low, core[0])
        weights += [low.reshape(-1, part.shape[1]), high.reshape(-1, part.shape[1])]
        found = jnp.array(order(links + core), jnp.int32) ^ me
        rows_at.append((found[:, None] * piece + jnp.arange(piece, dtype=jnp.int32)).reshape(1, -1))

    tall = (count, width)
    both, joined, totals, attn, middle, *seconds = call(
        forward_body,
        [
            ((count, 2 * width), LOW),
            ((count, 3 * width), LOW),
            ((count, LANES), WIDE),
            (tall, WIDE),
            (tall, WIDE),
            *[((count, share), LOW) for share in shares],
        ],
        (tokens, modulation, lengths, *rows_at, *weights),
        smem=(2,),
    )

    part_up = lax.all_to_all(expert_up[0], "batch", split_axis=1, concat_axis=0, tiled=True)
    part_shared_up = lax.all_to_all(shared_up, AXES, split_axis=1, concat_axis=0, tiled=True)
    held = gather_far([part_up, part_shared_up, expert_down[0], shared_down], far)
    ups = [h[0] for h in held] + [h[1] for h in held]
    downs = [h[2] for h in held] + [h[3] for h in held]
    units, shared_units = part_up.shape[1], part_shared_up.shape[1]
    slots = Slots(width, units, shared_units, len(held))

    def whole(array):
        return array, array.shape, lambda step, table: (0,) * array.ndim

    def rows_of(array):
        return array, (1,) + array.shape[1:], lambda step, table: (step, 0, 0)

    def rows_out(lanes):
        return (steps, 2 * count, lanes), LOW, (1, 2 * count, lanes), lambda step, table: (step, 0, 0)

    def block_in(array, row, lanes=None, lane_block=0):
        return (
            array,
            (1, array.shape[1], lanes or array.shape[2]),
            lambda step, table: (table[row, step], 0, lane_block),
        )

    def block_out_of(lanes, row):
        return (steps, count, lanes), LOW, (1, count, lanes), lambda step, table: (table[row, step], 0, 0)

    d_act, d_mlp = sweep(
        functools.partial(d_act_body, slots),
        steps,
        table,
        [
            block_in(team_all, 3, width),
            block_in(team_all, 4, width),
            block_in(gates, 5),
            block_in(gates, 6),
            *[whole(down) for down in downs],
        ],
        [rows_out(slots.hidden), rows_out(width)],
        scratch=[((slots.hidden, width), LOW)],
    )

    second_low = [spread(part[None], links) for part, links in zip(seconds, team_links)]
    second_high = [swap(part, core[0]) for part in second_low]
    lane = jnp.arange(LANES, dtype=jnp.int32)[None, :]
    mine = ((lane == my_expert) | (lane == my_expert + experts)).astype(WIDE)
    back = [block_out_of(share, row) for row, share in enumerate(shares)]
    *back_parts, d_pre, act, pairs, second_all = sweep(
        functools.partial(hidden_body, slots),
        steps,
        table,
        [
            *[block_in(part, row) for row, part in enumerate(second_low)],
            *[block_in(part, row) for row, part in enumerate(second_high)],
            block_in(team_all, 3, LANES, width // LANES),
            block_in(team_all, 4, LANES, width // LANES),
            whole(mine),
            rows_of(d_act),
            *[whole(up) for up in ups],
        ],
        [*back, *back, rows_out(slots.hidden), rows_out(slots.hidden), rows_out(LANES), rows_out(width)],
        scratch=[((width, slots.hidden), LOW)],
    )
    d_second = [
        fold(back_parts[at], back_parts[3 + at], team_links[at] + core) for at in range(len(shares))
    ]
    wider = [block_out_of(share + (0 if row else LANES), row) for row, share in enumerate(shares)]
    branch_parts = sweep(
        functools.partial(branch_body, slots),
        steps,
        table,
        [rows_of(act), rows_of(pairs), *[whole(down) for down in downs]],
        [*wider, *wider],
        scratch=[((slots.hidden, width), LOW)],
    )
    branch_terms = [
        fold(branch_parts[at], branch_parts[3 + at], team_links[at] + core) for at in range(len(shares))
    ]

    rows = steps * 2 * count
    grad_up = dot_tn(second_all.reshape(rows, width), d_pre.reshape(rows, slots.hidden))
    grad_down = dot_tn(act.reshape(rows, slots.hidden), d_mlp.reshape(rows, width))
    ups_held = [grad_up[:, start : start + size] for start, size, _ in slots.places]
    downs_held = [grad_down[start : start + size] for start, size, _ in slots.places]
    replicas = slots.replicas
    sums = []
    for held in (ups_held[:replicas], ups_held[replicas:], downs_held[:replicas], downs_held[replicas:]):
        for mask in reversed(far):
            some = len(held) // 2
            held = [
                low + swap(high.astype(LOW), mask).astype(WIDE) for low, high in zip(held[:some], held[some:])
            ]
        sums.append(held[0])
    grad_expert_down = sums[2][None]
    grad_shared_down = lax.all_to_all(
        sums[3].astype(LOW), "expert", split_axis=1, concat_axis=0, tiled=True
    ).astype(WIDE)
    up_rows = jnp.concatenate([sums[0], sums[1]], axis=1).astype(LOW).reshape(groups, group_rows, -1)
    up_rows = lax.all_to_all(up_rows, "batch", split_axis=0, concat_axis=0, tiled=True)
    (grad_expert_up,) = call(
        functools.partial(up_out_body, units), [((group_rows, groups * units), WIDE)], (up_rows,)
    )
    shared_rows = up_rows[:, :, units:].reshape(experts, groups // experts, group_rows, shared_units)
    shared_rows = lax.all_to_all(shared_rows, "expert", split_axis=0, concat_axis=0, tiled=True)
    grad_shared_up = shared_rows.transpose(2, 1, 0, 3).reshape(group_rows, groups * shared_units).astype(WIDE)

    grad_tokens, d_cols, d_mod = call(
        backward_body,
        [(tall, WIDE), ((experts, count, 4 * width // experts), LOW), ((1, 5 * width), WIDE)],
        (
            tokens, cotangent, modulation, lengths, *rows_at, *weights,
            joined, totals, attn, middle, *[half for pair in d_second for half in pair],
        ),
        scratch=[(tall, WIDE), ((count, 4 * width), LOW)],
        smem=(3,),
    )
    block_out, grad_gate_weights, sent = call(
        functools.partial(finish_body, experts),
        [(tall, WIDE), ((count, 2), WIDE), ((total, 6 * width // LANES, LANES), LOW)],
        (
            cotangent, modulation, middle, kept, d_mod, *[half for pair in branch_terms for half in pair],
        ),
        scratch=[(tall, WIDE)],
    )

    both_group = lax.all_gather(both, "expert", axis=0)
    d_cols = lax.all_to_all(d_cols, "expert", split_axis=0, concat_axis=0, tiled=True)
    (attn_terms,) = call(
        attn_grads_body, [((groups, group_rows, 4 * width // experts), LOW)], (both_group, d_cols)
    )
    attn_terms = lax.all_to_all(attn_terms, "batch", split_axis=0, concat_axis=0, tiled=True)
    grad_qkv, grad_out = call(
        attn_sum_body,
        [((group_rows, 3 * width // experts), WIDE), ((group_rows, width // experts), WIDE)],
        (attn_terms,),
    )

    d_mod_all = lax.all_to_all(sent, AXES, split_axis=0, concat_axis=0, tiled=True)
    grad_ada_weight, grad_ada_bias, sent = call(
        functools.partial(ada_body, experts),
        [((group_rows, 6 * width // experts), WIDE), ((1, 6 * width), WIDE), ((total, 8, LANES), WIDE)],
        (where, d_mod_all, cond_all, ada_weight),
        scratch=[((total, 6 * width), LOW)],
        smem=(0,),
    )
    d_cond_act = lax.all_to_all(sent, AXES, split_axis=0, concat_axis=0, tiled=True)
    d_cond_act = d_cond_act[:, 0, :piece].reshape(1, width)
    _, silu_back = jax.vjp(jax.nn.silu, cond.astype(WIDE))
    grad_cond = silu_back(d_cond_act)[0]

    return (
        block_out,
        grad_tokens,
        grad_cond,
        grad_gate_weights,
        grad_ada_weight,
        grad_ada_bias[0],
        grad_qkv,
        grad_out,
        grad_shared_up,
        grad_shared_down,
        grad_expert_up[None],
        grad_expert_down,
        expert_load,
    )


def solution(mesh):
    rows = P(AXES, None)
    line = P(AXES)
    tiles = P("batch", "expert")
    split = P("expert", "batch", None)
    in_specs = (rows, rows, line, rows, rows, rows, line, rows, rows, rows, rows, split, split, rows)
    out_specs = (rows, rows, rows, rows, tiles, P(), tiles, tiles, tiles, tiles, split, split, P())
    return jax.shard_map(shards, mesh=mesh, in_specs=in_specs, out_specs=out_specs, check_vma=False)
```

```python
import functools

import jax
import jax.numpy as jnp
from jax import lax
from jax.experimental import pallas as pl
from jax.experimental.pallas import tpu as pltpu
from jax.sharding import PartitionSpec as P

HEADS = 12
HEAD_DIM = 64
AXES = ("batch", "expert")
LOW = jnp.bfloat16
WIDE = jnp.float32
LANES = 128
SHARES = (1, 2, 3)
SPLIT = (5, 1)
CURVE = 0.7978845608028654
CUBIC = 0.044715


def dot(left, right):
    return lax.dot_general(left, right, (((1,), (0,)), ((), ())), preferred_element_type=WIDE)


def dot_nt(left, right):
    return lax.dot_general(left, right, (((1,), (1,)), ((), ())), preferred_element_type=WIDE)


def dot_tn(left, right):
    return lax.dot_general(left, right, (((0,), (0,)), ((), ())), preferred_element_type=WIDE)


def up_to(value, step):
    return -(-value // step) * step


def call(body, outs, args, scratch=(), smem=(), limit=48):
    specs = [pl.BlockSpec(memory_space=pltpu.SMEM) if at in smem else pl.BlockSpec() for at in range(len(args))]
    return pl.pallas_call(
        body,
        out_shape=[jax.ShapeDtypeStruct(shape, kind) for shape, kind in outs],
        in_specs=specs,
        out_specs=[pl.BlockSpec()] * len(outs),
        scratch_shapes=[pltpu.VMEM(shape, kind) for shape, kind in scratch],
        compiler_params=pltpu.CompilerParams(vmem_limit_bytes=limit * 1024 * 1024),
    )(*args)


def sweep(body, steps, ins, outs, scratch=(), limit=56):
    return pl.pallas_call(
        body,
        out_shape=[jax.ShapeDtypeStruct(shape, kind) for shape, kind, _, _ in outs],
        grid=(steps,),
        in_specs=[
            pl.BlockSpec(memory_space=pltpu.SMEM) if block is None else pl.BlockSpec(block, index)
            for _, block, index in ins
        ],
        out_specs=[pl.BlockSpec(block, index) for _, _, block, index in outs],
        scratch_shapes=[pltpu.VMEM(shape, kind) for shape, kind in scratch],
        compiler_params=pltpu.CompilerParams(vmem_limit_bytes=limit * 1024 * 1024),
    )(*[array for array, _, _ in ins])


def pad_lanes(values, width):
    return jnp.pad(values, ((0, 0),) * (values.ndim - 1) + ((0, width - values.shape[-1]),))


def tie(values, *others):
    return lax.optimization_barrier((values, *others))[0]


def bits_of(count):
    found = []
    step = 1
    while step < count:
        found.append(step)
        step *= 2
    assert step == count
    return found


def swap(values, mask):
    total = lax.axis_size("batch") * lax.axis_size("expert")
    return lax.ppermute(values, AXES, [(at, at ^ mask) for at in range(total)])


def spread(values, masks, waits=()):
    waits = dict(waits)
    for at, mask in enumerate(masks):
        if at in waits:
            values = tie(values, *waits[at])
        values = jnp.concatenate([values, swap(values, mask)], axis=0)
    return values


def order(masks):
    found = [0]
    for mask in masks:
        found = found + [at ^ mask for at in found]
    return found


def add_body(low, got, keep, send):
    half = keep.shape[0]
    keep[...] = (low[:half].astype(WIDE) + got[:half].astype(WIDE)).astype(keep.dtype)
    send[...] = (low[half:].astype(WIDE) + got[half:].astype(WIDE)).astype(send.dtype)


def fold(lows, highs, orders, waits=()):
    waits = dict(waits)
    lows, highs, sent = list(lows), list(highs), []
    for at in range(len(orders[0]) - 1):
        sent.append(list(highs))
        got = [swap(high, links[-1 - at]) for high, links in zip(highs, orders)]
        if at in waits:
            got = tie(tuple(got), *waits[at])
        for part, other in enumerate(got):
            half = ((other.shape[0] // 2,) + other.shape[1:], other.dtype)
            lows[part], highs[part] = call(add_body, [half, half], (lows[part], other))
    sent.append(list(highs))
    got = [swap(high, links[0]) for high, links in zip(highs, orders)]
    return [half[0] for pair in zip(lows, got) for half in pair], sent


def center_of(values):
    center = values - jnp.mean(values, axis=-1, keepdims=True)
    scale = lax.rsqrt(jnp.mean(center * center, axis=-1, keepdims=True) + 1e-06)
    return center * scale, scale


def norm_back(grad, unit, scale):
    return scale * (
        grad
        - jnp.mean(grad, axis=-1, keepdims=True)
        - unit * jnp.mean(grad * unit, axis=-1, keepdims=True)
    )


def route_body(
    experts, capacity, groups, routes, gates, lengths, cond, side, kept, sent
):
    count, width = routes.shape[0], cond.shape[1]
    lane = lax.broadcasted_iota(jnp.int32, (count, LANES), 1)
    row = lax.broadcasted_iota(jnp.int32, (count, LANES), 0)
    length = lengths[0]
    live = row < length
    first = (lane == routes[:, 0:1]) & live
    second = (lane == routes[:, 1:2]) & live
    hits = first.astype(WIDE) + second.astype(WIDE)
    below = (
        lax.broadcasted_iota(jnp.int32, (count, count), 1)
        < lax.broadcasted_iota(jnp.int32, (count, count), 0)
    ).astype(LOW)
    room = (dot(below, hits.astype(LOW)) < capacity).astype(WIDE)
    first = first.astype(WIDE) * room
    second = second.astype(WIDE) * room
    weight = first * gates[:, 0:1] + second * gates[:, 1:2]
    high = weight.astype(LOW).astype(WIDE)
    side[...] = (high + pltpu.roll(weight - high, experts, 1)).astype(LOW)
    kept[0] = first
    kept[1] = second
    tally = jnp.sum(hits, axis=0, keepdims=True)
    tally = jnp.where(lane[:1] == experts, length.astype(WIDE), tally)
    rows = width // groups
    tally = pltpu.roll(tally, rows, 1)
    value = cond[...].astype(WIDE)
    value = value / (1.0 + jnp.exp(-value))
    for group in range(groups):
        start = group * rows // LANES * LANES
        part = value[:, start : start + LANES]
        shift = group * rows - start
        if shift:
            tail = value[:, start + LANES : start + 2 * LANES] if start + 2 * LANES <= width else part
            part = jnp.where(
                lane[:1] < LANES - shift, pltpu.roll(part, LANES - shift, 1), pltpu.roll(tail, LANES - shift, 1)
            )
        part = jnp.where(lane[:1] < rows, part, tally).astype(LOW)
        for expert in range(experts):
            sent[group * experts + expert] = jnp.broadcast_to(part, sent.shape[1:])


def place_of(rows, width):
    return (lax.broadcasted_iota(jnp.int32, (width, width), 0) == rows[...]).astype(LOW)


def lines_of(values, out):
    for at in range(values.shape[-1] // LANES):
        out[:, at, :] = values[:, at * LANES : (at + 1) * LANES]


def terms_body(where, got, weight, bias, out, loads):
    me, expert = where[0], where[1]
    total, _, _ = got.shape
    piece, wide = weight.shape
    rows = got[:, 0, :]
    pick = (
        lax.broadcasted_iota(jnp.int32, (LANES, piece), 0)
        == lax.broadcasted_iota(jnp.int32, (LANES, piece), 1) + expert * piece
    ).astype(LOW)
    share = bias.shape[1]
    spot = (
        lax.broadcasted_iota(jnp.int32, (share, wide), 1)
        == lax.broadcasted_iota(jnp.int32, (share, wide), 0) + me * share
    ).astype(LOW)
    terms = dot(dot(rows, pick).astype(LOW), weight[...]) + dot(bias[...], spot)
    lines_of(terms.astype(LOW), out)
    load = jnp.sum(rows.astype(WIDE), axis=0, keepdims=True)
    loads[...] = load


def shift_body(terms, cotangent, side, modulation, *parts):
    lines = jnp.sum(terms[...].astype(WIDE), axis=0)
    for at in range(lines.shape[0]):
        modulation[:, at * LANES : (at + 1) * LANES] = lines[at : at + 1]
    width = cotangent.shape[1]
    d_mlp = (modulation[:, 5 * width :] * cotangent[...].astype(WIDE)).astype(LOW)
    start = 0
    for at, part in enumerate(parts):
        size = part.shape[1] - (0 if at else LANES)
        part[:, :size] = d_mlp[:, start : start + size]
        if at == 0:
            part[:, size:] = side[...]
        start += size


def head_pair(values, pair):
    both = values[:, pair * LANES : (pair + 1) * LANES]
    lane = lax.broadcasted_iota(jnp.int32, both.shape, 1)
    zero = jnp.zeros_like(both)
    return jnp.concatenate(
        [jnp.where(lane < HEAD_DIM, both, zero), jnp.where(lane < HEAD_DIM, zero, both)], axis=0
    )


def scores_of(queries, stacked, pair, length):
    count = queries.shape[0]
    raw = dot_nt(queries[:, pair * LANES : (pair + 1) * LANES], stacked) * HEAD_DIM ** (-0.5)
    lane = lax.broadcasted_iota(jnp.int32, raw.shape, 1)
    return jnp.where((lane & (count - 1)) < length, raw, -1e30)


def times(left, low, high, cols):
    half = low.shape[0]
    return dot(left[:, :half], low[:, cols]) + dot(left[:, half:], high[:, cols])


def times_back(left, low, high, cols):
    return jnp.concatenate([dot_nt(left, low[:, cols]), dot_nt(left, high[:, cols])], axis=1)


def forward_body(
    tokens, modulation, lengths, rows0, rows1, rows2, low0, high0, low1, high1, low2, high2,
    both, joined, totals, attn_out, middle_out, *parts,
):
    count, width = tokens.shape
    length = lengths[0]
    mod = modulation[...]
    tok = tokens[...].astype(WIDE)
    unit, _ = center_of(tok)
    first = (unit * (1.0 + mod[:, width : 2 * width]) + mod[:, :width]).astype(LOW)
    both[:, :width] = first
    start = 0
    for rows, low, high in ((rows0, low0, high0), (rows1, low1, high1), (rows2, low2, high2)):
        moved = dot(first, place_of(rows, width)).astype(LOW)
        size = min(low.shape[1], 3 * width - start)
        joined[:, start : start + size] = times(moved, low, high, slice(0, size)).astype(LOW)
        start += size
    queries, keys, values = joined[:, :width], joined[:, width : 2 * width], joined[:, 2 * width :]
    lane = lax.broadcasted_iota(jnp.int32, (count, LANES), 1)
    sums = jnp.zeros((count, LANES), WIDE)
    for pair in range(HEADS // 2):
        scores = scores_of(queries, head_pair(keys, pair), pair, length)
        probs = []
        for one in range(2):
            mine = scores[:, one * count : (one + 1) * count]
            top = jnp.max(mine, axis=-1, keepdims=True)
            total = top + jnp.log(jnp.sum(jnp.exp(mine - top), axis=-1, keepdims=True))
            sums = jnp.where(lane == 2 * pair + one, total, sums)
            probs.append(jnp.exp(mine - total).astype(LOW))
        both[:, width + pair * LANES : width + (pair + 1) * LANES] = dot(
            jnp.concatenate(probs, axis=1), head_pair(values, pair)
        ).astype(LOW)
    totals[...] = sums
    moved = dot(both[:, width:], place_of(rows2, width)).astype(LOW)
    attn = times(moved, low2, high2, slice(width, 2 * width))
    attn_out[...] = attn
    middle = tok + mod[:, 2 * width : 3 * width] * attn
    middle_out[...] = middle
    unit, _ = center_of(middle)
    second = (unit * (1.0 + mod[:, 4 * width : 5 * width]) + mod[:, 3 * width : 4 * width]).astype(LOW)
    start = 0
    for part in parts:
        part[...] = second[:, start : start + part.shape[1]]
        start += part.shape[1]


def backward_body(
    where, tokens, cotangent, modulation, lengths, rows0, rows1, rows2, low0, high0, low1, high1, low2, high2,
    joined, totals, attn_in, middle_in, near0, far0, near1, far1,
    grad_tokens, sent, d_mod, d_rows, d_cols,
):
    count, width = tokens.shape
    length = lengths[0]
    mod = modulation[...]
    start = 0
    for low, high in ((near0, far0), (near1, far1)):
        size = low.shape[1]
        d_rows[:, start : start + size] = low[...].astype(WIDE) + high[...].astype(WIDE)
        start += size
    d_second = d_rows[...]
    attn = attn_in[...]
    unit, scale = center_of(middle_in[...])
    d_mod[:, 3 * width : 4 * width] = jnp.sum(d_second, axis=0, keepdims=True)
    d_mod[:, 4 * width : 5 * width] = jnp.sum(d_second * unit, axis=0, keepdims=True)
    d_middle = cotangent[...].astype(WIDE) + norm_back(
        d_second * (1.0 + mod[:, 4 * width : 5 * width]), unit, scale
    )
    d_mod[:, 2 * width : 3 * width] = jnp.sum(d_middle * attn, axis=0, keepdims=True)
    d_attn = (mod[:, 2 * width : 3 * width] * d_middle).astype(LOW)
    d_cols[:, 3 * width :] = d_attn
    d_attended = dot_nt(
        times_back(d_attn, low2, high2, slice(width, 2 * width)).astype(LOW), place_of(rows2, width)
    ).astype(LOW)
    queries, keys, values = joined[:, :width], joined[:, width : 2 * width], joined[:, 2 * width :]
    sums = totals[...]
    lane = lax.broadcasted_iota(jnp.int32, (count, LANES), 1)
    factor = HEAD_DIM ** (-0.5)
    for pair in range(HEADS // 2):
        at = slice(pair * LANES, (pair + 1) * LANES)
        k_pair, v_pair = head_pair(keys, pair), head_pair(values, pair)
        scores = scores_of(queries, k_pair, pair, length)
        d_probs = dot_nt(d_attended[:, at], v_pair)
        probs_low, d_scores_low = [], []
        for one in range(2):
            half = slice(one * count, (one + 1) * count)
            total = jnp.sum(jnp.where(lane == 2 * pair + one, sums, 0.0), axis=1, keepdims=True)
            probs = jnp.exp(scores[:, half] - total)
            back = d_probs[:, half]
            d_scores = probs * (back - jnp.sum(probs * back, axis=-1, keepdims=True))
            probs_low.append(probs.astype(LOW))
            d_scores_low.append(d_scores.astype(LOW))
        d_scores_both = jnp.concatenate(d_scores_low, axis=1)
        d_cols[:, at] = (dot(d_scores_both, k_pair) * factor).astype(LOW)
        q_pair, d_pair = queries[:, at], d_attended[:, at]
        d_k = dot_tn(d_scores_both, q_pair) * factor
        d_v = dot_tn(jnp.concatenate(probs_low, axis=1), d_pair)
        d_k = jnp.where(lane < HEAD_DIM, d_k[:count], d_k[count:])
        d_v = jnp.where(lane < HEAD_DIM, d_v[:count], d_v[count:])
        d_cols[:, width + pair * LANES : width + (pair + 1) * LANES] = d_k.astype(LOW)
        d_cols[:, 2 * width + pair * LANES : 2 * width + (pair + 1) * LANES] = d_v.astype(LOW)
    d_first = jnp.zeros((count, width), WIDE)
    start = 0
    for rows, low, high in ((rows0, low0, high0), (rows1, low1, high1), (rows2, low2, high2)):
        size = min(low.shape[1], 3 * width - start)
        part = times_back(d_cols[:, start : start + size], low, high, slice(0, size))
        start += size
        place = place_of(rows, width)
        top = part.astype(LOW)
        rest = (part - top.astype(WIDE)).astype(LOW)
        d_first += dot_nt(top, place) + dot_nt(rest, place)
    unit, scale = center_of(tokens[...].astype(WIDE))
    d_mod[:, :width] = jnp.sum(d_first, axis=0, keepdims=True)
    d_mod[:, width : 2 * width] = jnp.sum(d_first * unit, axis=0, keepdims=True)
    grad_tokens[...] = d_middle + norm_back(
        d_first * (1.0 + mod[:, width : 2 * width]), unit, scale
    )
    experts = sent.shape[0]
    cols, out_cols = 3 * width // experts, width // experts
    for expert in range(experts):
        to = expert ^ where[1]
        sent[to, :, :cols] = d_cols[:, expert * cols : (expert + 1) * cols]
        sent[to, :, cols:] = d_cols[:, 3 * width + expert * out_cols : 3 * width + (expert + 1) * out_cols]


def join_rows(lows, highs, shares, rows):
    start = 0
    for low, high, share in zip(lows, highs, shares):
        for at, part in enumerate((low, high)):
            half = rows.shape[0] // 2
            rows[at * half : (at + 1) * half, start : start + share] = part[..., :share].reshape(half, share)
        start += share


def cut_rows(values, shares, refs):
    start = 0
    for ref, share in zip(refs, shares):
        ref[..., :share] = values[:, start : start + share].reshape(ref.shape[:-1] + (share,))
        start += share


def d_act_body(shares, *refs):
    lows, highs, (down, d_act, rows) = refs[:2], refs[2:4], refs[4:]
    join_rows(lows, highs, shares, rows)
    d_act[0] = dot_nt(rows[...], down[...]).astype(LOW)


def hidden_body(shares, routed, *refs):
    lows, highs, sides, mine, d_act, up = refs[:2], refs[2:4], refs[4:6], refs[6], refs[7], refs[8]
    back_lows, back_highs, (d_pre, act, pairs, rows) = refs[9:11], refs[11:13], refs[13:]
    join_rows(lows, highs, shares, rows)
    half = rows.shape[0] // 2
    for at, (side, backs) in enumerate(zip(sides, (back_lows, back_highs))):
        here = slice(at * half, (at + 1) * half)
        weight = jnp.sum(side[...].reshape(half, LANES).astype(WIDE) * mine[...], axis=1, keepdims=True)
        pre = dot(rows[here], up[...])
        square = pre * pre
        bend = jnp.tanh(pre * (CURVE + (CURVE * CUBIC) * square))
        gate = 0.5 + 0.5 * bend
        hidden = pre * gate
        slope = gate + hidden * (1.0 - bend) * (CURVE + (3.0 * CURVE * CUBIC) * square)
        d_hidden = d_act[0, here].astype(WIDE)
        d_full = d_hidden * slope
        d_low = jnp.concatenate([d_full[:, :routed] * weight, d_full[:, routed:]], axis=1).astype(LOW)
        d_pre[0, here] = d_low
        act[0, here] = jnp.concatenate([hidden[:, :routed] * weight, hidden[:, routed:]], axis=1).astype(LOW)
        pair = jnp.sum(hidden[:, :routed] * d_hidden[:, :routed], axis=1, keepdims=True)
        pairs[0, here] = (pair * mine[...]).astype(LOW)
        cut_rows(dot_nt(d_low, up[...]).astype(LOW), shares, backs)


def branch_body(shares, act, pairs, down, *refs):
    half = act.shape[1] // 2
    for at, parts in enumerate((refs[:2], refs[2:])):
        here = slice(at * half, (at + 1) * half)
        cut_rows(dot(act[0, here], down[...]).astype(LOW), shares, parts)
        parts[0][..., shares[0] :] = pairs[0, here].reshape(parts[0].shape[:-1] + (LANES,))


def grads_body(shares, write, where, *refs):
    second, d_mlp, d_pre, act = refs[:4], refs[4:8], refs[8], refs[9]
    outs, (rows, up_sum, down_sum) = refs[10:-3], refs[-3:]
    step = pl.program_id(0)

    @pl.when(step == 0)
    def _():
        up_sum[...] = jnp.zeros(up_sum.shape, WIDE)
        down_sum[...] = jnp.zeros(down_sum.shape, WIDE)

    join_rows(second[:2], second[2:], shares, rows)
    up_sum[...] += dot_tn(rows[...], d_pre[0])
    join_rows(d_mlp[:2], d_mlp[2:], shares, rows)
    down_sum[...] += dot_tn(act[0], rows[...])

    @pl.when(step == pl.num_programs(0) - 1)
    def _():
        write(where, up_sum, down_sum, outs)


def write_whole(where, up_sum, down_sum, outs):
    outs[0][...] = up_sum[...]
    outs[1][...] = down_sum[...]


def place_and_twin(where):
    return where[2] // 2, where[2] % 2


def rows_at(number, size):
    return pl.ds(pl.multiple_of(number * size, 16), size)


def lanes_at(number, size):
    return pl.ds(pl.multiple_of(number * size, LANES), size)


def up_sent_body(where, weight, *outs):
    place, _ = place_and_twin(where)
    for at, out in enumerate(outs):
        out[...] = weight[:, lanes_at(place ^ at, out.shape[1])]


def up_join_body(where, own, shared, other, shared_other, full):
    place, twin = place_and_twin(where)
    rows, cols = own.shape[1], own.shape[2]
    for at in range(own.shape[0]):
        full[rows_at(2 * (place ^ at) + twin, rows), :cols] = own[at]
        full[rows_at(2 * (place ^ at) + 1 - twin, rows), :cols] = other[at]
    size = shared.shape[1]
    blank = jnp.zeros((full.shape[0], LANES - size), LOW)
    for at, piece in enumerate((shared, shared_other)):
        start = cols + at * LANES
        full[:, start : start + size] = piece[...]
        full[:, start + size : start + LANES] = blank


def down_join_body(where, own, shared, other, shared_other, full):
    _, twin = place_and_twin(where)
    rows = own.shape[0]
    full[rows_at(twin, rows)] = own[...]
    full[rows_at(1 - twin, rows)] = other[...]
    size = shared.shape[0]
    blank = jnp.zeros((LANES - size, full.shape[1]), LOW)
    for at, piece in enumerate((shared, shared_other)):
        start = 2 * rows + at * LANES
        full[start : start + size] = piece[...]
        full[start + size : start + LANES] = blank


def write_twins(where, up_sum, down_sum, outs):
    keep_up, send_up, keep_down, send_down = outs
    place, twin = place_and_twin(where)
    rows, units = keep_up.shape[1], 2 * (down_sum.shape[0] - 2 * LANES) // 2
    size = (keep_up.shape[2] - units) // 2
    mine, other = slice(units, units + size), slice(units + LANES, units + LANES + size)
    for out, at_twin, order_ in ((keep_up, twin, (mine, other)), (send_up, 1 - twin, (other, mine))):
        for at in range(out.shape[0]):
            here = rows_at(2 * (place ^ at) + at_twin, rows)
            out[at, :, :units] = up_sum[here, :units].astype(LOW)
            for number, cols in enumerate(order_):
                start = units + number * size
                out[at, :, start : start + size] = up_sum[here, cols].astype(LOW)
    half = units // 2
    for out, at_twin, rows_ in ((keep_down, twin, mine), (send_down, 1 - twin, other)):
        out[:half] = down_sum[rows_at(at_twin, half)].astype(out.dtype)
        out[half:] = down_sum[rows_].astype(out.dtype)


def twins_body(keep_up, got_up, keep_down, got_down, grad_down, shared_down, *ups):
    for at, out in enumerate(ups):
        out[...] = (keep_up[at].astype(WIDE) + got_up[at].astype(WIDE)).astype(LOW)
    half = grad_down.shape[0]
    grad_down[...] = keep_down[:half] + got_down[:half].astype(WIDE)
    shared_down[...] = (keep_down[half:] + got_down[half:].astype(WIDE)).astype(LOW)


def up_rows_body(where, up0, up1, up2, up3, shared_down, grad_up, sent):
    place, twin = place_and_twin(where)
    expert = where[1]
    units = grad_up.shape[1] // 4
    size = (up0.shape[1] - units) // 2
    cols = sent.shape[2] - 2 * size
    for at, piece in enumerate((up0, up1, up2, up3)):
        grad_up[:, lanes_at(place ^ at, units)] = piece[:, :units].astype(WIDE)
        mine, other = piece[:, units : units + size], piece[:, units + size :]
        sent[(place ^ at) ^ expert, :, :size] = jnp.where(twin == 0, mine, other)
        sent[(place ^ at) ^ expert, :, size : 2 * size] = jnp.where(twin == 0, other, mine)
    for to in range(4):
        sent[to ^ expert, :, 2 * size :] = shared_down[:, to * cols : (to + 1) * cols]


def shared_rows_body(where, got0, got1, got2, got3, grad_up, grad_down, held):
    expert = where[1]
    for at, got in enumerate((got0, got1, got2, got3)):
        held[at ^ expert] = got[...]
    size = grad_up.shape[1] // 8
    for source in range(4):
        for twin in range(2):
            start = (4 * twin + source) * size
            grad_up[:, start : start + size] = held[source, :, twin * size : (twin + 1) * size].astype(WIDE)
        grad_down[source * size : (source + 1) * size] = held[source, :, 2 * size :].astype(WIDE)


def attn_terms_body(masks, where, both, cols0, cols1, cols2, cols3, low0, low1, high0, high1, term):
    expert, group = where[1], where[2]
    width = both.shape[2] // 2
    cut = 3 * width // 4
    rows = low0.shape[1]
    for at, cols in enumerate((cols0, cols1, cols2, cols3)):
        inputs = both[expert ^ at]
        parts = (dot_tn(inputs[:, :width], cols[:, :cut]), dot_tn(inputs[:, width:], cols[:, cut:]))
        for start, part in ((0, parts[0]), (cut, parts[1])):
            here = slice(start, start + part.shape[1])
            if at:
                term[:, here] += part
            else:
                term[:, here] = part
    half = width // 2
    for number, (low, high) in enumerate(((low0, high0), (low1, high1))):
        for at, mask in enumerate(masks[number]):
            ref = low if at < 4 else high
            ref[at % 4] = term[rows_at(group ^ mask, rows), number * half : (number + 1) * half].astype(LOW)


def attn_out_body(near0, far0, near1, far1, grad_qkv, grad_out, total):
    half = near0.shape[1]
    for at, (near, far) in enumerate(((near0, far0), (near1, far1))):
        total[:, at * half : (at + 1) * half] = near[...].astype(WIDE) + far[...].astype(WIDE)
    cut = grad_qkv.shape[1]
    grad_qkv[...] = total[:, :cut]
    grad_out[...] = total[:, cut:]


def finish_body(
    cotangent, modulation, middle, kept, d_mod, near0, far0, near1, far1, block_out, grad_gates, sent, branch
):
    count, width = cotangent.shape
    start = 0
    for number, (low, high) in enumerate(((near0, far0), (near1, far1))):
        total = low[...].astype(WIDE) + high[...].astype(WIDE)
        if number == 0:
            pairs = total[:, -LANES:]
            total = total[:, :-LANES]
        branch[:, start : start + total.shape[1]] = total
        start += total.shape[1]
    block_out[...] = middle[...] + modulation[:, 5 * width :] * branch[...]
    for choice in range(2):
        grad_gates[:, choice : choice + 1] = jnp.sum(kept[choice] * pairs, axis=1, keepdims=True)
    d_gate = jnp.sum(cotangent[...].astype(WIDE) * branch[...], axis=0, keepdims=True)
    for at in range(sent.shape[1]):
        cols = slice(at * LANES, (at + 1) * LANES)
        if at * LANES < 5 * width:
            line = d_mod[:, cols]
        else:
            line = d_gate[:, at * LANES - 5 * width : (at + 1) * LANES - 5 * width]
        sent[:, at, :] = jnp.broadcast_to(line.astype(LOW), (sent.shape[0], LANES))


def ada_body(experts, where, got, cond, weight, grad_weight, grad_bias, sent, d_mod):
    expert = where[1]
    total, lines, _ = got.shape
    for at in range(lines):
        d_mod[:, at * LANES : (at + 1) * LANES] = got[:, at, :]
    grad_bias[...] = jnp.sum(d_mod[...].astype(WIDE), axis=0, keepdims=True)
    cols = grad_weight.shape[1]
    mine = d_mod[:, pl.ds(pl.multiple_of(expert * cols, LANES), cols)]
    grad_weight[...] = dot_tn(cond[:, 0, :], mine)[: grad_weight.shape[0]]
    piece = weight.shape[0]
    back = dot_nt(d_mod[...], weight[...])
    sent[...] = jnp.zeros(sent.shape, WIDE)
    sent[:, 0, :piece] = back


def attn_grads_body(both, d_cols, out):
    experts, count, cols = d_cols.shape
    width = both.shape[2] // 2
    groups, rows, _ = out.shape
    flat = d_cols[...].reshape(experts * count, cols)
    inputs = both[...].reshape(experts * count, 2 * width)
    cut = 3 * cols // 4
    out[...] = jnp.concatenate(
        [dot_tn(inputs[:, :width], flat[:, :cut]), dot_tn(inputs[:, width:], flat[:, cut:])], axis=1
    ).astype(LOW).reshape(groups, rows, cols)


def attn_sum_body(got, grad_qkv, grad_out):
    total = jnp.sum(got[...].astype(WIDE), axis=0)
    cut = grad_qkv.shape[1]
    grad_qkv[...] = total[:, :cut]
    grad_out[...] = total[:, cut:]


def up_out_body(units, got, grad_up):
    for group in range(got.shape[0]):
        grad_up[:, group * units : (group + 1) * units] = got[group, :, :units].astype(WIDE)


def gather_far(pieces, masks):
    found = [pieces]
    for mask in masks:
        found = found + [[swap(piece, mask) for piece in held] for held in found]
    return found


def shards(
    tokens,
    cond,
    lengths,
    routes,
    gate_weights,
    ada_weight,
    ada_bias,
    qkv_weight,
    out_weight,
    shared_up,
    shared_down,
    expert_up,
    expert_down,
    cotangent,
):
    count, width = tokens.shape
    experts = lax.axis_size("expert")
    groups = lax.axis_size("batch")
    total = experts * groups
    me = lax.axis_index(AXES)
    my_expert = lax.axis_index("expert")
    my_group = lax.axis_index("batch")
    where = jnp.stack([me, my_expert, my_group]).astype(jnp.int32)
    capacity = 5 * 2 * count // (4 * experts)
    piece = ada_weight.shape[0]
    group_rows = width // groups
    shares = [width * share // sum(SPLIT) for share in SPLIT]

    expert_masks = bits_of(experts)
    group_masks = [experts * step for step in bits_of(groups)]
    away = list(reversed(group_masks[1:3]))
    far = group_masks[:1] + group_masks[3:]
    core, across = expert_masks[:1], expert_masks[1:]
    team_links = [away + across, across + away]
    steps = 2 ** len(across)
    paired = groups == 8 and experts == 4
    away_masks = order(sorted(away))
    weight_links = [
        across + far[:1] + far[1:] + away,
        far[:1] + far[1:] + away + across,
        far[1:] + away + across + far[:1],
    ]

    side, kept, sent = call(
        functools.partial(route_body, experts, capacity, groups),
        [((count, LANES), LOW), ((2, count, LANES), WIDE), ((total, 16, LANES), LOW)],
        (routes, gate_weights, lengths, cond),
        smem=(2,),
    )

    cond_all = lax.all_to_all(sent, AXES, split_axis=0, concat_axis=0, tiled=True)
    if paired:
        place_units = expert_up.shape[2] // 4
        up_sent = call(
            up_sent_body,
            [((group_rows, place_units), LOW)] * 4,
            (where, expert_up[0]),
            smem=(0,),
        )
        up_pieces = [piece if not mask else swap(piece, mask) for piece, mask in zip(up_sent, away_masks)]
        down_own = [expert_down[0], shared_down]
        down_other = [swap(piece, far[0]) for piece in down_own]
        cond_all = tie(cond_all, *up_pieces, *down_other)
    terms, loads = call(
        terms_body,
        [((total, 6 * width // LANES, LANES), LOW), ((1, LANES), WIDE)],
        (where, cond_all, ada_weight, ada_bias[None]),
        smem=(0,),
    )
    tallies = loads[0, group_rows : group_rows + experts + 1]
    expert_load = tallies[:experts] * experts / (2.0 * tallies[experts])
    terms_got = lax.all_to_all(terms, AXES, split_axis=0, concat_axis=0, tiled=True)
    modulation, *d_mlps = call(
        shift_body,
        [
            ((1, 6 * width), WIDE),
            *[((count, share + (0 if at else LANES)), LOW) for at, share in enumerate(shares)],
        ],
        (terms_got, cotangent, side),
    )

    wide_cut = 4 * width // sum(SHARES)
    own = [
        qkv_weight[:, :wide_cut],
        qkv_weight[:, wide_cut : 3 * wide_cut],
        jnp.concatenate([qkv_weight[:, 3 * wide_cut :], out_weight], axis=1),
    ]
    weights = []
    lows = []
    row_places = []
    for part, links in zip(own, weight_links):
        low = spread(part[None], links, {2: [terms]})
        lows.append(low)
        high = swap(low, core[0])
        weights += [low.reshape(-1, part.shape[1]), high.reshape(-1, part.shape[1])]
        found = jnp.array(order(links + core), jnp.int32) ^ me
        row_places.append((found[:, None] * piece + jnp.arange(piece, dtype=jnp.int32)).reshape(1, -1))

    tall = (count, width)
    both, joined, totals, attn, middle, *seconds = call(
        forward_body,
        [
            ((count, 2 * width), LOW),
            ((count, 3 * width), LOW),
            ((count, LANES), WIDE),
            (tall, WIDE),
            (tall, WIDE),
            *[((count, share), LOW) for share in shares],
        ],
        (tokens, modulation, lengths, *row_places, *weights),
        smem=(2,),
    )

    part_shared_up = lax.all_to_all(tie(shared_up, terms_got), AXES, split_axis=1, concat_axis=0, tiled=True)
    shared_units = part_shared_up.shape[1]
    units = expert_down.shape[1]
    shared_slot = up_to(shared_units, LANES)
    if paired:
        routed, hidden = 2 * units, 2 * units + 2 * shared_slot
        up_own = [jnp.stack(up_pieces), part_shared_up]
        up_other = [swap(piece, far[0]) for piece in up_own]
        (up_cat,) = call(
            up_join_body, [((width, hidden), LOW)], (where, *up_own, *up_other), smem=(0,)
        )
        (down_cat,) = call(
            down_join_body, [((hidden, width), LOW)], (where, *down_own, *down_other), smem=(0,)
        )
    else:
        part_up = lax.all_to_all(expert_up[0], "batch", split_axis=1, concat_axis=0, tiled=True)
        held = gather_far([part_up, part_shared_up, expert_down[0], shared_down], far)
        slot = up_to(units, LANES)
        routed, hidden = len(held) * slot, len(held) * (slot + shared_slot)
        up_cat = jnp.concatenate(
            [pad_lanes(h[0], slot) for h in held] + [pad_lanes(h[1], shared_slot) for h in held], axis=1
        )
        down_cat = jnp.concatenate(
            [pad_lanes(h[2].T, slot).T for h in held] + [pad_lanes(h[3].T, shared_slot).T for h in held], axis=0
        )

    def whole(array):
        return array, array.shape, lambda step: (0,) * array.ndim

    half = 4 * count

    def block_at(links, lanes, lane_block=0):
        bits = list(reversed(links))
        block = tuple(2 if mask in away else None for mask in bits) + (count, lanes)

        def index(step):
            spot = {mask: step // 2**at % 2 for at, mask in enumerate(across)}
            return tuple(spot.get(mask, 0) for mask in bits) + (0, lane_block)

        return block, index

    def block_in(array, links, lanes=None, lane_block=0):
        flat = array.reshape((2,) * len(links) + array.shape[1:])
        return flat, *block_at(links, lanes or array.shape[-1], lane_block)

    def block_out_of(lanes, links):
        return (2,) * len(links) + (count, lanes), LOW, *block_at(links, lanes)

    def rows_of(array):
        return array, (1,) + array.shape[1:], lambda step: (step, 0, 0)

    def rows_out(lanes):
        return (steps, 2 * half, lanes), LOW, (1, 2 * half, lanes), lambda step: (step, 0, 0)

    def parts_in(lows, highs, orders):
        return [block_in(part, links) for parts in (lows, highs) for part, links in zip(parts, orders)]

    def flat(part):
        return part.reshape((-1,) + part.shape[-2:])

    d_low = list(tie(tuple(part[None] for part in d_mlps), *lows))
    second_low = [part[None] for part in seconds]
    seen = seconds
    for at in range(len(team_links[0])):
        d_got = [swap(part, links[at]) for part, links in zip(d_low, team_links)]
        got = [swap(part, links[at]) for part, links in zip(second_low, team_links)]
        if at == 2:
            got = tie(tuple(got), up_cat)
        d_got = tie(tuple(d_got), *seen)
        d_low = [jnp.concatenate(pair, axis=0) for pair in zip(d_low, d_got)]
        second_low = [jnp.concatenate(pair, axis=0) for pair in zip(second_low, got)]
        seen = second_low
    d_high = [swap(part, core[0]) for part in d_low]
    (d_act,) = sweep(
        functools.partial(d_act_body, shares),
        steps,
        [*parts_in(d_low, d_high, team_links), whole(down_cat)],
        [rows_out(hidden)],
        scratch=[((2 * half, width), LOW)],
    )

    second_low = tie(tuple(second_low), d_act)
    second_high = [swap(part, core[0]) for part in second_low]
    lane = jnp.arange(LANES, dtype=jnp.int32)[None, :]
    mine = ((lane == my_expert) | (lane == my_expert + experts)).astype(WIDE)
    back = [block_out_of(share, links) for links, share in zip(team_links, shares)]
    *back_parts, d_pre, act, pairs = sweep(
        functools.partial(hidden_body, shares, routed),
        steps,
        [
            *parts_in(second_low, second_high, team_links),
            block_in(d_low[0], team_links[0], LANES, shares[0] // LANES),
            block_in(d_high[0], team_links[0], LANES, shares[0] // LANES),
            whole(mine),
            rows_of(d_act),
            whole(up_cat),
        ],
        [*back, *back, rows_out(hidden), rows_out(hidden), rows_out(LANES)],
        scratch=[((2 * half, width), LOW)],
    )
    back_parts = [flat(part) for part in back_parts]
    wider = [block_out_of(share + (0 if row else LANES), team_links[row]) for row, share in enumerate(shares)]
    branch_parts = sweep(
        functools.partial(branch_body, shares),
        steps,
        [rows_of(act), rows_of(pairs), whole(down_cat)],
        [*wider, *wider],
    )
    branch_parts = [flat(part) for part in branch_parts]

    def sum_out(shape, kind):
        return shape, kind, shape, lambda step: (0,) * len(shape)

    if paired:
        lanes = place_units + 2 * shared_units
        sum_outs = [
            sum_out((4, group_rows, lanes), LOW),
            sum_out((4, group_rows, lanes), LOW),
            sum_out((units + shared_units, width), WIDE),
            sum_out((units + shared_units, width), LOW),
        ]
    else:
        sum_outs = [sum_out((width, hidden), WIDE), sum_out((hidden, width), WIDE)]
    grads = sweep(
        functools.partial(grads_body, shares, write_twins if paired else write_whole),
        steps,
        [
            (where, None, None),
            *parts_in(second_low, second_high, team_links),
            *parts_in(d_low, d_high, team_links),
            rows_of(d_pre),
            rows_of(act),
        ],
        sum_outs,
        scratch=[((2 * half, width), LOW), ((width, hidden), WIDE), ((hidden, width), WIDE)],
    )
    if paired:
        twin_up, twin_down = swap(grads[1], far[0]), swap(grads[3], far[0])

    core_last = [links + core for links in team_links]
    folded, steps_sent = fold(
        back_parts[:2], back_parts[2:], core_last, {0: [branch_parts[0]], 1: [grads[0]]}
    )

    grad_tokens, d_cols, d_mod = call(
        backward_body,
        [(tall, WIDE), ((experts, count, 4 * width // experts), LOW), ((1, 5 * width), WIDE)],
        (
            where, tokens, cotangent, modulation, lengths, *row_places, *weights,
            joined, totals, attn, middle, *folded,
        ),
        scratch=[(tall, WIDE), ((count, 4 * width), LOW)],
        smem=(0, 4),
    )
    branch_parts = tie(tuple(branch_parts), *steps_sent[2])
    branch_terms, _ = fold(branch_parts[:2], branch_parts[2:], core_last, {1: [d_cols]})
    block_out, grad_gate_weights, sent = call(
        finish_body,
        [(tall, WIDE), ((count, 2), WIDE), ((total, 6 * width // LANES, LANES), LOW)],
        (
            cotangent, modulation, middle, kept, d_mod, *branch_terms,
        ),
        scratch=[(tall, WIDE)],
    )

    both_group = lax.all_gather(tie(both, *second_high), "expert", axis=0)
    if paired:
        cols_got = [d_cols[at] if not at else swap(d_cols[at], at) for at in range(4)]
        sum_links = [group_masks[1:] + group_masks[:1], group_masks[:1] + group_masks[1:]]
        sum_masks = [[mask // experts for mask in order(links)] for links in sum_links]
        term_half = ((4, group_rows, width // 2), LOW)
        attn_sent = call(
            functools.partial(attn_terms_body, sum_masks),
            [term_half] * 4,
            (where, both_group, *cols_got),
            scratch=[((width, width), WIDE)],
            smem=(0,),
        )
        attn_got, _ = fold(attn_sent[:2], attn_sent[2:], sum_links)
        grad_qkv, grad_out = call(
            attn_out_body,
            [((group_rows, 3 * width // experts), WIDE), ((group_rows, width // experts), WIDE)],
            attn_got,
            scratch=[((group_rows, width), WIDE)],
        )
    else:
        natural = jnp.arange(experts, dtype=jnp.int32) ^ my_expert
        d_cols = jnp.take(d_cols, natural, axis=0)
        d_cols = lax.all_to_all(d_cols, "expert", split_axis=0, concat_axis=0, tiled=True)
        (attn_terms,) = call(
            attn_grads_body, [((groups, group_rows, 4 * width // experts), LOW)], (both_group, d_cols)
        )
        attn_terms = lax.all_to_all(attn_terms, "batch", split_axis=0, concat_axis=0, tiled=True)
        grad_qkv, grad_out = call(
            attn_sum_body,
            [((group_rows, 3 * width // experts), WIDE), ((group_rows, width // experts), WIDE)],
            (attn_terms,),
        )

    if paired:
        twin_up, twin_down = tie((twin_up, twin_down), d_cols)
        grad_expert_down, shared_own, *up_own = call(
            twins_body,
            [
                ((units, width), WIDE),
                ((shared_units, width), LOW),
                *[((group_rows, lanes), LOW)] * 4,
            ],
            (grads[0], twin_up, grads[2], twin_down),
        )
        up_got = [piece if not mask else swap(piece, mask) for piece, mask in zip(up_own, away_masks)]
        up_got = tie(tuple(up_got), attn_sent[0])
        grad_expert_up, crossed = call(
            up_rows_body,
            [
                ((group_rows, groups * units), WIDE),
                ((4, group_rows, 2 * shared_units + width // experts), LOW),
            ],
            (where, *up_got, shared_own),
            smem=(0,),
        )
        crossed = [crossed[at] if not at else swap(crossed[at], at) for at in range(4)]
        grad_shared_up, grad_shared_down = call(
            shared_rows_body,
            [((group_rows, width), WIDE), ((experts * shared_units, width // experts), WIDE)],
            (where, *crossed),
            scratch=[((4, group_rows, 2 * shared_units + width // experts), LOW)],
            smem=(0,),
        )
    else:
        grad_up, grad_down = grads
        replicas = hidden // (slot + shared_slot)
        sums = []
        for taken, size, first in ((grad_up.T, units, 0), (grad_up.T, shared_units, routed), (grad_down, units, 0), (grad_down, shared_units, routed)):
            room = up_to(size, LANES)
            held = [taken[first + at * room : first + at * room + size] for at in range(replicas)]
            for mask in reversed(far):
                some = len(held) // 2
                held = [
                    low + swap(high.astype(LOW), mask).astype(WIDE) for low, high in zip(held[:some], held[some:])
                ]
            sums.append(held[0])
        grad_expert_down = sums[2]
        up_rows = jnp.concatenate([sums[0].T, sums[1].T], axis=1).astype(LOW).reshape(groups, group_rows, -1)
        up_rows = lax.all_to_all(up_rows, "batch", split_axis=0, concat_axis=0, tiled=True)
        grad_shared_down = lax.all_to_all(
            sums[3].astype(LOW), "expert", split_axis=1, concat_axis=0, tiled=True
        ).astype(WIDE)
        (grad_expert_up,) = call(
            functools.partial(up_out_body, units), [((group_rows, groups * units), WIDE)], (up_rows,)
        )
        shared_rows = up_rows[:, :, units:].reshape(experts, groups // experts, group_rows, shared_units)
        shared_rows = lax.all_to_all(shared_rows, "expert", split_axis=0, concat_axis=0, tiled=True)
        grad_shared_up = shared_rows.transpose(2, 1, 0, 3).reshape(group_rows, groups * shared_units).astype(WIDE)

    d_mod_all = lax.all_to_all(sent, AXES, split_axis=0, concat_axis=0, tiled=True)
    grad_ada_weight, grad_ada_bias, sent = call(
        functools.partial(ada_body, experts),
        [((group_rows, 6 * width // experts), WIDE), ((1, 6 * width), WIDE), ((total, 8, LANES), WIDE)],
        (where, d_mod_all, cond_all, ada_weight),
        scratch=[((total, 6 * width), LOW)],
        smem=(0,),
    )
    d_cond_act = lax.all_to_all(sent, AXES, split_axis=0, concat_axis=0, tiled=True)
    d_cond_act = d_cond_act[:, 0, :piece].reshape(1, width)
    _, silu_back = jax.vjp(jax.nn.silu, cond.astype(WIDE))
    grad_cond = silu_back(d_cond_act)[0]

    return (
        block_out,
        grad_tokens,
        grad_cond,
        grad_gate_weights,
        grad_ada_weight,
        grad_ada_bias[0],
        grad_qkv,
        grad_out,
        grad_shared_up,
        grad_shared_down,
        grad_expert_up[None],
        grad_expert_down[None],
        expert_load,
    )


def solution(mesh):
    rows = P(AXES, None)
    line = P(AXES)
    tiles = P("batch", "expert")
    split = P("expert", "batch", None)
    in_specs = (rows, rows, line, rows, rows, rows, line, rows, rows, rows, rows, split, split, rows)
    out_specs = (rows, rows, rows, rows, tiles, P(), tiles, tiles, tiles, tiles, split, split, P())
    return jax.shard_map(shards, mesh=mesh, in_specs=in_specs, out_specs=out_specs, check_vma=False)
```

```python
import functools

import jax
import jax.numpy as jnp
import numpy as np
from jax import lax
from jax.experimental import pallas as pl
from jax.experimental.pallas import tpu as pltpu
from jax.sharding import PartitionSpec as P

HEADS = 12
HEAD_DIM = 64
AXES = ("batch", "expert")
LOW = jnp.bfloat16
WIDE = jnp.float32
LANES = 128
EXTRA = 16
CURVE = 0.7978845608028654
CUBIC = 0.044715


def dot(left, right):
    return lax.dot_general(left, right, (((1,), (0,)), ((), ())), preferred_element_type=WIDE)


def dot_nt(left, right):
    return lax.dot_general(left, right, (((1,), (1,)), ((), ())), preferred_element_type=WIDE)


def dot_tn(left, right):
    return lax.dot_general(left, right, (((0,), (0,)), ((), ())), preferred_element_type=WIDE)


def up_to(value, step):
    return -(-value // step) * step


def call(body, outs, args, scratch=(), smem=(), limit=48):
    specs = [pl.BlockSpec(memory_space=pltpu.SMEM) if at in smem else pl.BlockSpec() for at in range(len(args))]
    return pl.pallas_call(
        body,
        out_shape=[jax.ShapeDtypeStruct(shape, kind) for shape, kind in outs],
        in_specs=specs,
        out_specs=[pl.BlockSpec()] * len(outs),
        scratch_shapes=[pltpu.VMEM(shape, kind) for shape, kind in scratch],
        compiler_params=pltpu.CompilerParams(vmem_limit_bytes=limit * 1024 * 1024),
    )(*args)


def sweep(body, steps, ins, outs, scratch=(), limit=56):
    return pl.pallas_call(
        body,
        out_shape=[jax.ShapeDtypeStruct(shape, kind) for shape, kind, _, _ in outs],
        grid=(steps,),
        in_specs=[
            pl.BlockSpec(memory_space=pltpu.SMEM) if block is None else pl.BlockSpec(block, index)
            for _, block, index in ins
        ],
        out_specs=[pl.BlockSpec(block, index) for _, _, block, index in outs],
        scratch_shapes=[pltpu.VMEM(shape, kind) for shape, kind in scratch],
        compiler_params=pltpu.CompilerParams(vmem_limit_bytes=limit * 1024 * 1024),
    )(*[array for array, _, _ in ins])


def pad_lanes(values, width):
    return jnp.pad(values, ((0, 0),) * (values.ndim - 1) + ((0, width - values.shape[-1]),))


def tie(values, *others):
    return lax.optimization_barrier((values, *others))[0]


def together(*values):
    leaves, tree = jax.tree.flatten(values)
    return jax.tree.unflatten(tree, lax.optimization_barrier(tuple(leaves)))


def grown(values, got):
    return jnp.concatenate([values, got], axis=0)


def added(low, got):
    half = ((low.shape[0] // 2,) + low.shape[1:], low.dtype)
    return call(add_body, [half, half], (low, got))


def bits_of(count):
    found = []
    step = 1
    while step < count:
        found.append(step)
        step *= 2
    assert step == count
    return found


def swap(values, mask):
    total = lax.axis_size("batch") * lax.axis_size("expert")
    return lax.ppermute(values, AXES, [(at, at ^ mask) for at in range(total)])


def spread(values, masks, waits=()):
    waits = dict(waits)
    for at, mask in enumerate(masks):
        if at in waits:
            values = tie(values, *waits[at])
        values = jnp.concatenate([values, swap(values, mask)], axis=0)
    return values


def order(masks):
    found = [0]
    for mask in masks:
        found = found + [at ^ mask for at in found]
    return found


def add_body(low, got, keep, send):
    half = keep.shape[0]
    keep[...] = (low[:half].astype(WIDE) + got[:half].astype(WIDE)).astype(keep.dtype)
    send[...] = (low[half:].astype(WIDE) + got[half:].astype(WIDE)).astype(send.dtype)


def fold(lows, highs, orders, waits=()):
    waits = dict(waits)
    lows, highs, sent = list(lows), list(highs), []
    for at in range(len(orders[0]) - 1):
        sent.append(list(highs))
        got = [swap(high, links[-1 - at]) for high, links in zip(highs, orders)]
        if at in waits:
            got = tie(tuple(got), *waits[at])
        for part, other in enumerate(got):
            half = ((other.shape[0] // 2,) + other.shape[1:], other.dtype)
            lows[part], highs[part] = call(add_body, [half, half], (lows[part], other))
    sent.append(list(highs))
    got = [swap(high, links[0]) for high, links in zip(highs, orders)]
    return [half[0] for pair in zip(lows, got) for half in pair], sent


def center_of(values):
    center = values - jnp.mean(values, axis=-1, keepdims=True)
    scale = lax.rsqrt(jnp.mean(center * center, axis=-1, keepdims=True) + 1e-06)
    return center * scale, scale


def norm_back(grad, unit, scale):
    return scale * (
        grad
        - jnp.mean(grad, axis=-1, keepdims=True)
        - unit * jnp.mean(grad * unit, axis=-1, keepdims=True)
    )


def route_body(experts, capacity, groups, routes, gates, lengths, cond, weight, kept, sent):
    count, width = routes.shape[1], cond.shape[1]
    lane = lax.broadcasted_iota(jnp.int32, (8, count), 1)
    row = lax.broadcasted_iota(jnp.int32, (8, count), 0)
    length = lengths[0]
    live = lane < length
    first = (row == routes[0:1]) & live
    second = (row == routes[1:2]) & live
    hits = first.astype(WIDE) + second.astype(WIDE)
    above = (
        lax.broadcasted_iota(jnp.int32, (count, count), 0)
        < lax.broadcasted_iota(jnp.int32, (count, count), 1)
    ).astype(LOW)
    room = (dot(hits.astype(LOW), above) < capacity).astype(WIDE)
    first = first.astype(WIDE) * room
    second = second.astype(WIDE) * room
    weight[...] = first * gates[0:1] + second * gates[1:2]
    kept[0] = first
    kept[1] = second
    rows = width // groups
    tally = jnp.sum(hits, axis=1, keepdims=True)
    spot = lax.broadcasted_iota(jnp.int32, (8, LANES), 1)
    line = lax.broadcasted_iota(jnp.int32, (8, LANES), 0)
    tally = jnp.sum(jnp.where(spot == line + rows, tally, 0.0), axis=0, keepdims=True)
    spot = spot[:1]
    tally = jnp.where(spot == rows + experts, length.astype(WIDE), tally)
    value = cond[...].astype(WIDE)
    value = value / (1.0 + jnp.exp(-value))
    for group in range(groups):
        start = group * rows // LANES * LANES
        part = value[:, start : start + LANES]
        shift = group * rows - start
        if shift:
            tail = value[:, start + LANES : start + 2 * LANES] if start + 2 * LANES <= width else part
            part = jnp.where(
                spot < LANES - shift, pltpu.roll(part, LANES - shift, 1), pltpu.roll(tail, LANES - shift, 1)
            )
        part = jnp.where(spot < rows, part, tally).astype(LOW)
        for expert in range(experts):
            sent[group * experts + expert] = jnp.broadcast_to(part, sent.shape[1:])


def place_of(me, rows, piece, width):
    natural = (rows[0:1] ^ me) * piece + rows[1:2]
    return (lax.broadcasted_iota(jnp.int32, (width, width), 0) == natural).astype(LOW)


def terms_body(where, got, weight, bias, shared, out, loads):
    me, expert = where[0], where[1]
    total, _, _ = got.shape
    piece, wide = weight.shape
    rows = got[:, 0, :]
    pick = (
        lax.broadcasted_iota(jnp.int32, (LANES, piece), 0)
        == lax.broadcasted_iota(jnp.int32, (LANES, piece), 1) + expert * piece
    ).astype(LOW)
    share = bias.shape[1]
    spot = (
        lax.broadcasted_iota(jnp.int32, (share, wide), 1)
        == lax.broadcasted_iota(jnp.int32, (share, wide), 0) + me * share
    ).astype(LOW)
    terms = dot(dot(rows, pick).astype(LOW), weight[...]) + dot(bias[...], spot)
    terms = terms.astype(LOW)
    first = up_to(piece, 8)
    for at in range(wide // LANES):
        out[:, first + at, :] = terms[:, at * LANES : (at + 1) * LANES]
    cols = shared.shape[1] // total
    for at in range(total):
        out[at, :piece, :cols] = shared[:, at * cols : (at + 1) * cols]
    load = jnp.sum(rows.astype(WIDE), axis=0, keepdims=True)
    loads[...] = load


def shift_body(piece, terms, weight, modulation, lines):
    total = modulation.shape[1] // LANES
    first = up_to(piece, 8)
    sums = jnp.sum(terms[:, first : first + total, :].astype(WIDE), axis=0)
    for at in range(total):
        modulation[:, at * LANES : (at + 1) * LANES] = sums[at : at + 1]
    gate = total // 6
    lines[:, :8] = jnp.zeros((lines.shape[0], 8, LANES), WIDE)
    lines[:, :gate] = jnp.broadcast_to(sums[5 * gate :], (lines.shape[0], gate, LANES))
    lines[:, 8:] = jnp.broadcast_to(weight[...], (lines.shape[0], 8, LANES))


def head_pair(values, pair):
    both = values[:, pair * LANES : (pair + 1) * LANES]
    lane = lax.broadcasted_iota(jnp.int32, both.shape, 1)
    zero = jnp.zeros_like(both)
    return jnp.concatenate(
        [jnp.where(lane < HEAD_DIM, both, zero), jnp.where(lane < HEAD_DIM, zero, both)], axis=0
    )


def scores_of(queries, stacked, pair, length):
    count = queries.shape[0]
    raw = dot_nt(queries[:, pair * LANES : (pair + 1) * LANES], stacked) * HEAD_DIM ** (-0.5)
    lane = lax.broadcasted_iota(jnp.int32, raw.shape, 1)
    return jnp.where((lane & (count - 1)) < length, raw, -1e30)


def times(left, low, high, cols):
    half = low.shape[0]
    return dot(left[:, :half], low[:, cols]) + dot(left[:, half:], high[:, cols])


def times_back(left, low, high, cols):
    return jnp.concatenate([dot_nt(left, low[:, cols]), dot_nt(left, high[:, cols])], axis=1)


def forward_body(
    piece, where, tokens, modulation, lengths, rows0, rows1, low0, high0, low1, high1,
    both, joined, totals, attn_out, middle_out, *parts,
):
    count, width = tokens.shape
    length = lengths[0]
    mod = modulation[...]
    tok = tokens[...].astype(WIDE)
    unit, _ = center_of(tok)
    first = (unit * (1.0 + mod[:, width : 2 * width]) + mod[:, :width]).astype(LOW)
    both[:, :width] = first
    start = 0
    for rows, low, high in ((rows0, low0, high0), (rows1, low1, high1)):
        moved = dot(first, place_of(where[0], rows, piece, width)).astype(LOW)
        size = min(low.shape[1], 3 * width - start)
        joined[:, start : start + size] = times(moved, low, high, slice(0, size)).astype(LOW)
        start += size
    queries, keys, values = joined[:, :width], joined[:, width : 2 * width], joined[:, 2 * width :]
    lane = lax.broadcasted_iota(jnp.int32, (count, LANES), 1)
    sums = jnp.zeros((count, LANES), WIDE)
    for pair in range(HEADS // 2):
        scores = scores_of(queries, head_pair(keys, pair), pair, length)
        probs = []
        for one in range(2):
            mine = scores[:, one * count : (one + 1) * count]
            top = jnp.max(mine, axis=-1, keepdims=True)
            total = top + jnp.log(jnp.sum(jnp.exp(mine - top), axis=-1, keepdims=True))
            sums = jnp.where(lane == 2 * pair + one, total, sums)
            probs.append(jnp.exp(mine - total).astype(LOW))
        both[:, width + pair * LANES : width + (pair + 1) * LANES] = dot(
            jnp.concatenate(probs, axis=1), head_pair(values, pair)
        ).astype(LOW)
    totals[...] = sums
    moved = dot(both[:, width:], place_of(where[0], rows1, piece, width)).astype(LOW)
    attn = times(moved, low1, high1, slice(width, 2 * width))
    attn_out[...] = attn
    middle = tok + mod[:, 2 * width : 3 * width] * attn
    middle_out[...] = middle
    unit, _ = center_of(middle)
    second = (unit * (1.0 + mod[:, 4 * width : 5 * width]) + mod[:, 3 * width : 4 * width]).astype(LOW)
    start = 0
    for part in parts:
        part[...] = second[:, start : start + part.shape[1]]
        start += part.shape[1]


def backward_body(
    piece, where, tokens, cotangent, modulation, lengths, rows0, rows1, low0, high0, low1, high1,
    joined, totals, attn_in, middle_in, near0, far0, near1, far1,
    grad_tokens, sent, lines, d_rows, d_cols, d_mod,
):
    count, width = tokens.shape
    length = lengths[0]
    mod = modulation[...]
    start = 0
    for low, high in ((near0, far0), (near1, far1)):
        size = low.shape[1]
        total = low[...].astype(WIDE) + high[...].astype(WIDE)
        d_rows[:, start : start + size] = total[:count]
        d_mod[:, 5 * width + start : 5 * width + start + size] = total[count : count + 1]
        start += size
    d_second = d_rows[...]
    attn = attn_in[...]
    unit, scale = center_of(middle_in[...])
    d_mod[:, 3 * width : 4 * width] = jnp.sum(d_second, axis=0, keepdims=True)
    d_mod[:, 4 * width : 5 * width] = jnp.sum(d_second * unit, axis=0, keepdims=True)
    d_middle = cotangent[...].astype(WIDE) + norm_back(
        d_second * (1.0 + mod[:, 4 * width : 5 * width]), unit, scale
    )
    d_mod[:, 2 * width : 3 * width] = jnp.sum(d_middle * attn, axis=0, keepdims=True)
    d_attn = (mod[:, 2 * width : 3 * width] * d_middle).astype(LOW)
    d_cols[:, 3 * width :] = d_attn
    d_attended = dot_nt(
        times_back(d_attn, low1, high1, slice(width, 2 * width)).astype(LOW), place_of(where[0], rows1, piece, width)
    ).astype(LOW)
    queries, keys, values = joined[:, :width], joined[:, width : 2 * width], joined[:, 2 * width :]
    sums = totals[...]
    lane = lax.broadcasted_iota(jnp.int32, (count, LANES), 1)
    factor = HEAD_DIM ** (-0.5)
    for pair in range(HEADS // 2):
        at = slice(pair * LANES, (pair + 1) * LANES)
        k_pair, v_pair = head_pair(keys, pair), head_pair(values, pair)
        scores = scores_of(queries, k_pair, pair, length)
        d_probs = dot_nt(d_attended[:, at], v_pair)
        probs_low, d_scores_low = [], []
        for one in range(2):
            half = slice(one * count, (one + 1) * count)
            total = jnp.sum(jnp.where(lane == 2 * pair + one, sums, 0.0), axis=1, keepdims=True)
            probs = jnp.exp(scores[:, half] - total)
            back = d_probs[:, half]
            d_scores = probs * (back - jnp.sum(probs * back, axis=-1, keepdims=True))
            probs_low.append(probs.astype(LOW))
            d_scores_low.append(d_scores.astype(LOW))
        d_scores_both = jnp.concatenate(d_scores_low, axis=1)
        d_cols[:, at] = (dot(d_scores_both, k_pair) * factor).astype(LOW)
        q_pair, d_pair = queries[:, at], d_attended[:, at]
        d_k = dot_tn(d_scores_both, q_pair) * factor
        d_v = dot_tn(jnp.concatenate(probs_low, axis=1), d_pair)
        d_k = jnp.where(lane < HEAD_DIM, d_k[:count], d_k[count:])
        d_v = jnp.where(lane < HEAD_DIM, d_v[:count], d_v[count:])
        d_cols[:, width + pair * LANES : width + (pair + 1) * LANES] = d_k.astype(LOW)
        d_cols[:, 2 * width + pair * LANES : 2 * width + (pair + 1) * LANES] = d_v.astype(LOW)
    d_first = jnp.zeros((count, width), WIDE)
    start = 0
    for rows, low, high in ((rows0, low0, high0), (rows1, low1, high1)):
        size = min(low.shape[1], 3 * width - start)
        part = times_back(d_cols[:, start : start + size], low, high, slice(0, size))
        start += size
        place = place_of(where[0], rows, piece, width)
        top = part.astype(LOW)
        rest = (part - top.astype(WIDE)).astype(LOW)
        d_first += dot_nt(top, place) + dot_nt(rest, place)
    unit, scale = center_of(tokens[...].astype(WIDE))
    d_mod[:, :width] = jnp.sum(d_first, axis=0, keepdims=True)
    d_mod[:, width : 2 * width] = jnp.sum(d_first * unit, axis=0, keepdims=True)
    grad_tokens[...] = d_middle + norm_back(
        d_first * (1.0 + mod[:, width : 2 * width]), unit, scale
    )
    for at in range(lines.shape[1]):
        line = d_mod[:, at * LANES : (at + 1) * LANES].astype(LOW)
        lines[:, at, :] = jnp.broadcast_to(line, (lines.shape[0], LANES))
    experts = sent.shape[0]
    cols, out_cols = 3 * width // experts, width // experts
    for expert in range(experts):
        to = expert ^ where[1]
        sent[to, :, :cols] = d_cols[:, expert * cols : (expert + 1) * cols]
        sent[to, :, cols:] = d_cols[:, 3 * width + expert * out_cols : 3 * width + (expert + 1) * out_cols]


def join_rows(lows, highs, rows):
    start = 0
    half = rows.shape[0] // 2
    for low, high in zip(lows, highs):
        share = low.shape[-1]
        for at, part in enumerate((low, high)):
            rows[at * half : (at + 1) * half, start : start + share] = part[...].reshape(half, share)
        start += share


def item_of(where, links, at, block):
    core, outer, inner = links
    item = where[0] ^ (core[0] * at) ^ (inner[0] * block)
    for bit, mask in enumerate(outer):
        item = item ^ ((pl.program_id(0) >> bit & 1) * mask)
    return item


def d_act_body(links, where, low, high, lines, down, d_act, rows):
    count, width = low.shape[-2:]
    for at, part in enumerate((low, high)):
        for block in range(2):
            item = item_of(where, links, at, block)
            here = slice((2 * at + block) * count, (2 * at + block + 1) * count)
            for line in range(width // LANES):
                cols = slice(line * LANES, (line + 1) * LANES)
                rows[0, here, cols] = (
                    part[block, :, cols].astype(WIDE) * lines[item, line : line + 1]
                ).astype(LOW)
    d_act[0] = dot_nt(rows[0], down[...]).astype(LOW)


def hidden_body(links, routed, where, *refs):
    lows, highs, cots, (lines, d_act, up, down) = refs[:2], refs[2:4], refs[4:6], refs[6:10]
    back_lows, back_highs, branches, (d_pre, act, rows) = refs[10:12], refs[12:14], refs[14:16], refs[16:]
    join_rows(lows, highs, rows)
    count = rows.shape[0] // 4
    width = up.shape[0]
    expert = where[1]
    flat = lax.broadcasted_iota(jnp.int32, (count, count), 0) == lax.broadcasted_iota(jnp.int32, (count, count), 1)
    spare = lax.broadcasted_iota(jnp.int32, (EXTRA, width), 0)
    blocks = [(at, block) for at in range(2) for block in range(2)]
    weights = []
    for at, block in blocks:
        line = lines[item_of(where, links, at, block), pl.ds(8 + expert, 1)]
        weights.append(jnp.sum(jnp.where(flat, line, 0.0), axis=1, keepdims=True))
    weight = jnp.concatenate(weights, axis=0)
    pre = dot(rows[...], up[...])
    square = pre * pre
    bend = jnp.tanh(pre * (CURVE + (CURVE * CUBIC) * square))
    gate = 0.5 + 0.5 * bend
    hidden = pre * gate
    slope = gate + hidden * (1.0 - bend) * (CURVE + (3.0 * CURVE * CUBIC) * square)
    d_hidden = d_act[0].astype(WIDE)
    d_full = d_hidden * slope
    d_low = jnp.concatenate([d_full[:, :routed] * weight, d_full[:, routed:]], axis=1).astype(LOW)
    d_pre[0] = d_low
    act_low = jnp.concatenate([hidden[:, :routed] * weight, hidden[:, routed:]], axis=1).astype(LOW)
    act[0] = act_low
    pair = jnp.sum(hidden[:, :routed] * d_hidden[:, :routed], axis=1, keepdims=True)
    back = dot_nt(d_low, up[...]).astype(LOW)
    out = dot(act_low, down[...])
    for number, (at, block) in enumerate(blocks):
        one = slice(number * count, (number + 1) * count)
        body, extra = slice(0, count), slice(count, count + EXTRA)
        d_gate = jnp.sum(out[one] * cots[at][block].astype(WIDE), axis=0, keepdims=True)
        d_gate = jnp.where(spare == 0, d_gate, 0.0).astype(LOW)
        start = 0
        for ref in (back_lows, back_highs)[at]:
            size = ref.shape[-1]
            ref[block, body] = back[one, start : start + size]
            ref[block, extra] = d_gate[:, start : start + size]
            start += size
        ref = branches[at]
        ref[block, body] = out[one].astype(LOW)
        line = jnp.sum(jnp.where(flat, pair[one], 0.0), axis=0, keepdims=True)
        ref[block, extra] = jnp.zeros((EXTRA, width), LOW)
        ref[block, extra, :count] = jnp.where(spare[:, :count] == expert, line, 0.0).astype(LOW)


def grads_body(write, where, *refs):
    second, d_mlp, d_pre, act = refs[:4], refs[4], refs[5], refs[6]
    outs, (rows, up_sum, down_sum) = refs[7:-3], refs[-3:]
    step = pl.program_id(0)

    @pl.when(step == 0)
    def _():
        up_sum[...] = jnp.zeros(up_sum.shape, WIDE)
        down_sum[...] = jnp.zeros(down_sum.shape, WIDE)

    join_rows(second[:2], second[2:], rows)
    up_sum[...] += dot_tn(rows[...], d_pre[0])
    down_sum[...] += dot_tn(act[0], d_mlp[0])

    @pl.when(step == pl.num_programs(0) - 1)
    def _():
        write(where, up_sum, down_sum, outs)


def write_whole(where, up_sum, down_sum, outs):
    outs[0][...] = up_sum[...]
    outs[1][...] = down_sum[...]


def place_and_twin(where):
    return where[2] // 2, where[2] % 2


def rows_at(number, size):
    return pl.ds(pl.multiple_of(number * size, 16), size)


def lanes_at(number, size):
    return pl.ds(pl.multiple_of(number * size, LANES), size)


def up_sent_body(where, weight, near, away):
    place, _ = place_and_twin(where)
    for at in range(4):
        (near if at < 2 else away)[at % 2] = weight[:, lanes_at(place ^ at, near.shape[2])]


def up_join_body(where, own, shared, other, shared_other, full):
    place, twin = place_and_twin(where)
    rows, cols = own.shape[1], own.shape[2]
    for at, mask in enumerate((0, 2, 1, 3)):
        full[rows_at(2 * (place ^ mask) + twin, rows), :cols] = own[at]
        full[rows_at(2 * (place ^ mask) + 1 - twin, rows), :cols] = other[at]
    size = shared.shape[1]
    blank = jnp.zeros((full.shape[0], LANES - size), LOW)
    for at, piece in enumerate((shared, shared_other)):
        start = cols + at * LANES
        full[:, start : start + size] = piece[...]
        full[:, start + size : start + LANES] = blank


def down_join_body(where, own, other, full):
    _, twin = place_and_twin(where)
    rows = (full.shape[0] - 2 * LANES) // 2
    size = own.shape[0] - rows
    blank = jnp.zeros((LANES - size, full.shape[1]), LOW)
    for at, piece in enumerate((own, other)):
        full[rows_at(twin if at == 0 else 1 - twin, rows)] = piece[:rows]
        start = 2 * rows + at * LANES
        full[start : start + size] = piece[rows:]
        full[start + size : start + LANES] = blank


def write_twins(where, up_sum, down_sum, outs):
    keep_up, send_up, keep_down, send_down = outs
    place, twin = place_and_twin(where)
    rows, units = keep_up.shape[1], 2 * (down_sum.shape[0] - 2 * LANES) // 2
    size = (keep_up.shape[2] - units) // 2
    mine, other = slice(units, units + size), slice(units + LANES, units + LANES + size)
    for out, at_twin, order_ in ((keep_up, twin, (mine, other)), (send_up, 1 - twin, (other, mine))):
        for at in range(out.shape[0]):
            here = rows_at(2 * (place ^ at) + at_twin, rows)
            out[at, :, :units] = up_sum[here, :units].astype(LOW)
            for number, cols in enumerate(order_):
                start = units + number * size
                out[at, :, start : start + size] = up_sum[here, cols].astype(LOW)
    half = units // 2
    for out, at_twin, rows_ in ((keep_down, twin, mine), (send_down, 1 - twin, other)):
        out[:half] = down_sum[rows_at(at_twin, half)].astype(out.dtype)
        out[half:] = down_sum[rows_].astype(out.dtype)


def twins_body(keep_up, got_up, keep_down, got_down, grad_down, shared_down, *ups):
    for at, out in enumerate(ups):
        out[...] = (keep_up[at].astype(WIDE) + got_up[at].astype(WIDE)).astype(LOW)
    half = grad_down.shape[0]
    grad_down[...] = keep_down[:half] + got_down[:half].astype(WIDE)
    shared_down[...] = (keep_down[half:] + got_down[half:].astype(WIDE)).astype(LOW)


def up_rows_body(where, up0, up1, up2, up3, shared_down, grad_up, sent):
    place, twin = place_and_twin(where)
    expert = where[1]
    units = grad_up.shape[1] // 4
    size = (up0.shape[1] - units) // 2
    cols = sent.shape[2] - 2 * size
    for at, piece in enumerate((up0, up1, up2, up3)):
        grad_up[:, lanes_at(place ^ at, units)] = piece[:, :units].astype(WIDE)
        mine, other = piece[:, units : units + size], piece[:, units + size :]
        sent[(place ^ at) ^ expert, :, :size] = jnp.where(twin == 0, mine, other)
        sent[(place ^ at) ^ expert, :, size : 2 * size] = jnp.where(twin == 0, other, mine)
    for to in range(4):
        sent[to ^ expert, :, 2 * size :] = shared_down[:, to * cols : (to + 1) * cols]


def shared_rows_body(where, got0, got1, got2, got3, grad_up, grad_down, held):
    expert = where[1]
    for at, got in enumerate((got0, got1, got2, got3)):
        held[at ^ expert] = got[...]
    size = grad_up.shape[1] // 8
    for source in range(4):
        for twin in range(2):
            start = (4 * twin + source) * size
            grad_up[:, start : start + size] = held[source, :, twin * size : (twin + 1) * size].astype(WIDE)
        grad_down[source * size : (source + 1) * size] = held[source, :, 2 * size :].astype(WIDE)


def attn_terms_body(masks, where, both, cols0, cols1, cols2, cols3, low0, low1, high0, high1, term):
    expert, group = where[1], where[2]
    width = both.shape[2] // 2
    cut = 3 * width // 4
    rows = low0.shape[1]
    for at, cols in enumerate((cols0, cols1, cols2, cols3)):
        inputs = both[expert ^ at]
        parts = (dot_tn(inputs[:, :width], cols[:, :cut]), dot_tn(inputs[:, width:], cols[:, cut:]))
        for start, part in ((0, parts[0]), (cut, parts[1])):
            here = slice(start, start + part.shape[1])
            if at:
                term[:, here] += part
            else:
                term[:, here] = part
    half = width // 2
    for number, (low, high) in enumerate(((low0, high0), (low1, high1))):
        for at, mask in enumerate(masks[number]):
            ref = low if at < 4 else high
            ref[at % 4] = term[rows_at(group ^ mask, rows), number * half : (number + 1) * half].astype(LOW)


def attn_out_body(near0, far0, near1, far1, grad_qkv, grad_out, total):
    half = near0.shape[1]
    for at, (near, far) in enumerate(((near0, far0), (near1, far1))):
        total[:, at * half : (at + 1) * half] = near[...].astype(WIDE) + far[...].astype(WIDE)
    cut = grad_qkv.shape[1]
    grad_qkv[...] = total[:, :cut]
    grad_out[...] = total[:, cut:]


def finish_body(modulation, middle, kept, low, high, block_out, grad_gates, total):
    count, width = middle.shape
    total[...] = low[...].astype(WIDE) + high[...].astype(WIDE)
    block_out[...] = middle[...] + modulation[:, 5 * width :] * total[:count]
    pairs = total[count : count + 8, :count]
    for choice in range(2):
        grad_gates[choice : choice + 1] = jnp.sum(kept[choice] * pairs, axis=0, keepdims=True)


def ada_body(experts, where, got, cond, weight, grad_weight, grad_bias, sent, d_mod):
    expert = where[1]
    total, lines, _ = got.shape
    for at in range(lines):
        d_mod[:, at * LANES : (at + 1) * LANES] = got[:, at, :]
    grad_bias[...] = jnp.sum(d_mod[...].astype(WIDE), axis=0, keepdims=True)
    cols = grad_weight.shape[1]
    mine = d_mod[:, pl.ds(pl.multiple_of(expert * cols, LANES), cols)]
    grad_weight[...] = dot_tn(cond[:, 0, :], mine)[: grad_weight.shape[0]]
    piece = weight.shape[0]
    back = dot_nt(d_mod[...], weight[...])
    sent[...] = jnp.zeros(sent.shape, WIDE)
    sent[:, 0, :piece] = back


def attn_grads_body(both, d_cols, out):
    experts, count, cols = d_cols.shape
    width = both.shape[2] // 2
    groups, rows, _ = out.shape
    flat = d_cols[...].reshape(experts * count, cols)
    inputs = both[...].reshape(experts * count, 2 * width)
    cut = 3 * cols // 4
    out[...] = jnp.concatenate(
        [dot_tn(inputs[:, :width], flat[:, :cut]), dot_tn(inputs[:, width:], flat[:, cut:])], axis=1
    ).astype(LOW).reshape(groups, rows, cols)


def attn_sum_body(got, grad_qkv, grad_out):
    total = jnp.sum(got[...].astype(WIDE), axis=0)
    cut = grad_qkv.shape[1]
    grad_qkv[...] = total[:, :cut]
    grad_out[...] = total[:, cut:]


def up_out_body(units, got, grad_up):
    for group in range(got.shape[0]):
        grad_up[:, group * units : (group + 1) * units] = got[group, :, :units].astype(WIDE)


def gather_far(pieces, masks):
    found = [pieces]
    for mask in masks:
        found = found + [[swap(piece, mask) for piece in held] for held in found]
    return found


def shards(
    tokens,
    cond,
    lengths,
    routes,
    gate_weights,
    ada_weight,
    ada_bias,
    qkv_weight,
    out_weight,
    shared_up,
    shared_down,
    expert_up,
    expert_down,
    cotangent,
):
    count, width = tokens.shape
    experts = lax.axis_size("expert")
    groups = lax.axis_size("batch")
    total = experts * groups
    me = lax.axis_index(AXES)
    my_expert = lax.axis_index("expert")
    my_group = lax.axis_index("batch")
    where = jnp.stack([me, my_expert, my_group]).astype(jnp.int32)
    capacity = 5 * 2 * count // (4 * experts)
    piece = ada_weight.shape[0]
    group_rows = width // groups
    shared_units = shared_down.shape[0]
    units = expert_down.shape[1]
    shares = [width // 2, width // 2]
    tall = (count, width)
    lines = 6 * width // LANES

    expert_masks = bits_of(experts)
    group_masks = [experts * step for step in bits_of(groups)]
    away = list(reversed(group_masks[1:3]))
    far = group_masks[:1] + group_masks[3:]
    core, across = expert_masks[:1], expert_masks[1:]
    team_links = [away + across, across + away]
    inner, outer = away[:1], across + away[1:]
    links = (core, outer, inner)
    steps = 2 ** len(outer)
    weight_links = [far[1:] + away + far[:1] + across, far[1:] + away + across + far[:1]]
    paired = groups == 8 and experts == 4
    away_masks = order(sorted(away))

    pair_weight, kept, sent = call(
        functools.partial(route_body, experts, capacity, groups),
        [((8, count), WIDE), ((2, 8, count), WIDE), ((total, 16, LANES), LOW)],
        (routes.T, gate_weights.T, lengths, cond),
        smem=(2,),
    )
    cond_all = lax.all_to_all(sent, AXES, split_axis=0, concat_axis=0, tiled=True)

    attn_w = jnp.concatenate([qkv_weight, out_weight], axis=1)[None]
    cot = cotangent[None]
    first_links = far[1:] + away
    for at, mask in enumerate(first_links):
        attn_got = swap(attn_w, mask)
        if at == len(far) - 1:
            cot_got = swap(cot, away[0])
            attn_got, cot_got, cond_all = together(attn_got, cot_got, cond_all)
            cot = grown(cot, cot_got)
            terms, loads = call(
                terms_body,
                [((total, up_to(up_to(piece, 8) + lines, 8), LANES), LOW), ((1, LANES), WIDE)],
                (where, cond_all, ada_weight, ada_bias[None], shared_up),
                smem=(0,),
            )
            terms_got = lax.all_to_all(terms, AXES, split_axis=0, concat_axis=0, tiled=True)
        attn_w = grown(attn_w, attn_got)
        if at == len(first_links) - 1:
            cot_links = away[:1] + across[:1]
            cot_got = swap(cot, across[0])
            attn_w, cot_got, terms = together(attn_w, cot_got, terms)
            cot = grown(cot, cot_got)
    cot_links = away[:1] + across + away[1:]
    for mask in across[1:]:
        cot = grown(cot, swap(cot, mask))
    tallies = loads[0, group_rows : group_rows + experts + 1]
    expert_load = tallies[:experts] * experts / (2.0 * tallies[experts])
    attn_parts = [attn_w[:, :, : 2 * width], attn_w[:, :, 2 * width :]]
    last_links = [far[:1] + across, across + far[:1]]
    weight_links = [first_links + masks for masks in last_links]
    if paired:
        place_units = expert_up.shape[2] // 4
        up_near, up_away = call(
            up_sent_body, [((2, group_rows, place_units), LOW)] * 2, (where, expert_up[0]), smem=(0,)
        )
        down_own = jnp.concatenate([expert_down[0], shared_down], axis=0)
        down_other = swap(down_own, far[0])
    for at in range(len(last_links[0])):
        got = [swap(part, masks[at]) for part, masks in zip(attn_parts, last_links)]
        if at == 0:
            cot_got = swap(cot, away[1])
            if paired:
                up_got = swap(up_away, away[0])
                got, up_got = together(got, up_got)
        elif at == len(last_links[0]) - 1:
            got, cot_got = together(got, cot_got)
            cot_low = grown(cot, cot_got)
            if paired:
                got, down_other = together(got, down_other)
        attn_parts = [grown(*pair) for pair in zip(attn_parts, got)]
    modulation, own_lines = call(
        functools.partial(shift_body, piece),
        [((1, 6 * width), WIDE), ((total, 16, LANES), WIDE)],
        (terms_got, pair_weight),
    )
    attn_far = [swap(part, core[0]) for part in attn_parts]
    cot_high = swap(cot_low, core[0])
    weights = []
    row_places = []
    for low, high, masks in zip(attn_parts, attn_far, weight_links):
        weights += [low.reshape(-1, 2 * width), high.reshape(-1, 2 * width)]
        found = np.repeat(np.array(order(masks + core), np.int32), piece)
        row_places.append(jnp.asarray(np.stack([found, np.tile(np.arange(piece, dtype=np.int32), total)])))

    both, joined, totals, attn, middle, *seconds = call(
        functools.partial(forward_body, piece),
        [
            ((count, 2 * width), LOW),
            ((count, 3 * width), LOW),
            ((count, LANES), WIDE),
            (tall, WIDE),
            (tall, WIDE),
            *[((count, share), LOW) for share in shares],
        ],
        (where, tokens, modulation, lengths, *row_places, *weights),
        smem=(0, 3),
    )

    part_shared_up = terms_got[:, :piece, :shared_units].reshape(width, shared_units)
    shared_slot = up_to(shared_units, LANES)
    second_low = [part[None] for part in seconds]
    for at in range(len(away + across)):
        got = [swap(part, masks[at]) for part, masks in zip(second_low, team_links)]
        if at == 0:
            item_lines = lax.all_to_all(tie(own_lines, *seconds), AXES, split_axis=0, concat_axis=0, tiled=True)
            if paired:
                up_mine = jnp.stack([up_near[0], up_got[0]])
                up_sent = jnp.stack([up_near[1], up_got[1]])
                up_last = swap(up_sent, away[1])
                got, up_last = together(got, up_last)
                up_own = jnp.concatenate([up_mine, up_last], axis=0)
                up_other = swap(up_own, far[0])
                shared_up_other = swap(part_shared_up, far[0])
        elif at == 1:
            got, item_lines = together(got, item_lines)
            if paired:
                routed, hidden = 2 * units, 2 * units + 2 * shared_slot
                (down_cat,) = call(
                    down_join_body, [((hidden, width), LOW)], (where, down_own, down_other), smem=(0,)
                )
        second_got = got
        if at < len(away + across) - 1:
            second_low = [grown(*pair) for pair in zip(second_low, got)]
    if paired:
        (up_cat,) = call(
            up_join_body,
            [((width, hidden), LOW)],
            (where, up_own, part_shared_up, up_other, shared_up_other),
            smem=(0,),
        )
    else:
        part_up = lax.all_to_all(expert_up[0], "batch", split_axis=1, concat_axis=0, tiled=True)
        held = gather_far([part_up, part_shared_up, expert_down[0], shared_down], far)
        slot = up_to(units, LANES)
        routed, hidden = len(held) * slot, len(held) * (slot + shared_slot)
        up_cat = jnp.concatenate(
            [pad_lanes(h[0], slot) for h in held] + [pad_lanes(h[1], shared_slot) for h in held], axis=1
        )
        down_cat = jnp.concatenate(
            [pad_lanes(h[2].T, slot).T for h in held] + [pad_lanes(h[3].T, shared_slot).T for h in held], axis=0
        )

    half = 2 * count

    def whole(array):
        return array, array.shape, lambda step: (0,) * array.ndim

    def block_at(masks, rows, lanes):
        bits = list(reversed(masks))
        block = tuple(2 if mask in inner else None for mask in bits) + (rows, lanes)

        def index(step):
            spot = {mask: step // 2**at % 2 for at, mask in enumerate(outer)}
            return tuple(spot.get(mask, 0) for mask in bits) + (0, 0)

        return block, index

    def block_in(array, masks):
        laid = array.reshape((2,) * len(masks) + array.shape[1:])
        return laid, *block_at(masks, *array.shape[1:])

    def block_out_of(rows, lanes, masks):
        return (2,) * len(masks) + (rows, lanes), LOW, *block_at(masks, rows, lanes)

    def rows_of(array):
        return array, (1,) + array.shape[1:], lambda step: (step, 0, 0)

    def rows_out(lanes):
        return (steps, 2 * half, lanes), LOW, (1, 2 * half, lanes), lambda step: (step, 0, 0)

    def sum_out(shape, kind):
        return shape, kind, shape, lambda step: (0,) * len(shape)

    def flat(part):
        return part.reshape((-1,) + part.shape[-2:])

    scalars = (where, None, None)

    cots = [block_in(cot_low, cot_links), block_in(cot_high, cot_links)]
    d_act, d_mlp = sweep(
        functools.partial(d_act_body, links),
        steps,
        [scalars, *cots, whole(item_lines), whole(down_cat)],
        [rows_out(hidden), rows_out(width)],
    )
    second_got, d_act, up_cat = together(second_got, d_act, up_cat)
    second_low = [grown(*pair) for pair in zip(second_low, second_got)]
    second_high = [swap(part, core[0]) for part in second_low]
    second_in = [block_in(part, masks) for parts in (second_low, second_high) for part, masks in zip(parts, team_links)]

    tall_rows = count + EXTRA
    back = [block_out_of(tall_rows, share, masks) for share, masks in zip(shares, team_links)]
    side = block_out_of(tall_rows, width, away + across)
    *parts, d_pre, act = sweep(
        functools.partial(hidden_body, links, routed),
        steps,
        [scalars, *second_in, *cots, whole(item_lines), rows_of(d_act), whole(up_cat), whole(down_cat)],
        [*back, *back, side, side, rows_out(hidden), rows_out(hidden)],
        scratch=[((2 * half, width), LOW)],
    )
    parts = [flat(part) for part in parts]
    if paired:
        up_lanes = place_units + 2 * shared_units
        sum_outs = [
            sum_out((4, group_rows, up_lanes), LOW),
            sum_out((4, group_rows, up_lanes), LOW),
            sum_out((units + shared_units, width), WIDE),
            sum_out((units + shared_units, width), LOW),
        ]
    else:
        sum_outs = [sum_out((width, hidden), WIDE), sum_out((hidden, width), WIDE)]
    grads = sweep(
        functools.partial(grads_body, write_twins if paired else write_whole),
        steps,
        [scalars, *second_in, rows_of(d_mlp), rows_of(d_pre), rows_of(act)],
        sum_outs,
        scratch=[((2 * half, width), LOW), ((width, hidden), WIDE), ((hidden, width), WIDE)],
    )

    lows, highs, orders = list(parts[:2]), list(parts[2:4]), [masks + core for masks in team_links]
    out_low, out_high, out_order = parts[4], parts[5], away + across + core
    sums_at = len(orders[0]) - 1
    for at in range(sums_at + 1):
        got = [swap(high, masks[-1 - at]) for high, masks in zip(highs, orders)]
        if at in (0, 2):
            out_got = swap(out_high, out_order[-1 - at // 2])
        if at == 1:
            got, grads, out_got = together(got, list(grads), out_got)
            if paired:
                twin_up, twin_down = swap(grads[1], far[0]), swap(grads[3], far[0])
        elif at < sums_at or not paired:
            got = together(*got)
        else:
            got, twin_up, twin_down = together(got, twin_up, twin_down)
        if at < sums_at:
            pairs = [added(low, other) for low, other in zip(lows, got)]
            lows, highs = [pair[0] for pair in pairs], [pair[1] for pair in pairs]
        if at == 1:
            out_low, out_high = added(out_low, out_got)
    folded = [half_[0] for pair in zip(lows, got) for half_ in pair]
    grad_tokens, d_cols, d_mod_sent = call(
        functools.partial(backward_body, piece),
        [(tall, WIDE), ((experts, count, 4 * width // experts), LOW), ((total, lines, LANES), LOW)],
        (
            where, tokens, cotangent, modulation, lengths, *row_places, *weights,
            joined, totals, attn, middle, *folded,
        ),
        scratch=[(tall, WIDE), ((count, 4 * width), LOW), ((1, 6 * width), WIDE)],
        smem=(0, 4),
    )

    both_group = lax.all_gather(tie(both, *second_high), "expert", axis=0)
    d_mod_all = lax.all_to_all(d_mod_sent, AXES, split_axis=0, concat_axis=0, tiled=True)
    if paired:
        cols_got = [d_cols[at] if not at else swap(d_cols[at], at) for at in range(4)]
        cols_got, out_got = together(cols_got, out_got)
        sum_links = [away + far, away[:1] + far + away[1:]]
        sum_masks = [[mask // experts for mask in order(masks)] for masks in sum_links]
        term_half = ((4, group_rows, width // 2), LOW)
        attn_sent = call(
            functools.partial(attn_terms_body, sum_masks),
            [term_half] * 4,
            (where, both_group, *cols_got),
            scratch=[((width, width), WIDE)],
            smem=(0,),
        )
        out_low, out_high = added(out_low, out_got)
        out_got = swap(out_high, out_order[-3])
        term_lows, term_highs = attn_sent[:2], attn_sent[2:]
        for at in range(3):
            got = [swap(high, masks[-1 - at]) for high, masks in zip(term_highs, sum_links)]
            if at == 1:
                got, out_got = together(got, out_got)
                out_low, out_high = added(out_low, out_got)
                out_got = swap(out_high, out_order[-4])
            else:
                got = together(*got)
            if at < 2:
                pairs = [added(low, other) for low, other in zip(term_lows, got)]
                term_lows, term_highs = [pair[0] for pair in pairs], [pair[1] for pair in pairs]
        grad_qkv, grad_out = call(
            attn_out_body,
            [((group_rows, 3 * width // experts), WIDE), ((group_rows, width // experts), WIDE)],
            [half_[0] for pair in zip(term_lows, got) for half_ in pair],
            scratch=[((group_rows, width), WIDE)],
        )
    else:
        natural = jnp.arange(experts, dtype=jnp.int32) ^ my_expert
        d_cols = jnp.take(d_cols, natural, axis=0)
        d_cols = lax.all_to_all(d_cols, "expert", split_axis=0, concat_axis=0, tiled=True)
        (attn_terms,) = call(
            attn_grads_body, [((groups, group_rows, 4 * width // experts), LOW)], (both_group, d_cols)
        )
        attn_terms = lax.all_to_all(attn_terms, "batch", split_axis=0, concat_axis=0, tiled=True)
        grad_qkv, grad_out = call(
            attn_sum_body,
            [((group_rows, 3 * width // experts), WIDE), ((group_rows, width // experts), WIDE)],
            (attn_terms,),
        )
        for mask in reversed(out_order[:-2]):
            out_low, out_high = added(out_low, out_got)
            out_got = swap(out_high, mask)

    block_out, grad_gate_weights = call(
        finish_body,
        [(tall, WIDE), ((2, count), WIDE)],
        (modulation, middle, kept, out_low[0], out_got[0]),
        scratch=[((tall_rows, width), WIDE)],
    )

    if paired:
        grad_expert_down, shared_own, *up_own = call(
            twins_body,
            [
                ((units, width), WIDE),
                ((shared_units, width), LOW),
                *[((group_rows, up_lanes), LOW)] * 4,
            ],
            (grads[0], twin_up, grads[2], twin_down),
        )
        up_got = [piece if not mask else swap(piece, mask) for piece, mask in zip(up_own, away_masks)]
        grad_expert_up, crossed = call(
            up_rows_body,
            [
                ((group_rows, groups * units), WIDE),
                ((4, group_rows, 2 * shared_units + width // experts), LOW),
            ],
            (where, *up_got, shared_own),
            smem=(0,),
        )
        crossed = [crossed[at] if not at else swap(crossed[at], at) for at in range(4)]
        grad_shared_up, grad_shared_down = call(
            shared_rows_body,
            [((group_rows, width), WIDE), ((experts * shared_units, width // experts), WIDE)],
            (where, *crossed),
            scratch=[((4, group_rows, 2 * shared_units + width // experts), LOW)],
            smem=(0,),
        )
    else:
        grad_up, grad_down = grads
        replicas = hidden // (slot + shared_slot)
        sums = []
        for taken, size, first in ((grad_up.T, units, 0), (grad_up.T, shared_units, routed), (grad_down, units, 0), (grad_down, shared_units, routed)):
            room = up_to(size, LANES)
            held = [taken[first + at * room : first + at * room + size] for at in range(replicas)]
            for mask in reversed(far):
                some = len(held) // 2
                held = [
                    low + swap(high.astype(LOW), mask).astype(WIDE) for low, high in zip(held[:some], held[some:])
                ]
            sums.append(held[0])
        grad_expert_down = sums[2]
        up_rows = jnp.concatenate([sums[0].T, sums[1].T], axis=1).astype(LOW).reshape(groups, group_rows, -1)
        up_rows = lax.all_to_all(up_rows, "batch", split_axis=0, concat_axis=0, tiled=True)
        grad_shared_down = lax.all_to_all(
            sums[3].astype(LOW), "expert", split_axis=1, concat_axis=0, tiled=True
        ).astype(WIDE)
        (grad_expert_up,) = call(
            functools.partial(up_out_body, units), [((group_rows, groups * units), WIDE)], (up_rows,)
        )
        shared_rows = up_rows[:, :, units:].reshape(experts, groups // experts, group_rows, shared_units)
        shared_rows = lax.all_to_all(shared_rows, "expert", split_axis=0, concat_axis=0, tiled=True)
        grad_shared_up = shared_rows.transpose(2, 1, 0, 3).reshape(group_rows, groups * shared_units).astype(WIDE)

    grad_ada_weight, grad_ada_bias, sent = call(
        functools.partial(ada_body, experts),
        [((group_rows, 6 * width // experts), WIDE), ((1, 6 * width), WIDE), ((total, 8, LANES), WIDE)],
        (where, d_mod_all, cond_all, ada_weight),
        scratch=[((total, 6 * width), LOW)],
        smem=(0,),
    )
    d_cond_act = lax.all_to_all(sent, AXES, split_axis=0, concat_axis=0, tiled=True)
    d_cond_act = d_cond_act[:, 0, :piece].reshape(1, width)
    _, silu_back = jax.vjp(jax.nn.silu, cond.astype(WIDE))
    grad_cond = silu_back(d_cond_act)[0]

    return (
        block_out,
        grad_tokens,
        grad_cond,
        grad_gate_weights.T,
        grad_ada_weight,
        grad_ada_bias[0],
        grad_qkv,
        grad_out,
        grad_shared_up,
        grad_shared_down,
        grad_expert_up[None],
        grad_expert_down[None],
        expert_load,
    )


def solution(mesh):
    rows = P(AXES, None)
    line = P(AXES)
    tiles = P("batch", "expert")
    split = P("expert", "batch", None)
    in_specs = (rows, rows, line, rows, rows, rows, line, rows, rows, rows, rows, split, split, rows)
    out_specs = (rows, rows, rows, rows, tiles, P(), tiles, tiles, tiles, tiles, split, split, P())
    return jax.shard_map(shards, mesh=mesh, in_specs=in_specs, out_specs=out_specs, check_vma=False)
```

```python
import functools

import jax
import jax.numpy as jnp
import numpy as np
from jax import lax
from jax.experimental import pallas as pl
from jax.experimental.pallas import tpu as pltpu
from jax.sharding import PartitionSpec as P

HEADS = 12
HEAD_DIM = 64
AXES = ("batch", "expert")
LOW = jnp.bfloat16
WIDE = jnp.float32
LANES = 128
EXTRA = 16
LIMIT = 24
CURVE = 0.7978845608028654
CUBIC = 0.044715


def dot(left, right):
    return lax.dot_general(left, right, (((1,), (0,)), ((), ())), preferred_element_type=WIDE)


def dot_nt(left, right):
    return lax.dot_general(left, right, (((1,), (1,)), ((), ())), preferred_element_type=WIDE)


def dot_tn(left, right):
    return lax.dot_general(left, right, (((0,), (0,)), ((), ())), preferred_element_type=WIDE)


def up_to(value, step):
    return -(-value // step) * step


def call(body, outs, args, scratch=(), smem=(), limit=LIMIT):
    specs = [pl.BlockSpec(memory_space=pltpu.SMEM) if at in smem else pl.BlockSpec() for at in range(len(args))]
    return pl.pallas_call(
        body,
        out_shape=[jax.ShapeDtypeStruct(shape, kind) for shape, kind in outs],
        in_specs=specs,
        out_specs=[pl.BlockSpec()] * len(outs),
        scratch_shapes=[pltpu.VMEM(shape, kind) for shape, kind in scratch],
        compiler_params=pltpu.CompilerParams(vmem_limit_bytes=limit * 1024 * 1024),
    )(*args)


def sweep(body, steps, ins, outs, scratch=(), limit=40):
    return pl.pallas_call(
        body,
        out_shape=[jax.ShapeDtypeStruct(shape, kind) for shape, kind, _, _ in outs],
        grid=(steps,),
        in_specs=[
            pl.BlockSpec(memory_space=pltpu.SMEM) if block is None else pl.BlockSpec(block, index)
            for _, block, index in ins
        ],
        out_specs=[pl.BlockSpec(block, index) for _, _, block, index in outs],
        scratch_shapes=[pltpu.VMEM(shape, kind) for shape, kind in scratch],
        compiler_params=pltpu.CompilerParams(vmem_limit_bytes=limit * 1024 * 1024),
    )(*[array for array, _, _ in ins])


def pad_lanes(values, width):
    return jnp.pad(values, ((0, 0),) * (values.ndim - 1) + ((0, width - values.shape[-1]),))


def tie(values, *others):
    return lax.optimization_barrier((values, *others))[0]


def together(*values):
    leaves, tree = jax.tree.flatten(values)
    return jax.tree.unflatten(tree, lax.optimization_barrier(tuple(leaves)))


def grown(values, got):
    return jnp.concatenate([values, got], axis=0)


def added(low, got):
    half = ((low.shape[0] // 2,) + low.shape[1:], low.dtype)
    return call(add_body, [half, half], (low, got))


def bits_of(count):
    found = []
    step = 1
    while step < count:
        found.append(step)
        step *= 2
    assert step == count
    return found


def swap(values, mask):
    total = lax.axis_size("batch") * lax.axis_size("expert")
    return lax.ppermute(values, AXES, [(at, at ^ mask) for at in range(total)])


def spread(values, masks, waits=()):
    waits = dict(waits)
    for at, mask in enumerate(masks):
        if at in waits:
            values = tie(values, *waits[at])
        values = jnp.concatenate([values, swap(values, mask)], axis=0)
    return values


def order(masks):
    found = [0]
    for mask in masks:
        found = found + [at ^ mask for at in found]
    return found


def add_body(low, got, keep, send):
    half = keep.shape[0]
    keep[...] = (low[:half].astype(WIDE) + got[:half].astype(WIDE)).astype(keep.dtype)
    send[...] = (low[half:].astype(WIDE) + got[half:].astype(WIDE)).astype(send.dtype)


def add_split_body(low, got, keep, send0, send1):
    half, part = keep.shape[0], send0.shape[0]
    for start, out in ((0, keep), (half, send0), (half + part, send1)):
        here = slice(start, start + out.shape[0])
        out[...] = (low[here].astype(WIDE) + got[here].astype(WIDE)).astype(out.dtype)


def add_join_body(low, got0, got1, keep, send):
    half = keep.shape[0]
    keep[...] = (low[:half].astype(WIDE) + got0[...].astype(WIDE)).astype(keep.dtype)
    send[...] = (low[half:].astype(WIDE) + got1[...].astype(WIDE)).astype(send.dtype)


def fold(lows, highs, orders, waits=()):
    waits = dict(waits)
    lows, highs, sent = list(lows), list(highs), []
    for at in range(len(orders[0]) - 1):
        sent.append(list(highs))
        got = [swap(high, links[-1 - at]) for high, links in zip(highs, orders)]
        if at in waits:
            got = tie(tuple(got), *waits[at])
        for part, other in enumerate(got):
            half = ((other.shape[0] // 2,) + other.shape[1:], other.dtype)
            lows[part], highs[part] = call(add_body, [half, half], (lows[part], other))
    sent.append(list(highs))
    got = [swap(high, links[0]) for high, links in zip(highs, orders)]
    return [half[0] for pair in zip(lows, got) for half in pair], sent


def center_of(values):
    center = values - jnp.mean(values, axis=-1, keepdims=True)
    scale = lax.rsqrt(jnp.mean(center * center, axis=-1, keepdims=True) + 1e-06)
    return center * scale, scale


def norm_back(grad, unit, scale):
    return scale * (
        grad
        - jnp.mean(grad, axis=-1, keepdims=True)
        - unit * jnp.mean(grad * unit, axis=-1, keepdims=True)
    )


def route_body(experts, capacity, groups, routes, gates, lengths, cond, weight, kept, sent):
    count, width = routes.shape[1], cond.shape[1]
    lane = lax.broadcasted_iota(jnp.int32, (8, count), 1)
    row = lax.broadcasted_iota(jnp.int32, (8, count), 0)
    length = lengths[0]
    live = lane < length
    first = (row == routes[0:1]) & live
    second = (row == routes[1:2]) & live
    hits = first.astype(WIDE) + second.astype(WIDE)
    above = (
        lax.broadcasted_iota(jnp.int32, (count, count), 0)
        < lax.broadcasted_iota(jnp.int32, (count, count), 1)
    ).astype(LOW)
    room = (dot(hits.astype(LOW), above) < capacity).astype(WIDE)
    first = first.astype(WIDE) * room
    second = second.astype(WIDE) * room
    weight[...] = first * gates[0:1] + second * gates[1:2]
    kept[0] = first
    kept[1] = second
    rows = width // groups
    tally = jnp.sum(hits, axis=1, keepdims=True)
    spot = lax.broadcasted_iota(jnp.int32, (8, LANES), 1)
    line = lax.broadcasted_iota(jnp.int32, (8, LANES), 0)
    tally = jnp.sum(jnp.where(spot == line + rows, tally, 0.0), axis=0, keepdims=True)
    spot = spot[:1]
    tally = jnp.where(spot == rows + experts, length.astype(WIDE), tally)
    value = cond[...].astype(WIDE)
    value = value / (1.0 + jnp.exp(-value))
    for group in range(groups):
        start = group * rows // LANES * LANES
        part = value[:, start : start + LANES]
        shift = group * rows - start
        if shift:
            tail = value[:, start + LANES : start + 2 * LANES] if start + 2 * LANES <= width else part
            part = jnp.where(
                spot < LANES - shift, pltpu.roll(part, LANES - shift, 1), pltpu.roll(tail, LANES - shift, 1)
            )
        part = jnp.where(spot < rows, part, tally).astype(LOW)
        for expert in range(experts):
            sent[group * experts + expert] = jnp.broadcast_to(part, sent.shape[1:])


def place_of(me, rows, piece, width):
    natural = (rows[0:1] ^ me) * piece + rows[1:2]
    return (lax.broadcasted_iota(jnp.int32, (width, width), 0) == natural).astype(LOW)


def terms_body(where, got, weight, bias, shared, out, loads):
    me, expert = where[0], where[1]
    total, _, _ = got.shape
    piece, wide = weight.shape
    rows = got[:, 0, :]
    pick = (
        lax.broadcasted_iota(jnp.int32, (LANES, piece), 0)
        == lax.broadcasted_iota(jnp.int32, (LANES, piece), 1) + expert * piece
    ).astype(LOW)
    share = bias.shape[1]
    spot = (
        lax.broadcasted_iota(jnp.int32, (share, wide), 1)
        == lax.broadcasted_iota(jnp.int32, (share, wide), 0) + me * share
    ).astype(LOW)
    terms = dot(dot(rows, pick).astype(LOW), weight[...]) + dot(bias[...], spot)
    terms = terms.astype(LOW)
    first = up_to(piece, 8)
    for at in range(wide // LANES):
        out[:, first + at, :] = terms[:, at * LANES : (at + 1) * LANES]
    cols = shared.shape[1] // total
    for at in range(total):
        out[at, :piece, :cols] = shared[:, at * cols : (at + 1) * cols]
    load = jnp.sum(rows.astype(WIDE), axis=0, keepdims=True)
    loads[...] = load


def shift_body(piece, terms, weight, modulation, lines):
    total = modulation.shape[1] // LANES
    first = up_to(piece, 8)
    sums = jnp.sum(terms[:, first : first + total, :].astype(WIDE), axis=0)
    for at in range(total):
        modulation[:, at * LANES : (at + 1) * LANES] = sums[at : at + 1]
    gate = total // 6
    lines[:, :8] = jnp.zeros((lines.shape[0], 8, LANES), WIDE)
    lines[:, :gate] = jnp.broadcast_to(sums[5 * gate :], (lines.shape[0], gate, LANES))
    lines[:, 8:] = jnp.broadcast_to(weight[...], (lines.shape[0], 8, LANES))


def head_pair(values, pair):
    both = values[:, pair * LANES : (pair + 1) * LANES]
    lane = lax.broadcasted_iota(jnp.int32, both.shape, 1)
    zero = jnp.zeros_like(both)
    return jnp.concatenate(
        [jnp.where(lane < HEAD_DIM, both, zero), jnp.where(lane < HEAD_DIM, zero, both)], axis=0
    )


def scores_of(queries, stacked, pair, length):
    count = queries.shape[0]
    raw = dot_nt(queries[:, pair * LANES : (pair + 1) * LANES], stacked) * HEAD_DIM ** (-0.5)
    lane = lax.broadcasted_iota(jnp.int32, raw.shape, 1)
    return jnp.where((lane & (count - 1)) < length, raw, -1e30)


def times(left, low, high, cols):
    half = low.shape[0]
    return dot(left[:, :half], low[:, cols]) + dot(left[:, half:], high[:, cols])


def times_back(left, low, high, cols):
    return jnp.concatenate([dot_nt(left, low[:, cols]), dot_nt(left, high[:, cols])], axis=1)


def forward_body(
    piece, where, tokens, modulation, lengths, rows0, rows1, low0, high0, low1, high1,
    both, joined, totals, attn_out, middle_out, *parts,
):
    count, width = tokens.shape
    length = lengths[0]
    mod = modulation[...]
    tok = tokens[...].astype(WIDE)
    unit, _ = center_of(tok)
    first = (unit * (1.0 + mod[:, width : 2 * width]) + mod[:, :width]).astype(LOW)
    both[:, :width] = first
    start = 0
    for rows, low, high in ((rows0, low0, high0), (rows1, low1, high1)):
        moved = dot(first, place_of(where[0], rows, piece, width)).astype(LOW)
        size = min(low.shape[1], 3 * width - start)
        joined[:, start : start + size] = times(moved, low, high, slice(0, size)).astype(LOW)
        start += size
    queries, keys, values = joined[:, :width], joined[:, width : 2 * width], joined[:, 2 * width :]
    lane = lax.broadcasted_iota(jnp.int32, (count, LANES), 1)
    sums = jnp.zeros((count, LANES), WIDE)
    for pair in range(HEADS // 2):
        scores = scores_of(queries, head_pair(keys, pair), pair, length)
        probs = []
        for one in range(2):
            mine = scores[:, one * count : (one + 1) * count]
            top = jnp.max(mine, axis=-1, keepdims=True)
            total = top + jnp.log(jnp.sum(jnp.exp(mine - top), axis=-1, keepdims=True))
            sums = jnp.where(lane == 2 * pair + one, total, sums)
            probs.append(jnp.exp(mine - total).astype(LOW))
        both[:, width + pair * LANES : width + (pair + 1) * LANES] = dot(
            jnp.concatenate(probs, axis=1), head_pair(values, pair)
        ).astype(LOW)
    totals[...] = sums
    moved = dot(both[:, width:], place_of(where[0], rows1, piece, width)).astype(LOW)
    attn = times(moved, low1, high1, slice(width, 2 * width))
    attn_out[...] = attn
    middle = tok + mod[:, 2 * width : 3 * width] * attn
    middle_out[...] = middle
    unit, _ = center_of(middle)
    second = (unit * (1.0 + mod[:, 4 * width : 5 * width]) + mod[:, 3 * width : 4 * width]).astype(LOW)
    start = 0
    for part in parts:
        part[...] = second[:, start : start + part.shape[1]]
        start += part.shape[1]


def backward_body(
    piece, where, tokens, cotangent, modulation, lengths, rows0, rows1, low0, high0, low1, high1,
    joined, totals, attn_in, middle_in, near0, far0, near1, far1,
    grad_tokens, sent, lines, d_rows, d_cols, d_mod,
):
    count, width = tokens.shape
    length = lengths[0]
    mod = modulation[...]
    start = 0
    for low, high in ((near0, far0), (near1, far1)):
        size = low.shape[1]
        total = low[...].astype(WIDE) + high[...].astype(WIDE)
        d_rows[:, start : start + size] = total[:count]
        d_mod[:, 5 * width + start : 5 * width + start + size] = total[count : count + 1]
        start += size
    d_second = d_rows[...]
    attn = attn_in[...]
    unit, scale = center_of(middle_in[...])
    d_mod[:, 3 * width : 4 * width] = jnp.sum(d_second, axis=0, keepdims=True)
    d_mod[:, 4 * width : 5 * width] = jnp.sum(d_second * unit, axis=0, keepdims=True)
    d_middle = cotangent[...].astype(WIDE) + norm_back(
        d_second * (1.0 + mod[:, 4 * width : 5 * width]), unit, scale
    )
    d_mod[:, 2 * width : 3 * width] = jnp.sum(d_middle * attn, axis=0, keepdims=True)
    d_attn = (mod[:, 2 * width : 3 * width] * d_middle).astype(LOW)
    d_cols[:, 3 * width :] = d_attn
    d_attended = dot_nt(
        times_back(d_attn, low1, high1, slice(width, 2 * width)).astype(LOW), place_of(where[0], rows1, piece, width)
    ).astype(LOW)
    queries, keys, values = joined[:, :width], joined[:, width : 2 * width], joined[:, 2 * width :]
    sums = totals[...]
    lane = lax.broadcasted_iota(jnp.int32, (count, LANES), 1)
    factor = HEAD_DIM ** (-0.5)
    for pair in range(HEADS // 2):
        at = slice(pair * LANES, (pair + 1) * LANES)
        k_pair, v_pair = head_pair(keys, pair), head_pair(values, pair)
        scores = scores_of(queries, k_pair, pair, length)
        d_probs = dot_nt(d_attended[:, at], v_pair)
        probs_low, d_scores_low = [], []
        for one in range(2):
            half = slice(one * count, (one + 1) * count)
            total = jnp.sum(jnp.where(lane == 2 * pair + one, sums, 0.0), axis=1, keepdims=True)
            probs = jnp.exp(scores[:, half] - total)
            back = d_probs[:, half]
            d_scores = probs * (back - jnp.sum(probs * back, axis=-1, keepdims=True))
            probs_low.append(probs.astype(LOW))
            d_scores_low.append(d_scores.astype(LOW))
        d_scores_both = jnp.concatenate(d_scores_low, axis=1)
        d_cols[:, at] = (dot(d_scores_both, k_pair) * factor).astype(LOW)
        q_pair, d_pair = queries[:, at], d_attended[:, at]
        d_k = dot_tn(d_scores_both, q_pair) * factor
        d_v = dot_tn(jnp.concatenate(probs_low, axis=1), d_pair)
        d_k = jnp.where(lane < HEAD_DIM, d_k[:count], d_k[count:])
        d_v = jnp.where(lane < HEAD_DIM, d_v[:count], d_v[count:])
        d_cols[:, width + pair * LANES : width + (pair + 1) * LANES] = d_k.astype(LOW)
        d_cols[:, 2 * width + pair * LANES : 2 * width + (pair + 1) * LANES] = d_v.astype(LOW)
    d_first = jnp.zeros((count, width), WIDE)
    start = 0
    for rows, low, high in ((rows0, low0, high0), (rows1, low1, high1)):
        size = min(low.shape[1], 3 * width - start)
        part = times_back(d_cols[:, start : start + size], low, high, slice(0, size))
        start += size
        place = place_of(where[0], rows, piece, width)
        top = part.astype(LOW)
        rest = (part - top.astype(WIDE)).astype(LOW)
        d_first += dot_nt(top, place) + dot_nt(rest, place)
    unit, scale = center_of(tokens[...].astype(WIDE))
    d_mod[:, :width] = jnp.sum(d_first, axis=0, keepdims=True)
    d_mod[:, width : 2 * width] = jnp.sum(d_first * unit, axis=0, keepdims=True)
    grad_tokens[...] = d_middle + norm_back(
        d_first * (1.0 + mod[:, width : 2 * width]), unit, scale
    )
    for at in range(lines.shape[1]):
        line = d_mod[:, at * LANES : (at + 1) * LANES].astype(LOW)
        lines[:, at, :] = jnp.broadcast_to(line, (lines.shape[0], LANES))
    experts = sent.shape[0]
    cols, out_cols = 3 * width // experts, width // experts
    for expert in range(experts):
        to = expert ^ where[1]
        sent[to, :, :cols] = d_cols[:, expert * cols : (expert + 1) * cols]
        sent[to, :, cols:] = d_cols[:, 3 * width + expert * out_cols : 3 * width + (expert + 1) * out_cols]


def join_rows(lows, highs, rows):
    start = 0
    half = rows.shape[0] // 2
    for low, high in zip(lows, highs):
        share = low.shape[-1]
        for at, part in enumerate((low, high)):
            rows[at * half : (at + 1) * half, start : start + share] = part[...].reshape(half, share)
        start += share


def item_of(where, links, at, block):
    core, outer, inner = links
    item = where[0] ^ (core[0] * at) ^ (inner[0] * block)
    for bit, mask in enumerate(outer):
        item = item ^ ((pl.program_id(0) >> bit & 1) * mask)
    return item


def d_act_body(links, where, low, high, lines, down, d_act, rows):
    count, width = low.shape[-2:]
    for at, part in enumerate((low, high)):
        for block in range(2):
            item = item_of(where, links, at, block)
            here = slice((2 * at + block) * count, (2 * at + block + 1) * count)
            for line in range(width // LANES):
                cols = slice(line * LANES, (line + 1) * LANES)
                rows[0, here, cols] = (
                    part[block, :, cols].astype(WIDE) * lines[item, line : line + 1]
                ).astype(LOW)
    d_act[0] = dot_nt(rows[0], down[...]).astype(LOW)


def hidden_body(links, routed, where, *refs):
    lows, highs, cots, (lines, d_act, up, down) = refs[:2], refs[2:4], refs[4:6], refs[6:10]
    back_lows, back_highs, branches, (d_pre, act, rows) = refs[10:12], refs[12:14], refs[14:16], refs[16:]
    join_rows(lows, highs, rows)
    count = rows.shape[0] // 4
    width = up.shape[0]
    expert = where[1]
    flat = lax.broadcasted_iota(jnp.int32, (count, count), 0) == lax.broadcasted_iota(jnp.int32, (count, count), 1)
    spare = lax.broadcasted_iota(jnp.int32, (EXTRA, width), 0)
    blocks = [(at, block) for at in range(2) for block in range(2)]
    weights = []
    for at, block in blocks:
        line = lines[item_of(where, links, at, block), pl.ds(8 + expert, 1)]
        weights.append(jnp.sum(jnp.where(flat, line, 0.0), axis=1, keepdims=True))
    weight = jnp.concatenate(weights, axis=0)
    pre = dot(rows[...], up[...])
    square = pre * pre
    bend = jnp.tanh(pre * (CURVE + (CURVE * CUBIC) * square))
    gate = 0.5 + 0.5 * bend
    hidden = pre * gate
    slope = gate + hidden * (1.0 - bend) * (CURVE + (3.0 * CURVE * CUBIC) * square)
    d_hidden = d_act[0].astype(WIDE)
    d_full = d_hidden * slope
    d_low = jnp.concatenate([d_full[:, :routed] * weight, d_full[:, routed:]], axis=1).astype(LOW)
    d_pre[0] = d_low
    act_low = jnp.concatenate([hidden[:, :routed] * weight, hidden[:, routed:]], axis=1).astype(LOW)
    act[0] = act_low
    pair = jnp.sum(hidden[:, :routed] * d_hidden[:, :routed], axis=1, keepdims=True)
    back = dot_nt(d_low, up[...]).astype(LOW)
    out = dot(act_low, down[...])
    for number, (at, block) in enumerate(blocks):
        one = slice(number * count, (number + 1) * count)
        body, extra = slice(0, count), slice(count, count + EXTRA)
        d_gate = jnp.sum(out[one] * cots[at][block].astype(WIDE), axis=0, keepdims=True)
        d_gate = jnp.where(spare == 0, d_gate, 0.0).astype(LOW)
        start = 0
        for ref in (back_lows, back_highs)[at]:
            size = ref.shape[-1]
            ref[block, body] = back[one, start : start + size]
            ref[block, extra] = d_gate[:, start : start + size]
            start += size
        ref = branches[at]
        ref[block, body] = out[one].astype(LOW)
        line = jnp.sum(jnp.where(flat, pair[one], 0.0), axis=0, keepdims=True)
        ref[block, extra] = jnp.zeros((EXTRA, width), LOW)
        ref[block, extra, :count] = jnp.where(spare[:, :count] == expert, line, 0.0).astype(LOW)


def grads_body(write, where, *refs):
    second, d_mlp, d_pre, act = refs[:4], refs[4], refs[5], refs[6]
    outs, (rows, up_sum, down_sum) = refs[7:-3], refs[-3:]
    step = pl.program_id(0)

    @pl.when(step == 0)
    def _():
        up_sum[...] = jnp.zeros(up_sum.shape, WIDE)
        down_sum[...] = jnp.zeros(down_sum.shape, WIDE)

    join_rows(second[:2], second[2:], rows)
    up_sum[...] += dot_tn(rows[...], d_pre[0])
    down_sum[...] += dot_tn(act[0], d_mlp[0])

    @pl.when(step == pl.num_programs(0) - 1)
    def _():
        write(where, up_sum, down_sum, outs)


def write_whole(where, up_sum, down_sum, outs):
    outs[0][...] = up_sum[...]
    outs[1][...] = down_sum[...]


def place_and_twin(where):
    return where[2] // 2, where[2] % 2


def rows_at(number, size):
    return pl.ds(pl.multiple_of(number * size, 16), size)


def lanes_at(number, size):
    return pl.ds(pl.multiple_of(number * size, LANES), size)


def up_sent_body(where, weight, near, away):
    place, _ = place_and_twin(where)
    for at in range(4):
        (near if at < 2 else away)[at % 2] = weight[:, lanes_at(place ^ at, near.shape[2])]


def up_join_body(where, own, shared, other, shared_other, full):
    place, twin = place_and_twin(where)
    rows, cols = own.shape[1], own.shape[2]
    for at, mask in enumerate((0, 2, 1, 3)):
        full[rows_at(2 * (place ^ mask) + twin, rows), :cols] = own[at]
        full[rows_at(2 * (place ^ mask) + 1 - twin, rows), :cols] = other[at]
    size = shared.shape[1]
    blank = jnp.zeros((full.shape[0], LANES - size), LOW)
    for at, piece in enumerate((shared, shared_other)):
        start = cols + at * LANES
        full[:, start : start + size] = piece[...]
        full[:, start + size : start + LANES] = blank


def down_join_body(where, own, other, full):
    _, twin = place_and_twin(where)
    rows = (full.shape[0] - 2 * LANES) // 2
    size = own.shape[0] - rows
    blank = jnp.zeros((LANES - size, full.shape[1]), LOW)
    for at, piece in enumerate((own, other)):
        full[rows_at(twin if at == 0 else 1 - twin, rows)] = piece[:rows]
        start = 2 * rows + at * LANES
        full[start : start + size] = piece[rows:]
        full[start + size : start + LANES] = blank


def write_twins(where, up_sum, down_sum, outs):
    keep_up, send_up0, send_up1, keep_down, send_down = outs
    place, twin = place_and_twin(where)
    rows, units = keep_up.shape[1], 2 * (down_sum.shape[0] - 2 * LANES) // 2
    size = (keep_up.shape[2] - units) // 2
    mine, other = slice(units, units + size), slice(units + LANES, units + LANES + size)
    for out, first, at_twin, order_ in (
        (keep_up, 0, twin, (mine, other)),
        (send_up0, 0, 1 - twin, (other, mine)),
        (send_up1, 2, 1 - twin, (other, mine)),
    ):
        for at in range(out.shape[0]):
            here = rows_at(2 * (place ^ (first + at)) + at_twin, rows)
            out[at, :, :units] = up_sum[here, :units].astype(LOW)
            for number, cols in enumerate(order_):
                start = units + number * size
                out[at, :, start : start + size] = up_sum[here, cols].astype(LOW)
    half = units // 2
    for out, at_twin, rows_ in ((keep_down, twin, mine), (send_down, 1 - twin, other)):
        out[:half] = down_sum[rows_at(at_twin, half)].astype(out.dtype)
        out[half:] = down_sum[rows_].astype(out.dtype)


def twin_up_body(keep, got0, got1, *ups):
    for at, out in enumerate(ups):
        got = (got0, got1)[at // 2][at % 2]
        out[...] = (keep[at].astype(WIDE) + got.astype(WIDE)).astype(LOW)


def twin_down_body(keep, got, grad_down, shared_down):
    half = grad_down.shape[0]
    grad_down[...] = keep[:half] + got[:half].astype(WIDE)
    shared_down[...] = (keep[half:] + got[half:].astype(WIDE)).astype(LOW)


def up_rows_body(where, up0, up1, up2, up3, shared_down, grad_up, sent):
    place, twin = place_and_twin(where)
    expert = where[1]
    units = grad_up.shape[1] // 4
    size = (up0.shape[1] - units) // 2
    cols = sent.shape[2] - 2 * size
    for at, piece in enumerate((up0, up1, up2, up3)):
        grad_up[:, lanes_at(place ^ at, units)] = piece[:, :units].astype(WIDE)
        mine, other = piece[:, units : units + size], piece[:, units + size :]
        sent[(place ^ at) ^ expert, :, :size] = jnp.where(twin == 0, mine, other)
        sent[(place ^ at) ^ expert, :, size : 2 * size] = jnp.where(twin == 0, other, mine)
    for to in range(4):
        sent[to ^ expert, :, 2 * size :] = shared_down[:, to * cols : (to + 1) * cols]


def shared_rows_body(where, got0, got1, got2, got3, grad_up, grad_down, held):
    expert = where[1]
    for at, got in enumerate((got0, got1, got2, got3)):
        held[at ^ expert] = got[...]
    size = grad_up.shape[1] // 8
    for source in range(4):
        for twin in range(2):
            start = (4 * twin + source) * size
            grad_up[:, start : start + size] = held[source, :, twin * size : (twin + 1) * size].astype(WIDE)
        grad_down[source * size : (source + 1) * size] = held[source, :, 2 * size :].astype(WIDE)


def attn_terms_body(masks, where, both0, both1, both2, both3, cols0, cols1, cols2, cols3, low0, low1, high0, high1, term):
    group = where[2]
    width = both0.shape[1] // 2
    cut = 3 * width // 4
    rows = low0.shape[1]
    pairs = zip((both0, both1, both2, both3), (cols0, cols1, cols2, cols3))
    for at, (inputs, cols) in enumerate(pairs):
        parts = (dot_tn(inputs[:, :width], cols[:, :cut]), dot_tn(inputs[:, width:], cols[:, cut:]))
        for start, part in ((0, parts[0]), (cut, parts[1])):
            here = slice(start, start + part.shape[1])
            if at:
                term[:, here] += part
            else:
                term[:, here] = part
    half = width // 2
    for number, (low, high) in enumerate(((low0, high0), (low1, high1))):
        for at, mask in enumerate(masks[number]):
            ref = low if at < 4 else high
            ref[at % 4] = term[rows_at(group ^ mask, rows), number * half : (number + 1) * half].astype(LOW)


def attn_out_body(near0, far0, near1, far1, grad_qkv, grad_out, total):
    half = near0.shape[1]
    for at, (near, far) in enumerate(((near0, far0), (near1, far1))):
        total[:, at * half : (at + 1) * half] = near[...].astype(WIDE) + far[...].astype(WIDE)
    cut = grad_qkv.shape[1]
    grad_qkv[...] = total[:, :cut]
    grad_out[...] = total[:, cut:]


def finish_body(modulation, middle, kept, low, high, block_out, grad_gates, total):
    count, width = middle.shape
    total[...] = low[...].astype(WIDE) + high[...].astype(WIDE)
    block_out[...] = middle[...] + modulation[:, 5 * width :] * total[:count]
    pairs = total[count : count + 8, :count]
    for choice in range(2):
        grad_gates[choice : choice + 1] = jnp.sum(kept[choice] * pairs, axis=0, keepdims=True)


def ada_body(experts, where, got, cond, weight, grad_weight, grad_bias, sent, d_mod):
    expert = where[1]
    total, lines, _ = got.shape
    for at in range(lines):
        d_mod[:, at * LANES : (at + 1) * LANES] = got[:, at, :]
    grad_bias[...] = jnp.sum(d_mod[...].astype(WIDE), axis=0, keepdims=True)
    cols = grad_weight.shape[1]
    mine = d_mod[:, pl.ds(pl.multiple_of(expert * cols, LANES), cols)]
    grad_weight[...] = dot_tn(cond[:, 0, :], mine)[: grad_weight.shape[0]]
    piece = weight.shape[0]
    back = dot_nt(d_mod[...], weight[...])
    sent[...] = jnp.zeros(sent.shape, WIDE)
    sent[:, 0, :piece] = back


def attn_grads_body(both, d_cols, out):
    experts, count, cols = d_cols.shape
    width = both.shape[2] // 2
    groups, rows, _ = out.shape
    flat = d_cols[...].reshape(experts * count, cols)
    inputs = both[...].reshape(experts * count, 2 * width)
    cut = 3 * cols // 4
    out[...] = jnp.concatenate(
        [dot_tn(inputs[:, :width], flat[:, :cut]), dot_tn(inputs[:, width:], flat[:, cut:])], axis=1
    ).astype(LOW).reshape(groups, rows, cols)


def attn_sum_body(got, grad_qkv, grad_out):
    total = jnp.sum(got[...].astype(WIDE), axis=0)
    cut = grad_qkv.shape[1]
    grad_qkv[...] = total[:, :cut]
    grad_out[...] = total[:, cut:]


def up_out_body(units, got, grad_up):
    for group in range(got.shape[0]):
        grad_up[:, group * units : (group + 1) * units] = got[group, :, :units].astype(WIDE)


def gather_far(pieces, masks):
    found = [pieces]
    for mask in masks:
        found = found + [[swap(piece, mask) for piece in held] for held in found]
    return found


def shards(
    tokens,
    cond,
    lengths,
    routes,
    gate_weights,
    ada_weight,
    ada_bias,
    qkv_weight,
    out_weight,
    shared_up,
    shared_down,
    expert_up,
    expert_down,
    cotangent,
):
    count, width = tokens.shape
    experts = lax.axis_size("expert")
    groups = lax.axis_size("batch")
    total = experts * groups
    me = lax.axis_index(AXES)
    my_expert = lax.axis_index("expert")
    my_group = lax.axis_index("batch")
    where = jnp.stack([me, my_expert, my_group]).astype(jnp.int32)
    capacity = 5 * 2 * count // (4 * experts)
    piece = ada_weight.shape[0]
    group_rows = width // groups
    shared_units = shared_down.shape[0]
    units = expert_down.shape[1]
    shares = [width // 2, width // 2]
    tall = (count, width)
    lines = 6 * width // LANES

    expert_masks = bits_of(experts)
    group_masks = [experts * step for step in bits_of(groups)]
    away = list(reversed(group_masks[1:3]))
    far = group_masks[:1] + group_masks[3:]
    core, across = expert_masks[:1], expert_masks[1:]
    team_links = [away + across, across + away]
    inner, outer = away[:1], across + away[1:]
    links = (core, outer, inner)
    steps = 2 ** len(outer)
    weight_links = [far[1:] + away + far[:1] + across, far[1:] + away + across + far[:1]]
    paired = groups == 8 and experts == 4
    away_masks = order(sorted(away))

    pair_weight, kept, sent = call(
        functools.partial(route_body, experts, capacity, groups),
        [((8, count), WIDE), ((2, 8, count), WIDE), ((total, 16, LANES), LOW)],
        (routes.T, gate_weights.T, lengths, cond),
        smem=(2,),
    )
    cond_all = lax.all_to_all(sent, AXES, split_axis=0, concat_axis=0, tiled=True)

    attn_w = jnp.concatenate([qkv_weight, out_weight], axis=1)[None]
    cot = cotangent[None]
    down_own = jnp.concatenate([expert_down[0], shared_down], axis=0)
    down_other = swap(down_own, far[0])
    first_links = far[1:] + away
    for at, mask in enumerate(first_links):
        attn_got = swap(attn_w, mask)
        if at == 0:
            cot_got = swap(cot, away[0])
            attn_got, cond_all = together(attn_got, cond_all)
            terms, loads = call(
                terms_body,
                [((total, up_to(up_to(piece, 8) + lines, 8), LANES), LOW), ((1, LANES), WIDE)],
                (where, cond_all, ada_weight, ada_bias[None], shared_up),
                smem=(0,),
            )
            terms_got = lax.all_to_all(terms, AXES, split_axis=0, concat_axis=0, tiled=True)
        if at == len(first_links) - 1:
            attn_got, terms, down_other, cot_got = together(attn_got, terms, down_other, cot_got)
            cot = grown(cot, cot_got)
        attn_w = grown(attn_w, attn_got)
    cot_links = away + across
    tallies = loads[0, group_rows : group_rows + experts + 1]
    expert_load = tallies[:experts] * experts / (2.0 * tallies[experts])
    attn_parts = [attn_w[:, :, : 2 * width], attn_w[:, :, 2 * width :]]
    last_links = [far[:1] + across, across + far[:1]]
    weight_links = [first_links + masks for masks in last_links]
    if paired:
        place_units = expert_up.shape[2] // 4
        up_near, up_away = call(
            up_sent_body, [((2, group_rows, place_units), LOW)] * 2, (where, expert_up[0]), smem=(0,)
        )
    for at in range(len(last_links[0])):
        got = [swap(part, masks[at]) for part, masks in zip(attn_parts, last_links)]
        if at == 0:
            if paired:
                up_got = swap(up_away, away[0])
                got, up_got = together(got, up_got)
        elif at == len(last_links[0]) - 1:
            cot_got = swap(cot, away[1])
            got, cot_got, terms_got = together(got, cot_got, terms_got)
            cot = grown(cot, cot_got)
        attn_parts = [grown(*pair) for pair in zip(attn_parts, got)]
    part_shared_up = terms_got[:, :piece, :shared_units].reshape(width, shared_units)
    modulation, own_lines = call(
        functools.partial(shift_body, piece),
        [((1, 6 * width), WIDE), ((total, 16, LANES), WIDE)],
        (terms_got, pair_weight),
    )
    attn_far = [swap(part, core[0]) for part in attn_parts]
    cot_got = swap(cot, across[0])
    if paired:
        up_mine = jnp.stack([up_near[0], up_got[0]])
        up_sent = jnp.stack([up_near[1], up_got[1]])
        up_last = swap(up_sent, away[1])
        shared_up_other = swap(part_shared_up, far[0])
    weights = []
    row_places = []
    for low, high, masks in zip(attn_parts, attn_far, weight_links):
        weights += [low.reshape(-1, 2 * width), high.reshape(-1, 2 * width)]
        found = np.repeat(np.array(order(masks + core), np.int32), piece)
        row_places.append(jnp.asarray(np.stack([found, np.tile(np.arange(piece, dtype=np.int32), total)])))

    both, joined, totals, attn, middle, *seconds = call(
        functools.partial(forward_body, piece),
        [
            ((count, 2 * width), LOW),
            ((count, 3 * width), LOW),
            ((count, LANES), WIDE),
            (tall, WIDE),
            (tall, WIDE),
            *[((count, share), LOW) for share in shares],
        ],
        (where, tokens, modulation, lengths, *row_places, *weights),
        smem=(0, 3),
    )

    shared_slot = up_to(shared_units, LANES)
    second_low = [part[None] for part in seconds]
    for at in range(len(away + across)):
        got = [swap(part, masks[at]) for part, masks in zip(second_low, team_links)]
        if at == 0:
            item_lines = lax.all_to_all(tie(own_lines, *seconds), AXES, split_axis=0, concat_axis=0, tiled=True)
            if paired:
                got, up_last, shared_up_other = together(got, up_last, shared_up_other)
                up_own = jnp.concatenate([up_mine, up_last], axis=0)
                up_other = swap(up_own, far[0])
        elif at == 1:
            got, item_lines = together(got, item_lines)
            if paired:
                got, up_other = together(got, up_other)
                routed, hidden = 2 * units, 2 * units + 2 * shared_slot
                (down_cat,) = call(
                    down_join_body, [((hidden, width), LOW)], (where, down_own, down_other), smem=(0,)
                )
        second_got = got
        if at < len(away + across) - 1:
            second_low = [grown(*pair) for pair in zip(second_low, got)]
    if paired:
        (up_cat,) = call(
            up_join_body,
            [((width, hidden), LOW)],
            (where, up_own, part_shared_up, up_other, shared_up_other),
            smem=(0,),
        )
    else:
        part_up = lax.all_to_all(expert_up[0], "batch", split_axis=1, concat_axis=0, tiled=True)
        held = gather_far([part_up, part_shared_up, expert_down[0], shared_down], far)
        slot = up_to(units, LANES)
        routed, hidden = len(held) * slot, len(held) * (slot + shared_slot)
        up_cat = jnp.concatenate(
            [pad_lanes(h[0], slot) for h in held] + [pad_lanes(h[1], shared_slot) for h in held], axis=1
        )
        down_cat = jnp.concatenate(
            [pad_lanes(h[2].T, slot).T for h in held] + [pad_lanes(h[3].T, shared_slot).T for h in held], axis=0
        )

    half = 2 * count

    def whole(array):
        return array, array.shape, lambda step: (0,) * array.ndim

    def block_at(masks, rows, lanes):
        bits = list(reversed(masks))
        block = tuple(2 if mask in inner else None for mask in bits) + (rows, lanes)

        def index(step):
            spot = {mask: step // 2**at % 2 for at, mask in enumerate(outer)}
            return tuple(spot.get(mask, 0) for mask in bits) + (0, 0)

        return block, index

    def block_in(array, masks):
        laid = array.reshape((2,) * len(masks) + array.shape[1:])
        return laid, *block_at(masks, *array.shape[1:])

    def block_out_of(rows, lanes, masks):
        return (2,) * len(masks) + (rows, lanes), LOW, *block_at(masks, rows, lanes)

    def rows_of(array):
        return array, (1,) + array.shape[1:], lambda step: (step, 0, 0)

    def rows_out(lanes):
        return (steps, 2 * half, lanes), LOW, (1, 2 * half, lanes), lambda step: (step, 0, 0)

    def sum_out(shape, kind):
        return shape, kind, shape, lambda step: (0,) * len(shape)

    def flat(part):
        return part.reshape((-1,) + part.shape[-2:])

    scalars = (where, None, None)

    cot_low = grown(cot, tie(cot_got, *second_low))
    for mask in across[1:]:
        cot_low = grown(cot_low, swap(cot_low, mask))
    cot_high = swap(cot_low, core[0])
    cots = [block_in(cot_low, cot_links), block_in(cot_high, cot_links)]
    d_act, d_mlp = sweep(
        functools.partial(d_act_body, links),
        steps,
        [scalars, *cots, whole(item_lines), whole(down_cat)],
        [rows_out(hidden), rows_out(width)],
    )
    second_got, d_act, up_cat = together(second_got, d_act, up_cat)
    second_low = [grown(*pair) for pair in zip(second_low, second_got)]
    second_high = [swap(part, core[0]) for part in second_low]
    second_in = [block_in(part, masks) for parts in (second_low, second_high) for part, masks in zip(parts, team_links)]

    tall_rows = count + EXTRA
    back = [block_out_of(tall_rows, share, masks) for share, masks in zip(shares, team_links)]
    side = block_out_of(tall_rows, width, away + across)
    *parts, d_pre, act = sweep(
        functools.partial(hidden_body, links, routed),
        steps,
        [scalars, *second_in, *cots, whole(item_lines), rows_of(d_act), whole(up_cat), whole(down_cat)],
        [*back, *back, side, side, rows_out(hidden), rows_out(hidden)],
        scratch=[((2 * half, width), LOW)],
    )
    parts = [flat(part) for part in parts]
    if paired:
        both_sent = tie(both, *second_high)
        both_group = [swap(both_sent, mask) for mask in range(1, 4)]
        parts, both_group = together(parts, both_group)
        both_group = [both] + both_group
    if paired:
        up_lanes = place_units + 2 * shared_units
        sum_outs = [
            sum_out((4, group_rows, up_lanes), LOW),
            sum_out((2, group_rows, up_lanes), LOW),
            sum_out((2, group_rows, up_lanes), LOW),
            sum_out((units + shared_units, width), WIDE),
            sum_out((units + shared_units, width), LOW),
        ]
    else:
        sum_outs = [sum_out((width, hidden), WIDE), sum_out((hidden, width), WIDE)]
    grads = sweep(
        functools.partial(grads_body, write_twins if paired else write_whole),
        steps,
        [scalars, *second_in, rows_of(d_mlp), rows_of(d_pre), rows_of(act)],
        sum_outs,
        scratch=[((2 * half, width), LOW), ((width, hidden), WIDE), ((hidden, width), WIDE)],
    )

    lows, highs, orders = list(parts[:2]), list(parts[2:4]), [masks + core for masks in team_links]
    out_low, out_high, out_order = parts[4], parts[5], away + across + core
    sums_at = len(orders[0]) - 1
    out_got = swap(out_high, core[0])
    for at in range(sums_at + 1):
        got = [swap(high, masks[-1 - at]) for high, masks in zip(highs, orders)]
        if at == 1:
            got, grads, out_got = together(got, list(grads), out_got)
            if paired:
                keep_up, send_up0, send_up1, keep_down, send_down = grads
                twin_up0, twin_up1 = swap(send_up0, far[0]), swap(send_up1, far[0])
                twin_down = swap(send_down, far[0])
        elif at == 2 and paired:
            out_got = swap(out_send0, across[0])
            got, out_got, twin_up0 = together(got, out_got, twin_up0)
        elif at == sums_at and paired:
            out_got1 = swap(out_send1, across[0])
            got, twin_up1 = together(got, twin_up1)
        else:
            got = together(*got)
        if at < sums_at:
            pairs = [added(low, other) for low, other in zip(lows, got)]
            lows, highs = [pair[0] for pair in pairs], [pair[1] for pair in pairs]
        if at == 1 and paired:
            block = out_low.shape[1:]
            out_low, out_send0, out_send1 = call(
                add_split_body,
                [((4, *block), LOW), ((2, *block), LOW), ((2, *block), LOW)],
                (out_low, out_got),
            )
        elif at == 1:
            for mask in reversed((away + across)):
                out_low, out_high = added(out_low, out_got)
                out_got = swap(out_high, mask)
    folded = [half_[0] for pair in zip(lows, got) for half_ in pair]
    if paired:
        up_own = call(twin_up_body, [((group_rows, up_lanes), LOW)] * 4, (keep_up, twin_up0, twin_up1))
        folded, up_own = together(folded, up_own)
        up_got = [piece_ if at < 2 else swap(piece_, away_masks[at]) for at, piece_ in enumerate(up_own)]

    grad_tokens, d_cols, d_mod_sent = call(
        functools.partial(backward_body, piece),
        [(tall, WIDE), ((experts, count, 4 * width // experts), LOW), ((total, lines, LANES), LOW)],
        (
            where, tokens, cotangent, modulation, lengths, *row_places, *weights,
            joined, totals, attn, middle, *folded,
        ),
        scratch=[(tall, WIDE), ((count, 4 * width), LOW), ((1, 6 * width), WIDE)],
        smem=(0, 4),
    )

    d_mod_all = lax.all_to_all(d_mod_sent, AXES, split_axis=0, concat_axis=0, tiled=True)
    if paired:
        d_cols, up_got[2], out_got1 = together(d_cols, up_got[2], out_got1)
        cols_got = [d_cols[at] if not at else swap(d_cols[at], at) for at in range(4)]
        out_low, out_high = call(
            add_join_body, [((2, *block), LOW), ((2, *block), LOW)], (out_low, out_got, out_got1)
        )
        cols_got, up_got, twin_down = together(cols_got, up_got, twin_down)
        out_got = swap(out_high, away[1])
        up_got[1] = swap(up_got[1], away_masks[1])
        grad_expert_down, shared_own = call(
            twin_down_body, [((units, width), WIDE), ((shared_units, width), LOW)], (keep_down, twin_down)
        )
        sum_links = [away + far, away[:1] + far + away[1:]]
        sum_masks = [[mask // experts for mask in order(masks)] for masks in sum_links]
        term_half = ((4, group_rows, width // 2), LOW)
        attn_sent = call(
            functools.partial(attn_terms_body, sum_masks),
            [term_half] * 4,
            (where, *both_group, *cols_got),
            scratch=[((width, width), WIDE)],
            smem=(0,),
        )
        term_lows, term_highs = attn_sent[:2], attn_sent[2:]
        for at in range(3):
            got = [swap(high, masks[-1 - at]) for high, masks in zip(term_highs, sum_links)]
            if at == 0:
                got, out_got = together(got, out_got)
                out_low, out_high = added(out_low, out_got)
                out_got = swap(out_high, away[0])
            elif at == 1:
                got, up_got = together(got, up_got)
                grad_expert_up, crossed = call(
                    up_rows_body,
                    [
                        ((group_rows, groups * units), WIDE),
                        ((4, group_rows, 2 * shared_units + width // experts), LOW),
                    ],
                    (where, *up_got, shared_own),
                    smem=(0,),
                )
                crossed = [crossed[mask] if not mask else swap(crossed[mask], mask) for mask in range(4)]
            else:
                got, out_got, crossed = together(got, out_got, crossed)
            if at < 2:
                pairs = [added(low, other) for low, other in zip(term_lows, got)]
                term_lows, term_highs = [pair[0] for pair in pairs], [pair[1] for pair in pairs]
        grad_qkv, grad_out = call(
            attn_out_body,
            [((group_rows, 3 * width // experts), WIDE), ((group_rows, width // experts), WIDE)],
            [half_[0] for pair in zip(term_lows, got) for half_ in pair],
            scratch=[((group_rows, width), WIDE)],
        )
    else:
        natural = jnp.arange(experts, dtype=jnp.int32) ^ my_expert
        both_group = lax.all_gather(both, "expert", axis=0)
        d_cols = jnp.take(d_cols, natural, axis=0)
        d_cols = lax.all_to_all(d_cols, "expert", split_axis=0, concat_axis=0, tiled=True)
        (attn_terms,) = call(
            attn_grads_body, [((groups, group_rows, 4 * width // experts), LOW)], (both_group, d_cols)
        )
        attn_terms = lax.all_to_all(attn_terms, "batch", split_axis=0, concat_axis=0, tiled=True)
        grad_qkv, grad_out = call(
            attn_sum_body,
            [((group_rows, 3 * width // experts), WIDE), ((group_rows, width // experts), WIDE)],
            (attn_terms,),
        )

    block_out, grad_gate_weights = call(
        finish_body,
        [(tall, WIDE), ((2, count), WIDE)],
        (modulation, middle, kept, out_low[0], out_got[0]),
        scratch=[((tall_rows, width), WIDE)],
    )

    if paired:
        grad_shared_up, grad_shared_down = call(
            shared_rows_body,
            [((group_rows, width), WIDE), ((experts * shared_units, width // experts), WIDE)],
            (where, *crossed),
            scratch=[((4, group_rows, 2 * shared_units + width // experts), LOW)],
            smem=(0,),
        )
    else:
        grad_up, grad_down = grads
        replicas = hidden // (slot + shared_slot)
        sums = []
        for taken, size, first in ((grad_up.T, units, 0), (grad_up.T, shared_units, routed), (grad_down, units, 0), (grad_down, shared_units, routed)):
            room = up_to(size, LANES)
            held = [taken[first + at * room : first + at * room + size] for at in range(replicas)]
            for mask in reversed(far):
                some = len(held) // 2
                held = [
                    low + swap(high.astype(LOW), mask).astype(WIDE) for low, high in zip(held[:some], held[some:])
                ]
            sums.append(held[0])
        grad_expert_down = sums[2]
        up_rows = jnp.concatenate([sums[0].T, sums[1].T], axis=1).astype(LOW).reshape(groups, group_rows, -1)
        up_rows = lax.all_to_all(up_rows, "batch", split_axis=0, concat_axis=0, tiled=True)
        grad_shared_down = lax.all_to_all(
            sums[3].astype(LOW), "expert", split_axis=1, concat_axis=0, tiled=True
        ).astype(WIDE)
        (grad_expert_up,) = call(
            functools.partial(up_out_body, units), [((group_rows, groups * units), WIDE)], (up_rows,)
        )
        shared_rows = up_rows[:, :, units:].reshape(experts, groups // experts, group_rows, shared_units)
        shared_rows = lax.all_to_all(shared_rows, "expert", split_axis=0, concat_axis=0, tiled=True)
        grad_shared_up = shared_rows.transpose(2, 1, 0, 3).reshape(group_rows, groups * shared_units).astype(WIDE)

    grad_ada_weight, grad_ada_bias, sent = call(
        functools.partial(ada_body, experts),
        [((group_rows, 6 * width // experts), WIDE), ((1, 6 * width), WIDE), ((total, 8, LANES), WIDE)],
        (where, d_mod_all, cond_all, ada_weight),
        scratch=[((total, 6 * width), LOW)],
        smem=(0,),
    )
    d_cond_act = lax.all_to_all(sent, AXES, split_axis=0, concat_axis=0, tiled=True)
    d_cond_act = d_cond_act[:, 0, :piece].reshape(1, width)
    _, silu_back = jax.vjp(jax.nn.silu, cond.astype(WIDE))
    grad_cond = silu_back(d_cond_act)[0]

    return (
        block_out,
        grad_tokens,
        grad_cond,
        grad_gate_weights.T,
        grad_ada_weight,
        grad_ada_bias[0],
        grad_qkv,
        grad_out,
        grad_shared_up,
        grad_shared_down,
        grad_expert_up[None],
        grad_expert_down[None],
        expert_load,
    )


def solution(mesh):
    rows = P(AXES, None)
    line = P(AXES)
    tiles = P("batch", "expert")
    split = P("expert", "batch", None)
    in_specs = (rows, rows, line, rows, rows, rows, line, rows, rows, rows, rows, split, split, rows)
    out_specs = (rows, rows, rows, rows, tiles, P(), tiles, tiles, tiles, tiles, split, split, P())
    return jax.shard_map(shards, mesh=mesh, in_specs=in_specs, out_specs=out_specs, check_vma=False)
```

```python
import functools

import jax
import jax.numpy as jnp
import numpy as np
from jax import lax
from jax.experimental import pallas as pl
from jax.experimental.pallas import tpu as pltpu
from jax.sharding import PartitionSpec as P

HEADS = 12
HEAD_DIM = 64
AXES = ("batch", "expert")
LOW = jnp.bfloat16
WIDE = jnp.float32
LANES = 128
EXTRA = 16
LIMIT = 24
CURVE = 0.7978845608028654
CUBIC = 0.044715


def dot(left, right):
    return lax.dot_general(left, right, (((1,), (0,)), ((), ())), preferred_element_type=WIDE)


def dot_nt(left, right):
    return lax.dot_general(left, right, (((1,), (1,)), ((), ())), preferred_element_type=WIDE)


def dot_tn(left, right):
    return lax.dot_general(left, right, (((0,), (0,)), ((), ())), preferred_element_type=WIDE)


def up_to(value, step):
    return -(-value // step) * step


def call(body, outs, args, scratch=(), smem=(), limit=LIMIT):
    specs = [pl.BlockSpec(memory_space=pltpu.SMEM) if at in smem else pl.BlockSpec() for at in range(len(args))]
    return pl.pallas_call(
        body,
        out_shape=[jax.ShapeDtypeStruct(shape, kind) for shape, kind in outs],
        in_specs=specs,
        out_specs=[pl.BlockSpec()] * len(outs),
        scratch_shapes=[pltpu.VMEM(shape, kind) for shape, kind in scratch],
        compiler_params=pltpu.CompilerParams(vmem_limit_bytes=limit * 1024 * 1024),
    )(*args)


def sweep(body, steps, ins, outs, scratch=(), limit=48):
    return pl.pallas_call(
        body,
        out_shape=[jax.ShapeDtypeStruct(shape, kind) for shape, kind, _, _ in outs],
        grid=(steps,),
        in_specs=[
            pl.BlockSpec(memory_space=pltpu.SMEM) if block is None else pl.BlockSpec(block, index)
            for _, block, index in ins
        ],
        out_specs=[pl.BlockSpec(block, index) for _, _, block, index in outs],
        scratch_shapes=[pltpu.VMEM(shape, kind) for shape, kind in scratch],
        compiler_params=pltpu.CompilerParams(vmem_limit_bytes=limit * 1024 * 1024),
    )(*[array for array, _, _ in ins])


def pad_lanes(values, width):
    return jnp.pad(values, ((0, 0),) * (values.ndim - 1) + ((0, width - values.shape[-1]),))


def tie(values, *others):
    return lax.optimization_barrier((values, *others))[0]


def together(*values):
    leaves, tree = jax.tree.flatten(values)
    return jax.tree.unflatten(tree, lax.optimization_barrier(tuple(leaves)))


def grown(values, got):
    return jnp.concatenate([values, got], axis=0)


def added(low, got):
    half = ((low.shape[0] // 2,) + low.shape[1:], low.dtype)
    return call(add_body, [half, half], (low, got))


def bits_of(count):
    found = []
    step = 1
    while step < count:
        found.append(step)
        step *= 2
    assert step == count
    return found


def swap(values, mask):
    total = lax.axis_size("batch") * lax.axis_size("expert")
    return lax.ppermute(values, AXES, [(at, at ^ mask) for at in range(total)])


def spread(values, masks, waits=()):
    waits = dict(waits)
    for at, mask in enumerate(masks):
        if at in waits:
            values = tie(values, *waits[at])
        values = jnp.concatenate([values, swap(values, mask)], axis=0)
    return values


def order(masks):
    found = [0]
    for mask in masks:
        found = found + [at ^ mask for at in found]
    return found


def add_body(low, got, keep, send):
    half = keep.shape[0]
    keep[...] = (low[:half].astype(WIDE) + got[:half].astype(WIDE)).astype(keep.dtype)
    send[...] = (low[half:].astype(WIDE) + got[half:].astype(WIDE)).astype(send.dtype)


def add_split_body(low, got, keep, send0, send1):
    half, part = keep.shape[0], send0.shape[0]
    for start, out in ((0, keep), (half, send0), (half + part, send1)):
        here = slice(start, start + out.shape[0])
        out[...] = (low[here].astype(WIDE) + got[here].astype(WIDE)).astype(out.dtype)


def add_join_body(low, got0, got1, keep, send):
    half = keep.shape[0]
    keep[...] = (low[:half].astype(WIDE) + got0[...].astype(WIDE)).astype(keep.dtype)
    send[...] = (low[half:].astype(WIDE) + got1[...].astype(WIDE)).astype(send.dtype)


def fold(lows, highs, orders, waits=()):
    waits = dict(waits)
    lows, highs, sent = list(lows), list(highs), []
    for at in range(len(orders[0]) - 1):
        sent.append(list(highs))
        got = [swap(high, links[-1 - at]) for high, links in zip(highs, orders)]
        if at in waits:
            got = tie(tuple(got), *waits[at])
        for part, other in enumerate(got):
            half = ((other.shape[0] // 2,) + other.shape[1:], other.dtype)
            lows[part], highs[part] = call(add_body, [half, half], (lows[part], other))
    sent.append(list(highs))
    got = [swap(high, links[0]) for high, links in zip(highs, orders)]
    return [half[0] for pair in zip(lows, got) for half in pair], sent


def center_of(values):
    center = values - jnp.mean(values, axis=-1, keepdims=True)
    scale = lax.rsqrt(jnp.mean(center * center, axis=-1, keepdims=True) + 1e-06)
    return center * scale, scale


def norm_back(grad, unit, scale):
    return scale * (
        grad
        - jnp.mean(grad, axis=-1, keepdims=True)
        - unit * jnp.mean(grad * unit, axis=-1, keepdims=True)
    )


def route_body(experts, capacity, groups, routes, gates, lengths, cond, weight, kept, sent):
    count, width = routes.shape[1], cond.shape[1]
    lane = lax.broadcasted_iota(jnp.int32, (8, count), 1)
    row = lax.broadcasted_iota(jnp.int32, (8, count), 0)
    length = lengths[0]
    live = lane < length
    first = (row == routes[0:1]) & live
    second = (row == routes[1:2]) & live
    hits = first.astype(WIDE) + second.astype(WIDE)
    above = (
        lax.broadcasted_iota(jnp.int32, (count, count), 0)
        < lax.broadcasted_iota(jnp.int32, (count, count), 1)
    ).astype(LOW)
    room = (dot(hits.astype(LOW), above) < capacity).astype(WIDE)
    first = first.astype(WIDE) * room
    second = second.astype(WIDE) * room
    weight[...] = first * gates[0:1] + second * gates[1:2]
    kept[0] = first
    kept[1] = second
    rows = width // groups
    tally = jnp.sum(hits, axis=1, keepdims=True)
    spot = lax.broadcasted_iota(jnp.int32, (8, LANES), 1)
    line = lax.broadcasted_iota(jnp.int32, (8, LANES), 0)
    tally = jnp.sum(jnp.where(spot == line + rows, tally, 0.0), axis=0, keepdims=True)
    spot = spot[:1]
    tally = jnp.where(spot == rows + experts, length.astype(WIDE), tally)
    value = cond[...].astype(WIDE)
    value = value / (1.0 + jnp.exp(-value))
    for group in range(groups):
        start = group * rows // LANES * LANES
        part = value[:, start : start + LANES]
        shift = group * rows - start
        if shift:
            tail = value[:, start + LANES : start + 2 * LANES] if start + 2 * LANES <= width else part
            part = jnp.where(
                spot < LANES - shift, pltpu.roll(part, LANES - shift, 1), pltpu.roll(tail, LANES - shift, 1)
            )
        part = jnp.where(spot < rows, part, tally).astype(LOW)
        for expert in range(experts):
            sent[group * experts + expert] = jnp.broadcast_to(part, sent.shape[1:])


def place_of(me, rows, piece, width):
    natural = (rows[0:1] ^ me) * piece + rows[1:2]
    return (lax.broadcasted_iota(jnp.int32, (width, width), 0) == natural).astype(LOW)


def terms_body(spot_at, where, got, weight, bias, shared, out, loads):
    me, expert = where[0], where[1]
    total, _, _ = got.shape
    piece, wide = weight.shape
    rows = got[:, 0, :]
    pick = (
        lax.broadcasted_iota(jnp.int32, (LANES, piece), 0)
        == lax.broadcasted_iota(jnp.int32, (LANES, piece), 1) + expert * piece
    ).astype(LOW)
    share = bias.shape[1]
    spot = (
        lax.broadcasted_iota(jnp.int32, (share, wide), 1)
        == lax.broadcasted_iota(jnp.int32, (share, wide), 0) + me * share
    ).astype(LOW)
    terms = dot(dot(rows, pick).astype(LOW), weight[...]) + dot(bias[...], spot)
    terms = terms.astype(LOW)
    first = up_to(piece, 8)
    for at in range(wide // LANES):
        out[:, first + at, :] = terms[:, at * LANES : (at + 1) * LANES]
    cols = shared.shape[1] // total
    for at in range(total):
        out[at, :piece, :cols] = shared[:, at * cols : (at + 1) * cols]
    experts = loads.shape[1]
    tally = pltpu.roll(jnp.sum(rows.astype(WIDE), axis=0, keepdims=True), LANES - spot_at, 1)
    valid = jnp.sum(
        jnp.where(lax.broadcasted_iota(jnp.int32, tally.shape, 1) == experts, tally, 0.0), axis=1, keepdims=True
    )
    loads[...] = (tally * experts / (2.0 * valid))[:, :experts]


def shift_body(piece, terms, weight, modulation, lines):
    total = modulation.shape[1] // LANES
    first = up_to(piece, 8)
    sums = jnp.sum(terms[:, first : first + total, :].astype(WIDE), axis=0)
    for at in range(total):
        modulation[:, at * LANES : (at + 1) * LANES] = sums[at : at + 1]
    gate = total // 6
    lines[:, :8] = jnp.zeros((lines.shape[0], 8, LANES), WIDE)
    lines[:, :gate] = jnp.broadcast_to(sums[5 * gate :], (lines.shape[0], gate, LANES))
    lines[:, 8:] = jnp.broadcast_to(weight[...], (lines.shape[0], 8, LANES))


def head_pair(values, pair):
    both = values[:, pair * LANES : (pair + 1) * LANES]
    lane = lax.broadcasted_iota(jnp.int32, both.shape, 1)
    zero = jnp.zeros_like(both)
    return jnp.concatenate(
        [jnp.where(lane < HEAD_DIM, both, zero), jnp.where(lane < HEAD_DIM, zero, both)], axis=0
    )


def scores_of(queries, stacked, pair, length):
    count = queries.shape[0]
    raw = dot_nt(queries[:, pair * LANES : (pair + 1) * LANES], stacked) * HEAD_DIM ** (-0.5)
    lane = lax.broadcasted_iota(jnp.int32, raw.shape, 1)
    return jnp.where((lane & (count - 1)) < length, raw, -1e30)


def times(left, low, high, cols):
    half = low.shape[0]
    return dot(left[:, :half], low[:, cols]) + dot(left[:, half:], high[:, cols])


def times_back(left, low, high, cols):
    return jnp.concatenate([dot_nt(left, low[:, cols]), dot_nt(left, high[:, cols])], axis=1)


def forward_body(
    piece, where, tokens, modulation, lengths, rows0, rows1, low0, high0, low1, high1,
    both, joined, totals, attn_out, middle_out, *parts,
):
    count, width = tokens.shape
    length = lengths[0]
    mod = modulation[...]
    tok = tokens[...].astype(WIDE)
    unit, _ = center_of(tok)
    first = (unit * (1.0 + mod[:, width : 2 * width]) + mod[:, :width]).astype(LOW)
    both[:, :width] = first
    start = 0
    for rows, low, high in ((rows0, low0, high0), (rows1, low1, high1)):
        moved = dot(first, place_of(where[0], rows, piece, width)).astype(LOW)
        size = min(low.shape[1], 3 * width - start)
        joined[:, start : start + size] = times(moved, low, high, slice(0, size)).astype(LOW)
        start += size
    queries, keys, values = joined[:, :width], joined[:, width : 2 * width], joined[:, 2 * width :]
    lane = lax.broadcasted_iota(jnp.int32, (count, LANES), 1)
    sums = jnp.zeros((count, LANES), WIDE)
    for pair in range(HEADS // 2):
        scores = scores_of(queries, head_pair(keys, pair), pair, length)
        probs = []
        for one in range(2):
            mine = scores[:, one * count : (one + 1) * count]
            top = jnp.max(mine, axis=-1, keepdims=True)
            total = top + jnp.log(jnp.sum(jnp.exp(mine - top), axis=-1, keepdims=True))
            sums = jnp.where(lane == 2 * pair + one, total, sums)
            probs.append(jnp.exp(mine - total).astype(LOW))
        both[:, width + pair * LANES : width + (pair + 1) * LANES] = dot(
            jnp.concatenate(probs, axis=1), head_pair(values, pair)
        ).astype(LOW)
    totals[...] = sums
    moved = dot(both[:, width:], place_of(where[0], rows1, piece, width)).astype(LOW)
    attn = times(moved, low1, high1, slice(width, 2 * width))
    attn_out[...] = attn
    middle = tok + mod[:, 2 * width : 3 * width] * attn
    middle_out[...] = middle
    unit, _ = center_of(middle)
    second = (unit * (1.0 + mod[:, 4 * width : 5 * width]) + mod[:, 3 * width : 4 * width]).astype(LOW)
    start = 0
    for part in parts:
        part[...] = second[:, start : start + part.shape[1]]
        start += part.shape[1]


def backward_body(
    piece, where, tokens, cotangent, modulation, lengths, rows0, rows1, low0, high0, low1, high1,
    joined, totals, attn_in, middle_in, near0, far0, near1, far1,
    grad_tokens, lines, *refs,
):
    sents, (sent, d_rows, d_cols, d_mod) = refs[:-4], refs[-4:]
    count, width = tokens.shape
    length = lengths[0]
    mod = modulation[...]
    start = 0
    for low, high in ((near0, far0), (near1, far1)):
        size = low.shape[1]
        total = low[...].astype(WIDE) + high[...].astype(WIDE)
        d_rows[:, start : start + size] = total[:count]
        d_mod[:, 5 * width + start : 5 * width + start + size] = total[count : count + 1]
        start += size
    d_second = d_rows[...]
    attn = attn_in[...]
    unit, scale = center_of(middle_in[...])
    d_mod[:, 3 * width : 4 * width] = jnp.sum(d_second, axis=0, keepdims=True)
    d_mod[:, 4 * width : 5 * width] = jnp.sum(d_second * unit, axis=0, keepdims=True)
    d_middle = cotangent[...].astype(WIDE) + norm_back(
        d_second * (1.0 + mod[:, 4 * width : 5 * width]), unit, scale
    )
    d_mod[:, 2 * width : 3 * width] = jnp.sum(d_middle * attn, axis=0, keepdims=True)
    d_attn = (mod[:, 2 * width : 3 * width] * d_middle).astype(LOW)
    d_cols[:, 3 * width :] = d_attn
    d_attended = dot_nt(
        times_back(d_attn, low1, high1, slice(width, 2 * width)).astype(LOW), place_of(where[0], rows1, piece, width)
    ).astype(LOW)
    queries, keys, values = joined[:, :width], joined[:, width : 2 * width], joined[:, 2 * width :]
    sums = totals[...]
    lane = lax.broadcasted_iota(jnp.int32, (count, LANES), 1)
    factor = HEAD_DIM ** (-0.5)
    for pair in range(HEADS // 2):
        at = slice(pair * LANES, (pair + 1) * LANES)
        k_pair, v_pair = head_pair(keys, pair), head_pair(values, pair)
        scores = scores_of(queries, k_pair, pair, length)
        d_probs = dot_nt(d_attended[:, at], v_pair)
        probs_low, d_scores_low = [], []
        for one in range(2):
            half = slice(one * count, (one + 1) * count)
            total = jnp.sum(jnp.where(lane == 2 * pair + one, sums, 0.0), axis=1, keepdims=True)
            probs = jnp.exp(scores[:, half] - total)
            back = d_probs[:, half]
            d_scores = probs * (back - jnp.sum(probs * back, axis=-1, keepdims=True))
            probs_low.append(probs.astype(LOW))
            d_scores_low.append(d_scores.astype(LOW))
        d_scores_both = jnp.concatenate(d_scores_low, axis=1)
        d_cols[:, at] = (dot(d_scores_both, k_pair) * factor).astype(LOW)
        q_pair, d_pair = queries[:, at], d_attended[:, at]
        d_k = dot_tn(d_scores_both, q_pair) * factor
        d_v = dot_tn(jnp.concatenate(probs_low, axis=1), d_pair)
        d_k = jnp.where(lane < HEAD_DIM, d_k[:count], d_k[count:])
        d_v = jnp.where(lane < HEAD_DIM, d_v[:count], d_v[count:])
        d_cols[:, width + pair * LANES : width + (pair + 1) * LANES] = d_k.astype(LOW)
        d_cols[:, 2 * width + pair * LANES : 2 * width + (pair + 1) * LANES] = d_v.astype(LOW)
    d_first = jnp.zeros((count, width), WIDE)
    start = 0
    for rows, low, high in ((rows0, low0, high0), (rows1, low1, high1)):
        size = min(low.shape[1], 3 * width - start)
        part = times_back(d_cols[:, start : start + size], low, high, slice(0, size))
        start += size
        place = place_of(where[0], rows, piece, width)
        top = part.astype(LOW)
        rest = (part - top.astype(WIDE)).astype(LOW)
        d_first += dot_nt(top, place) + dot_nt(rest, place)
    unit, scale = center_of(tokens[...].astype(WIDE))
    d_mod[:, :width] = jnp.sum(d_first, axis=0, keepdims=True)
    d_mod[:, width : 2 * width] = jnp.sum(d_first * unit, axis=0, keepdims=True)
    grad_tokens[...] = d_middle + norm_back(
        d_first * (1.0 + mod[:, width : 2 * width]), unit, scale
    )
    for at in range(lines.shape[1]):
        line = d_mod[:, at * LANES : (at + 1) * LANES].astype(LOW)
        lines[:, at, :] = jnp.broadcast_to(line, (lines.shape[0], LANES))
    experts = sent.shape[0]
    cols, out_cols = 3 * width // experts, width // experts
    for expert in range(experts):
        to = expert ^ where[1]
        sent[to, :, :cols] = d_cols[:, expert * cols : (expert + 1) * cols]
        sent[to, :, cols:] = d_cols[:, 3 * width + expert * out_cols : 3 * width + (expert + 1) * out_cols]
    for to, out in enumerate(sents):
        out[...] = sent[to]


def join_rows(lows, highs, rows):
    start = 0
    half = rows.shape[0] // 2
    for low, high in zip(lows, highs):
        share = low.shape[-1]
        for at, part in enumerate((low, high)):
            rows[at * half : (at + 1) * half, start : start + share] = part[...].reshape(half, share)
        start += share


def item_of(where, links, at, block):
    core, outer, inner = links
    item = where[0] ^ (core[0] * at) ^ (inner[0] * block)
    for bit, mask in enumerate(outer):
        item = item ^ ((pl.program_id(0) >> bit & 1) * mask)
    return item


def d_act_body(links, where, low, high, lines, down, d_act, rows):
    count, width = low.shape[-2:]
    for at, part in enumerate((low, high)):
        for block in range(2):
            item = item_of(where, links, at, block)
            here = slice((2 * at + block) * count, (2 * at + block + 1) * count)
            for line in range(width // LANES):
                cols = slice(line * LANES, (line + 1) * LANES)
                rows[0, here, cols] = (
                    part[block, :, cols].astype(WIDE) * lines[item, line : line + 1]
                ).astype(LOW)
    d_act[0] = dot_nt(rows[0], down[...]).astype(LOW)


def hidden_body(links, routed, where, *refs):
    lows, highs, cots, (lines, d_act, up, down) = refs[:2], refs[2:4], refs[4:6], refs[6:10]
    back_lows, back_highs, branches, (d_pre, act, rows) = refs[10:12], refs[12:14], refs[14:16], refs[16:]
    join_rows(lows, highs, rows)
    count = rows.shape[0] // 4
    width = up.shape[0]
    expert = where[1]
    flat = lax.broadcasted_iota(jnp.int32, (count, count), 0) == lax.broadcasted_iota(jnp.int32, (count, count), 1)
    spare = lax.broadcasted_iota(jnp.int32, (EXTRA, width), 0)
    blocks = [(at, block) for at in range(2) for block in range(2)]
    weights = []
    for at, block in blocks:
        line = lines[item_of(where, links, at, block), pl.ds(8 + expert, 1)]
        weights.append(jnp.sum(jnp.where(flat, line, 0.0), axis=1, keepdims=True))
    weight = jnp.concatenate(weights, axis=0)
    pre = dot(rows[...], up[...])
    square = pre * pre
    bend = jnp.tanh(pre * (CURVE + (CURVE * CUBIC) * square))
    gate = 0.5 + 0.5 * bend
    hidden = pre * gate
    slope = gate + hidden * (1.0 - bend) * (CURVE + (3.0 * CURVE * CUBIC) * square)
    d_hidden = d_act[0].astype(WIDE)
    d_full = d_hidden * slope
    d_low = jnp.concatenate([d_full[:, :routed] * weight, d_full[:, routed:]], axis=1).astype(LOW)
    d_pre[0] = d_low
    act_low = jnp.concatenate([hidden[:, :routed] * weight, hidden[:, routed:]], axis=1).astype(LOW)
    act[0] = act_low
    pair = jnp.sum(hidden[:, :routed] * d_hidden[:, :routed], axis=1, keepdims=True)
    back = dot_nt(d_low, up[...]).astype(LOW)
    out = dot(act_low, down[...])
    for number, (at, block) in enumerate(blocks):
        one = slice(number * count, (number + 1) * count)
        body, extra = slice(0, count), slice(count, count + EXTRA)
        d_gate = jnp.sum(out[one] * cots[at][block].astype(WIDE), axis=0, keepdims=True)
        d_gate = jnp.where(spare == 0, d_gate, 0.0).astype(LOW)
        start = 0
        for ref in (back_lows, back_highs)[at]:
            size = ref.shape[-1]
            ref[block, body] = back[one, start : start + size]
            ref[block, extra] = d_gate[:, start : start + size]
            start += size
        ref = branches[at]
        ref[block, body] = out[one].astype(LOW)
        line = jnp.sum(jnp.where(flat, pair[one], 0.0), axis=0, keepdims=True)
        ref[block, extra] = jnp.zeros((EXTRA, width), LOW)
        ref[block, extra, :count] = jnp.where(spare[:, :count] == expert, line, 0.0).astype(LOW)


def up_grads_body(write, where, *refs):
    second, d_pre, outs, (rows, up_sum) = refs[:4], refs[4], refs[5:-2], refs[-2:]
    step = pl.program_id(0)

    @pl.when(step == 0)
    def _():
        up_sum[...] = jnp.zeros(up_sum.shape, WIDE)

    join_rows(second[:2], second[2:], rows)
    up_sum[...] += dot_tn(rows[...], d_pre[0])

    @pl.when(step == pl.num_programs(0) - 1)
    def _():
        write(where, up_sum, outs)


def down_grads_body(write, where, d_mlp, act, *refs):
    outs, down_sum = refs[:-1], refs[-1]
    step = pl.program_id(0)

    @pl.when(step == 0)
    def _():
        down_sum[...] = jnp.zeros(down_sum.shape, WIDE)

    down_sum[...] += dot_tn(act[0], d_mlp[0])

    @pl.when(step == pl.num_programs(0) - 1)
    def _():
        write(where, down_sum, outs)


def write_whole(where, total, outs):
    outs[0][...] = total[...]


def place_and_twin(where):
    return where[2] // 2, where[2] % 2


def rows_at(number, size):
    return pl.ds(pl.multiple_of(number * size, 16), size)


def lanes_at(number, size):
    return pl.ds(pl.multiple_of(number * size, LANES), size)


def up_sent_body(where, weight, near, away):
    place, _ = place_and_twin(where)
    for at in range(4):
        (near if at < 2 else away)[at % 2] = weight[:, lanes_at(place ^ at, near.shape[2])]


def up_join_body(where, own, shared, other, shared_other, full):
    place, twin = place_and_twin(where)
    rows, cols = own.shape[1], own.shape[2]
    for at, mask in enumerate((0, 2, 1, 3)):
        full[rows_at(2 * (place ^ mask) + twin, rows), :cols] = own[at]
        full[rows_at(2 * (place ^ mask) + 1 - twin, rows), :cols] = other[at]
    size = shared.shape[1]
    blank = jnp.zeros((full.shape[0], LANES - size), LOW)
    for at, piece in enumerate((shared, shared_other)):
        start = cols + at * LANES
        full[:, start : start + size] = piece[...]
        full[:, start + size : start + LANES] = blank


def down_join_body(where, own, other, full):
    _, twin = place_and_twin(where)
    rows = (full.shape[0] - 2 * LANES) // 2
    size = own.shape[0] - rows
    blank = jnp.zeros((LANES - size, full.shape[1]), LOW)
    for at, piece in enumerate((own, other)):
        full[rows_at(twin if at == 0 else 1 - twin, rows)] = piece[:rows]
        start = 2 * rows + at * LANES
        full[start : start + size] = piece[rows:]
        full[start + size : start + LANES] = blank


def write_up_twins(where, up_sum, outs):
    keep_up, send_up0, send_up1 = outs
    place, twin = place_and_twin(where)
    rows, units = keep_up.shape[1], up_sum.shape[1] - 2 * LANES
    size = (keep_up.shape[2] - units) // 2
    mine, other = slice(units, units + size), slice(units + LANES, units + LANES + size)
    for out, first, at_twin, order_ in (
        (keep_up, 0, twin, (mine, other)),
        (send_up0, 0, 1 - twin, (other, mine)),
        (send_up1, 2, 1 - twin, (other, mine)),
    ):
        for at in range(out.shape[0]):
            here = rows_at(2 * (place ^ (first + at)) + at_twin, rows)
            out[at, :, :units] = up_sum[here, :units].astype(LOW)
            for number, cols in enumerate(order_):
                start = units + number * size
                out[at, :, start : start + size] = up_sum[here, cols].astype(LOW)


def write_down_twins(where, down_sum, outs):
    keep_down, send_down = outs
    _, twin = place_and_twin(where)
    half = (down_sum.shape[0] - 2 * LANES) // 2
    size = keep_down.shape[0] - half
    start = 2 * half
    for out, at_twin, first in ((keep_down, twin, start), (send_down, 1 - twin, start + LANES)):
        out[:half] = down_sum[rows_at(at_twin, half)].astype(out.dtype)
        out[half:] = down_sum[first : first + size].astype(out.dtype)


def twin_up_body(keep, got0, got1, *ups):
    for at, out in enumerate(ups):
        got = (got0, got1)[at // 2][at % 2]
        out[...] = (keep[at].astype(WIDE) + got.astype(WIDE)).astype(LOW)


def twin_down_body(keep, got, grad_down, shared_down):
    half = grad_down.shape[0]
    grad_down[...] = keep[:half] + got[:half].astype(WIDE)
    shared_down[...] = (keep[half:] + got[half:].astype(WIDE)).astype(LOW)


def up_rows_body(where, up0, up1, up2, up3, shared_down, grad_up, sent):
    place, twin = place_and_twin(where)
    expert = where[1]
    units = grad_up.shape[1] // 4
    size = (up0.shape[1] - units) // 2
    cols = sent.shape[2] - 2 * size
    for at, piece in enumerate((up0, up1, up2, up3)):
        grad_up[:, lanes_at(place ^ at, units)] = piece[:, :units].astype(WIDE)
        mine, other = piece[:, units : units + size], piece[:, units + size :]
        sent[(place ^ at) ^ expert, :, :size] = jnp.where(twin == 0, mine, other)
        sent[(place ^ at) ^ expert, :, size : 2 * size] = jnp.where(twin == 0, other, mine)
    for to in range(4):
        sent[to ^ expert, :, 2 * size :] = shared_down[:, to * cols : (to + 1) * cols]


def shared_rows_body(where, got0, got1, got2, got3, grad_up, grad_down, held):
    expert = where[1]
    for at, got in enumerate((got0, got1, got2, got3)):
        held[at ^ expert] = got[...]
    size = grad_up.shape[1] // 8
    for source in range(4):
        for twin in range(2):
            start = (4 * twin + source) * size
            grad_up[:, start : start + size] = held[source, :, twin * size : (twin + 1) * size].astype(WIDE)
        grad_down[source * size : (source + 1) * size] = held[source, :, 2 * size :].astype(WIDE)


def attn_terms_body(masks, where, both0, both1, both2, both3, cols0, cols1, cols2, cols3, low0, low1, high0, high1, term):
    group = where[2]
    width = both0.shape[1] // 2
    cut = 3 * width // 4
    rows = low0.shape[1]
    pairs = zip((both0, both1, both2, both3), (cols0, cols1, cols2, cols3))
    for at, (inputs, cols) in enumerate(pairs):
        parts = (dot_tn(inputs[:, :width], cols[:, :cut]), dot_tn(inputs[:, width:], cols[:, cut:]))
        for start, part in ((0, parts[0]), (cut, parts[1])):
            here = slice(start, start + part.shape[1])
            if at:
                term[:, here] += part
            else:
                term[:, here] = part
    half = width // 2
    for number, (low, high) in enumerate(((low0, high0), (low1, high1))):
        for at, mask in enumerate(masks[number]):
            ref = low if at < 4 else high
            ref[at % 4] = term[rows_at(group ^ mask, rows), number * half : (number + 1) * half].astype(LOW)


def attn_out_body(near0, far0, near1, far1, grad_qkv, grad_out, total):
    half = near0.shape[1]
    for at, (near, far) in enumerate(((near0, far0), (near1, far1))):
        total[:, at * half : (at + 1) * half] = near[...].astype(WIDE) + far[...].astype(WIDE)
    cut = grad_qkv.shape[1]
    grad_qkv[...] = total[:, :cut]
    grad_out[...] = total[:, cut:]


def finish_body(modulation, middle, kept, low, high, block_out, grad_gates, total):
    count, width = middle.shape
    total[...] = low[...].astype(WIDE) + high[...].astype(WIDE)
    block_out[...] = middle[...] + modulation[:, 5 * width :] * total[:count]
    pairs = total[count : count + 8, :count]
    for choice in range(2):
        grad_gates[choice : choice + 1] = jnp.sum(kept[choice] * pairs, axis=0, keepdims=True)


def ada_body(experts, where, got, cond, weight, grad_weight, grad_bias, sent, d_mod):
    expert = where[1]
    total, lines, _ = got.shape
    for at in range(lines):
        d_mod[:, at * LANES : (at + 1) * LANES] = got[:, at, :]
    grad_bias[...] = jnp.sum(d_mod[...].astype(WIDE), axis=0, keepdims=True)
    cols = grad_weight.shape[1]
    mine = d_mod[:, pl.ds(pl.multiple_of(expert * cols, LANES), cols)]
    grad_weight[...] = dot_tn(cond[:, 0, :], mine)[: grad_weight.shape[0]]
    piece = weight.shape[0]
    back = dot_nt(d_mod[...], weight[...])
    sent[...] = jnp.zeros(sent.shape, WIDE)
    sent[:, 0, :piece] = back


def attn_grads_body(both, d_cols, out):
    experts, count, cols = d_cols.shape
    width = both.shape[2] // 2
    groups, rows, _ = out.shape
    flat = d_cols[...].reshape(experts * count, cols)
    inputs = both[...].reshape(experts * count, 2 * width)
    cut = 3 * cols // 4
    out[...] = jnp.concatenate(
        [dot_tn(inputs[:, :width], flat[:, :cut]), dot_tn(inputs[:, width:], flat[:, cut:])], axis=1
    ).astype(LOW).reshape(groups, rows, cols)


def attn_sum_body(got, grad_qkv, grad_out):
    total = jnp.sum(got[...].astype(WIDE), axis=0)
    cut = grad_qkv.shape[1]
    grad_qkv[...] = total[:, :cut]
    grad_out[...] = total[:, cut:]


def up_out_body(units, got, grad_up):
    for group in range(got.shape[0]):
        grad_up[:, group * units : (group + 1) * units] = got[group, :, :units].astype(WIDE)


def gather_far(pieces, masks):
    found = [pieces]
    for mask in masks:
        found = found + [[swap(piece, mask) for piece in held] for held in found]
    return found


def shards(
    tokens,
    cond,
    lengths,
    routes,
    gate_weights,
    ada_weight,
    ada_bias,
    qkv_weight,
    out_weight,
    shared_up,
    shared_down,
    expert_up,
    expert_down,
    cotangent,
):
    count, width = tokens.shape
    experts = lax.axis_size("expert")
    groups = lax.axis_size("batch")
    total = experts * groups
    me = lax.axis_index(AXES)
    my_expert = lax.axis_index("expert")
    my_group = lax.axis_index("batch")
    where = jnp.stack([me, my_expert, my_group]).astype(jnp.int32)
    capacity = 5 * 2 * count // (4 * experts)
    piece = ada_weight.shape[0]
    group_rows = width // groups
    shared_units = shared_down.shape[0]
    units = expert_down.shape[1]
    shares = [width // 2, width // 2]
    tall = (count, width)
    lines = 6 * width // LANES

    expert_masks = bits_of(experts)
    group_masks = [experts * step for step in bits_of(groups)]
    away = list(reversed(group_masks[1:3]))
    far = group_masks[:1] + group_masks[3:]
    core, across = expert_masks[:1], expert_masks[1:]
    team_links = [away + across, across + away]
    inner, outer = away[:1], across + away[1:]
    links = (core, outer, inner)
    steps = 2 ** len(outer)
    weight_links = [far[1:] + away + far[:1] + across, far[1:] + away + across + far[:1]]
    paired = groups == 8 and experts == 4
    room = 24 if paired else 48
    away_masks = order(sorted(away))

    pair_weight, kept, sent = call(
        functools.partial(route_body, experts, capacity, groups),
        [((8, count), WIDE), ((2, 8, count), WIDE), ((total, 16, LANES), LOW)],
        (routes.T, gate_weights.T, lengths, cond),
        smem=(2,),
    )
    cond_all = lax.all_to_all(sent, AXES, split_axis=0, concat_axis=0, tiled=True)

    attn_w = jnp.concatenate([qkv_weight, out_weight], axis=1)[None]
    cot = cotangent[None]
    down_own = jnp.concatenate([expert_down[0], shared_down], axis=0)
    down_other = swap(down_own, far[0])
    first_links = far[1:] + away
    for at, mask in enumerate(first_links):
        attn_got = swap(attn_w, mask)
        if at == 0:
            cot_got = swap(cot, away[0])
            attn_got, cond_all = together(attn_got, cond_all)
            terms, loads = call(
                functools.partial(terms_body, group_rows),
                [((total, up_to(up_to(piece, 8) + lines, 8), LANES), LOW), ((1, experts), WIDE)],
                (where, cond_all, ada_weight, ada_bias[None], shared_up),
                smem=(0,),
            )
            terms_got = lax.all_to_all(terms, AXES, split_axis=0, concat_axis=0, tiled=True)
        if at == len(first_links) - 1:
            attn_got, terms, down_other, cot_got = together(attn_got, terms, down_other, cot_got)
            cot = grown(cot, cot_got)
        attn_w = grown(attn_w, attn_got)
    cot_links = away + across
    attn_parts = [attn_w[:, :, : 2 * width], attn_w[:, :, 2 * width :]]
    last_links = [far[:1] + across, across + far[:1]]
    weight_links = [first_links + masks for masks in last_links]
    if paired:
        place_units = expert_up.shape[2] // 4
        up_near, up_away = call(
            up_sent_body, [((2, group_rows, place_units), LOW)] * 2, (where, expert_up[0]), smem=(0,)
        )
    for at in range(len(last_links[0])):
        got = [swap(part, masks[at]) for part, masks in zip(attn_parts, last_links)]
        if at == 0:
            if paired:
                up_got = swap(up_away, away[0])
                got, up_got = together(got, up_got)
        elif at == len(last_links[0]) - 1:
            cot_got = swap(cot, away[1])
            got, cot_got, terms_got = together(got, cot_got, terms_got)
            cot = grown(cot, cot_got)
        attn_parts = [grown(*pair) for pair in zip(attn_parts, got)]
    part_shared_up = terms_got[:, :piece, :shared_units].reshape(width, shared_units)
    modulation, own_lines = call(
        functools.partial(shift_body, piece),
        [((1, 6 * width), WIDE), ((total, 16, LANES), WIDE)],
        (terms_got, pair_weight),
    )
    attn_far = [swap(part, core[0]) for part in attn_parts]
    cot_got = swap(cot, across[0])
    if paired:
        up_mine = jnp.stack([up_near[0], up_got[0]])
        up_sent = jnp.stack([up_near[1], up_got[1]])
        up_last = swap(up_sent, away[1])
        shared_up_other = swap(part_shared_up, far[0])
    weights = []
    row_places = []
    for low, high, masks in zip(attn_parts, attn_far, weight_links):
        weights += [low.reshape(-1, 2 * width), high.reshape(-1, 2 * width)]
        found = np.repeat(np.array(order(masks + core), np.int32), piece)
        row_places.append(jnp.asarray(np.stack([found, np.tile(np.arange(piece, dtype=np.int32), total)])))

    both, joined, totals, attn, middle, *seconds = call(
        functools.partial(forward_body, piece),
        [
            ((count, 2 * width), LOW),
            ((count, 3 * width), LOW),
            ((count, LANES), WIDE),
            (tall, WIDE),
            (tall, WIDE),
            *[((count, share), LOW) for share in shares],
        ],
        (where, tokens, modulation, lengths, *row_places, *weights),
        smem=(0, 3),
    )

    shared_slot = up_to(shared_units, LANES)
    second_low = [part[None] for part in seconds]
    for at in range(len(away + across)):
        got = [swap(part, masks[at]) for part, masks in zip(second_low, team_links)]
        if at == 0:
            item_lines = lax.all_to_all(own_lines, AXES, split_axis=0, concat_axis=0, tiled=True)
            got, item_lines = together(got, item_lines)
            if paired:
                got, up_last, shared_up_other = together(got, up_last, shared_up_other)
                up_own = jnp.concatenate([up_mine, up_last], axis=0)
                up_other = swap(up_own, far[0])
        elif at == 1:
            if paired:
                got, up_other, cot_got = together(got, up_other, cot_got)
                routed, hidden = 2 * units, 2 * units + 2 * shared_slot
                (down_cat,) = call(
                    down_join_body, [((hidden, width), LOW)], (where, down_own, down_other), smem=(0,)
                )
        second_got = got
        if at < len(away + across) - 1:
            second_low = [grown(*pair) for pair in zip(second_low, got)]
    if paired:
        (up_cat,) = call(
            up_join_body,
            [((width, hidden), LOW)],
            (where, up_own, part_shared_up, up_other, shared_up_other),
            smem=(0,),
        )
    else:
        part_up = lax.all_to_all(expert_up[0], "batch", split_axis=1, concat_axis=0, tiled=True)
        held = gather_far([part_up, part_shared_up, expert_down[0], shared_down], far)
        slot = up_to(units, LANES)
        routed, hidden = len(held) * slot, len(held) * (slot + shared_slot)
        up_cat = jnp.concatenate(
            [pad_lanes(h[0], slot) for h in held] + [pad_lanes(h[1], shared_slot) for h in held], axis=1
        )
        down_cat = jnp.concatenate(
            [pad_lanes(h[2].T, slot).T for h in held] + [pad_lanes(h[3].T, shared_slot).T for h in held], axis=0
        )

    half = 2 * count

    def whole(array):
        return array, array.shape, lambda step: (0,) * array.ndim

    def block_at(masks, rows, lanes):
        bits = list(reversed(masks))
        block = tuple(2 if mask in inner else None for mask in bits) + (rows, lanes)

        def index(step):
            spot = {mask: step // 2**at % 2 for at, mask in enumerate(outer)}
            return tuple(spot.get(mask, 0) for mask in bits) + (0, 0)

        return block, index

    def block_in(array, masks):
        laid = array.reshape((2,) * len(masks) + array.shape[1:])
        return laid, *block_at(masks, *array.shape[1:])

    def block_out_of(rows, lanes, masks):
        return (2,) * len(masks) + (rows, lanes), LOW, *block_at(masks, rows, lanes)

    def rows_of(array):
        return array, (1,) + array.shape[1:], lambda step: (step, 0, 0)

    def rows_out(lanes):
        return (steps, 2 * half, lanes), LOW, (1, 2 * half, lanes), lambda step: (step, 0, 0)

    def sum_out(shape, kind):
        return shape, kind, shape, lambda step: (0,) * len(shape)

    def flat(part):
        return part.reshape((-1,) + part.shape[-2:])

    scalars = (where, None, None)

    cot_low = grown(cot, tie(cot_got, *second_low))
    for mask in across[1:]:
        cot_low = grown(cot_low, swap(cot_low, mask))
    cot_high = swap(cot_low, core[0])
    cots = [block_in(cot_low, cot_links), block_in(cot_high, cot_links)]
    d_act, d_mlp = sweep(
        functools.partial(d_act_body, links),
        steps,
        [scalars, *cots, whole(item_lines), whole(down_cat)],
        [rows_out(hidden), rows_out(width)],
        limit=room,
    )
    second_got, d_act, up_cat = together(second_got, d_act, up_cat)
    second_low = [grown(*pair) for pair in zip(second_low, second_got)]
    second_high = [swap(part, core[0]) for part in second_low]
    second_in = [block_in(part, masks) for parts in (second_low, second_high) for part, masks in zip(parts, team_links)]

    tall_rows = count + EXTRA
    back = [block_out_of(tall_rows, share, masks) for share, masks in zip(shares, team_links)]
    side = block_out_of(tall_rows, width, away + across)
    *parts, d_pre, act = sweep(
        functools.partial(hidden_body, links, routed),
        steps,
        [scalars, *second_in, *cots, whole(item_lines), rows_of(d_act), whole(up_cat), whole(down_cat)],
        [*back, *back, side, side, rows_out(hidden), rows_out(hidden)],
        scratch=[((2 * half, width), LOW)],
        limit=room,
    )
    parts = [flat(part) for part in parts]
    if paired:
        both_sent = tie(both, *second_high)
        both_group = [swap(both_sent, mask) for mask in range(1, 4)]
        parts, both_group = together(parts, both_group)
        both_group = [both] + both_group
    if paired:
        up_lanes = place_units + 2 * shared_units
        up_outs = [sum_out((blocks, group_rows, up_lanes), LOW) for blocks in (4, 2, 2)]
        down_outs = [sum_out((units + shared_units, width), kind) for kind in (WIDE, LOW)]
    else:
        up_outs, down_outs = [sum_out((width, hidden), WIDE)], [sum_out((hidden, width), WIDE)]
    up_grads = sweep(
        functools.partial(up_grads_body, write_up_twins if paired else write_whole),
        steps,
        [scalars, *second_in, rows_of(d_pre)],
        up_outs,
        scratch=[((2 * half, width), LOW), ((width, hidden), WIDE)],
        limit=room,
    )
    down_grads = sweep(
        functools.partial(down_grads_body, write_down_twins if paired else write_whole),
        steps,
        [scalars, rows_of(d_mlp), rows_of(act)],
        down_outs,
        scratch=[((hidden, width), WIDE)],
        limit=room,
    )

    lows, highs, orders = list(parts[:2]), list(parts[2:4]), [masks + core for masks in team_links]
    out_low, out_high, out_order = parts[4], parts[5], away + across + core
    sums_at = len(orders[0]) - 1
    out_got = swap(out_high, core[0])
    for at in range(sums_at + 1):
        got = [swap(high, masks[-1 - at]) for high, masks in zip(highs, orders)]
        if at == 0:
            got, up_grads = together(got, list(up_grads))
        elif at == 1:
            got, down_grads, out_got = together(got, list(down_grads), out_got)
            if paired:
                keep_up, send_up0, send_up1 = up_grads
                keep_down, send_down = down_grads
                twin_up0, twin_up1 = swap(send_up0, far[0]), swap(send_up1, far[0])
        elif at == 2 and paired:
            out_got = swap(out_send0, across[0])
            got, out_got, twin_up0 = together(got, out_got, twin_up0)
            twin_down = swap(tie(send_down, twin_up0), far[0])
        elif at == sums_at and paired:
            out_got1 = swap(out_send1, across[0])
            got, twin_up1 = together(got, twin_up1)
        else:
            got = together(*got)
        if at < sums_at:
            pairs = [added(low, other) for low, other in zip(lows, got)]
            lows, highs = [pair[0] for pair in pairs], [pair[1] for pair in pairs]
        if at == 1 and paired:
            block = out_low.shape[1:]
            out_low, out_send0, out_send1 = call(
                add_split_body,
                [((4, *block), LOW), ((2, *block), LOW), ((2, *block), LOW)],
                (out_low, out_got),
            )
        elif at == 1:
            for mask in reversed((away + across)):
                out_low, out_high = added(out_low, out_got)
                out_got = swap(out_high, mask)
    folded = [half_[0] for pair in zip(lows, got) for half_ in pair]
    if paired:
        up_own = call(twin_up_body, [((group_rows, up_lanes), LOW)] * 4, (keep_up, twin_up0, twin_up1))
        folded, up_own = together(folded, up_own)
        up_got = [piece_ if at < 2 else swap(piece_, away_masks[at]) for at, piece_ in enumerate(up_own)]

    sent_cols = (count, 4 * width // experts)
    grad_tokens, d_mod_sent, *d_cols = call(
        functools.partial(backward_body, piece),
        [(tall, WIDE), ((total, lines, LANES), LOW), *[(sent_cols, LOW)] * experts],
        (
            where, tokens, cotangent, modulation, lengths, *row_places, *weights,
            joined, totals, attn, middle, *folded,
        ),
        scratch=[((experts, *sent_cols), LOW), (tall, WIDE), ((count, 4 * width), LOW), ((1, 6 * width), WIDE)],
        smem=(0, 4),
    )

    if paired:
        d_cols, up_got[2], out_got1 = together(d_cols, up_got[2], out_got1)
        cols_got = [d_cols[at] if not at else swap(d_cols[at], at) for at in range(4)]
        out_low, out_high = call(
            add_join_body, [((2, *block), LOW), ((2, *block), LOW)], (out_low, out_got, out_got1)
        )
        out_got = swap(out_high, away[1])
        cols_got[1], twin_down, up_got[3] = together(cols_got[1], twin_down, up_got[3])
        grad_expert_down, shared_own = call(
            twin_down_body, [((units, width), WIDE), ((shared_units, width), LOW)], (keep_down, twin_down)
        )
        d_mod_sent = tie(d_mod_sent, shared_own)
        cols_got, up_got, shared_own = together(cols_got, up_got, shared_own)
        up_got[1] = swap(up_got[1], away_masks[1])
        sum_links = [away + far, away[:1] + far + away[1:]]
        sum_masks = [[mask // experts for mask in order(masks)] for masks in sum_links]
        term_half = ((4, group_rows, width // 2), LOW)
        attn_sent = call(
            functools.partial(attn_terms_body, sum_masks),
            [term_half] * 4,
            (where, *both_group, *cols_got),
            scratch=[((width, width), WIDE)],
            smem=(0,),
        )
        term_lows, term_highs = attn_sent[:2], attn_sent[2:]
        for at in range(3):
            got = [swap(high, masks[-1 - at]) for high, masks in zip(term_highs, sum_links)]
            if at == 0:
                got, out_got, up_got = together(got, out_got, up_got)
                out_low, out_high = added(out_low, out_got)
                out_got = swap(out_high, away[0])
            elif at == 1:
                grad_expert_up, crossed = call(
                    up_rows_body,
                    [
                        ((group_rows, groups * units), WIDE),
                        ((4, group_rows, 2 * shared_units + width // experts), LOW),
                    ],
                    (where, *up_got, shared_own),
                    smem=(0,),
                )
                got, crossed = together(got, crossed)
                crossed = [crossed[mask] if not mask else swap(crossed[mask], mask) for mask in range(4)]
            else:
                got, out_got, crossed = together(got, out_got, crossed)
            if at < 2:
                pairs = [added(low, other) for low, other in zip(term_lows, got)]
                term_lows, term_highs = [pair[0] for pair in pairs], [pair[1] for pair in pairs]
        grad_qkv, grad_out = call(
            attn_out_body,
            [((group_rows, 3 * width // experts), WIDE), ((group_rows, width // experts), WIDE)],
            [half_[0] for pair in zip(term_lows, got) for half_ in pair],
            scratch=[((group_rows, width), WIDE)],
        )
    else:
        natural = jnp.arange(experts, dtype=jnp.int32) ^ my_expert
        both_group = lax.all_gather(both, "expert", axis=0)
        d_cols = jnp.take(jnp.stack(d_cols), natural, axis=0)
        d_cols = lax.all_to_all(d_cols, "expert", split_axis=0, concat_axis=0, tiled=True)
        (attn_terms,) = call(
            attn_grads_body, [((groups, group_rows, 4 * width // experts), LOW)], (both_group, d_cols)
        )
        attn_terms = lax.all_to_all(attn_terms, "batch", split_axis=0, concat_axis=0, tiled=True)
        grad_qkv, grad_out = call(
            attn_sum_body,
            [((group_rows, 3 * width // experts), WIDE), ((group_rows, width // experts), WIDE)],
            (attn_terms,),
        )

    block_out, grad_gate_weights = call(
        finish_body,
        [(tall, WIDE), ((2, count), WIDE)],
        (modulation, middle, kept, out_low[0], out_got[0]),
        scratch=[((tall_rows, width), WIDE)],
    )

    if paired:
        grad_shared_up, grad_shared_down = call(
            shared_rows_body,
            [((group_rows, width), WIDE), ((experts * shared_units, width // experts), WIDE)],
            (where, *crossed),
            scratch=[((4, group_rows, 2 * shared_units + width // experts), LOW)],
            smem=(0,),
        )
    else:
        (grad_up,), (grad_down,) = up_grads, down_grads
        replicas = hidden // (slot + shared_slot)
        sums = []
        for taken, size, first in ((grad_up.T, units, 0), (grad_up.T, shared_units, routed), (grad_down, units, 0), (grad_down, shared_units, routed)):
            room = up_to(size, LANES)
            held = [taken[first + at * room : first + at * room + size] for at in range(replicas)]
            for mask in reversed(far):
                some = len(held) // 2
                held = [
                    low + swap(high.astype(LOW), mask).astype(WIDE) for low, high in zip(held[:some], held[some:])
                ]
            sums.append(held[0])
        grad_expert_down = sums[2]
        up_rows = jnp.concatenate([sums[0].T, sums[1].T], axis=1).astype(LOW).reshape(groups, group_rows, -1)
        up_rows = lax.all_to_all(up_rows, "batch", split_axis=0, concat_axis=0, tiled=True)
        grad_shared_down = lax.all_to_all(
            sums[3].astype(LOW), "expert", split_axis=1, concat_axis=0, tiled=True
        ).astype(WIDE)
        (grad_expert_up,) = call(
            functools.partial(up_out_body, units), [((group_rows, groups * units), WIDE)], (up_rows,)
        )
        shared_rows = up_rows[:, :, units:].reshape(experts, groups // experts, group_rows, shared_units)
        shared_rows = lax.all_to_all(shared_rows, "expert", split_axis=0, concat_axis=0, tiled=True)
        grad_shared_up = shared_rows.transpose(2, 1, 0, 3).reshape(group_rows, groups * shared_units).astype(WIDE)

    d_mod_all = lax.all_to_all(d_mod_sent, AXES, split_axis=0, concat_axis=0, tiled=True)
    grad_ada_weight, grad_ada_bias, sent = call(
        functools.partial(ada_body, experts),
        [((group_rows, 6 * width // experts), WIDE), ((1, 6 * width), WIDE), ((total, 8, LANES), WIDE)],
        (where, d_mod_all, cond_all, ada_weight),
        scratch=[((total, 6 * width), LOW)],
        smem=(0,),
    )
    d_cond_act = lax.all_to_all(sent, AXES, split_axis=0, concat_axis=0, tiled=True)
    d_cond_act = d_cond_act[:, 0, :piece].reshape(1, width)
    _, silu_back = jax.vjp(jax.nn.silu, cond.astype(WIDE))
    grad_cond = silu_back(d_cond_act)[0]

    return (
        block_out,
        grad_tokens,
        grad_cond,
        grad_gate_weights.T,
        grad_ada_weight,
        grad_ada_bias[0],
        grad_qkv,
        grad_out,
        grad_shared_up,
        grad_shared_down,
        grad_expert_up[None],
        grad_expert_down[None],
        loads.reshape(experts),
    )


def solution(mesh):
    rows = P(AXES, None)
    line = P(AXES)
    tiles = P("batch", "expert")
    split = P("expert", "batch", None)
    in_specs = (rows, rows, line, rows, rows, rows, line, rows, rows, rows, rows, split, split, rows)
    out_specs = (rows, rows, rows, rows, tiles, P(), tiles, tiles, tiles, tiles, split, split, P())
    return jax.shard_map(shards, mesh=mesh, in_specs=in_specs, out_specs=out_specs, check_vma=False)
```

```python
import functools

import jax
import jax.numpy as jnp
import numpy as np
from jax import lax
from jax.experimental import pallas as pl
from jax.experimental.pallas import tpu as pltpu
from jax.sharding import PartitionSpec as P

HEADS = 12
HEAD_DIM = 64
AXES = ("batch", "expert")
LOW = jnp.bfloat16
WIDE = jnp.float32
LANES = 128
EXTRA = 16
LIMIT = 16
CURVE = 0.7978845608028654
CUBIC = 0.044715


def dot(left, right):
    return lax.dot_general(left, right, (((1,), (0,)), ((), ())), preferred_element_type=WIDE)


def dot_nt(left, right):
    return lax.dot_general(left, right, (((1,), (1,)), ((), ())), preferred_element_type=WIDE)


def dot_tn(left, right):
    return lax.dot_general(left, right, (((0,), (0,)), ((), ())), preferred_element_type=WIDE)


def up_to(value, step):
    return -(-value // step) * step


def call(body, outs, args, scratch=(), smem=(), limit=LIMIT):
    specs = [pl.BlockSpec(memory_space=pltpu.SMEM) if at in smem else pl.BlockSpec() for at in range(len(args))]
    return pl.pallas_call(
        body,
        out_shape=[jax.ShapeDtypeStruct(shape, kind) for shape, kind in outs],
        in_specs=specs,
        out_specs=[pl.BlockSpec()] * len(outs),
        scratch_shapes=[pltpu.VMEM(shape, kind) for shape, kind in scratch],
        compiler_params=pltpu.CompilerParams(vmem_limit_bytes=limit * 1024 * 1024),
    )(*args)


def sweep(body, steps, ins, outs, scratch=(), limit=48):
    return pl.pallas_call(
        body,
        out_shape=[jax.ShapeDtypeStruct(shape, kind) for shape, kind, _, _ in outs],
        grid=(steps,),
        in_specs=[
            pl.BlockSpec(memory_space=pltpu.SMEM) if block is None else pl.BlockSpec(block, index)
            for _, block, index in ins
        ],
        out_specs=[pl.BlockSpec(block, index) for _, _, block, index in outs],
        scratch_shapes=[pltpu.VMEM(shape, kind) for shape, kind in scratch],
        compiler_params=pltpu.CompilerParams(vmem_limit_bytes=limit * 1024 * 1024),
    )(*[array for array, _, _ in ins])


def pad_lanes(values, width):
    return jnp.pad(values, ((0, 0),) * (values.ndim - 1) + ((0, width - values.shape[-1]),))


def tie(values, *others):
    return lax.optimization_barrier((values, *others))[0]


def together(*values):
    leaves, tree = jax.tree.flatten(values)
    return jax.tree.unflatten(tree, lax.optimization_barrier(tuple(leaves)))


def grown(values, got):
    return jnp.concatenate([values, got], axis=0)


def added(low, got):
    half = ((low.shape[0] // 2,) + low.shape[1:], low.dtype)
    return call(add_body, [half, half], (low, got))


def bits_of(count):
    found = []
    step = 1
    while step < count:
        found.append(step)
        step *= 2
    assert step == count
    return found


def swap(values, mask):
    total = lax.axis_size("batch") * lax.axis_size("expert")
    return lax.ppermute(values, AXES, [(at, at ^ mask) for at in range(total)])


def spread(values, masks, waits=()):
    waits = dict(waits)
    for at, mask in enumerate(masks):
        if at in waits:
            values = tie(values, *waits[at])
        values = jnp.concatenate([values, swap(values, mask)], axis=0)
    return values


def order(masks):
    found = [0]
    for mask in masks:
        found = found + [at ^ mask for at in found]
    return found


def add_body(low, got, keep, send):
    half = keep.shape[0]
    keep[...] = (low[:half].astype(WIDE) + got[:half].astype(WIDE)).astype(keep.dtype)
    send[...] = (low[half:].astype(WIDE) + got[half:].astype(WIDE)).astype(send.dtype)


def add_split_body(low, got, keep, send0, send1):
    half, part = keep.shape[0], send0.shape[0]
    for start, out in ((0, keep), (half, send0), (half + part, send1)):
        here = slice(start, start + out.shape[0])
        out[...] = (low[here].astype(WIDE) + got[here].astype(WIDE)).astype(out.dtype)


def add_join_body(low, got0, got1, keep, send):
    half = keep.shape[0]
    keep[...] = (low[:half].astype(WIDE) + got0[...].astype(WIDE)).astype(keep.dtype)
    send[...] = (low[half:].astype(WIDE) + got1[...].astype(WIDE)).astype(send.dtype)


def fold(lows, highs, orders, waits=()):
    waits = dict(waits)
    lows, highs, sent = list(lows), list(highs), []
    for at in range(len(orders[0]) - 1):
        sent.append(list(highs))
        got = [swap(high, links[-1 - at]) for high, links in zip(highs, orders)]
        if at in waits:
            got = tie(tuple(got), *waits[at])
        for part, other in enumerate(got):
            half = ((other.shape[0] // 2,) + other.shape[1:], other.dtype)
            lows[part], highs[part] = call(add_body, [half, half], (lows[part], other))
    sent.append(list(highs))
    got = [swap(high, links[0]) for high, links in zip(highs, orders)]
    return [half[0] for pair in zip(lows, got) for half in pair], sent


def center_of(values):
    center = values - jnp.mean(values, axis=-1, keepdims=True)
    scale = lax.rsqrt(jnp.mean(center * center, axis=-1, keepdims=True) + 1e-06)
    return center * scale, scale


def norm_back(grad, unit, scale):
    return scale * (
        grad
        - jnp.mean(grad, axis=-1, keepdims=True)
        - unit * jnp.mean(grad * unit, axis=-1, keepdims=True)
    )


def route_body(experts, capacity, groups, routes, gates, lengths, cond, weight, kept, sent):
    count, width = routes.shape[1], cond.shape[1]
    lane = lax.broadcasted_iota(jnp.int32, (8, count), 1)
    row = lax.broadcasted_iota(jnp.int32, (8, count), 0)
    length = lengths[0]
    live = lane < length
    first = (row == routes[0:1]) & live
    second = (row == routes[1:2]) & live
    hits = first.astype(WIDE) + second.astype(WIDE)
    above = (
        lax.broadcasted_iota(jnp.int32, (count, count), 0)
        < lax.broadcasted_iota(jnp.int32, (count, count), 1)
    ).astype(LOW)
    room = (dot(hits.astype(LOW), above) < capacity).astype(WIDE)
    first = first.astype(WIDE) * room
    second = second.astype(WIDE) * room
    weight[...] = first * gates[0:1] + second * gates[1:2]
    kept[0] = first
    kept[1] = second
    rows = width // groups
    tally = jnp.sum(hits, axis=1, keepdims=True)
    spot = lax.broadcasted_iota(jnp.int32, (8, LANES), 1)
    line = lax.broadcasted_iota(jnp.int32, (8, LANES), 0)
    tally = jnp.sum(jnp.where(spot == line + rows, tally, 0.0), axis=0, keepdims=True)
    spot = spot[:1]
    tally = jnp.where(spot == rows + experts, length.astype(WIDE), tally)
    value = cond[...].astype(WIDE)
    value = value / (1.0 + jnp.exp(-value))
    for group in range(groups):
        start = group * rows // LANES * LANES
        part = value[:, start : start + LANES]
        shift = group * rows - start
        if shift:
            tail = value[:, start + LANES : start + 2 * LANES] if start + 2 * LANES <= width else part
            part = jnp.where(
                spot < LANES - shift, pltpu.roll(part, LANES - shift, 1), pltpu.roll(tail, LANES - shift, 1)
            )
        part = jnp.where(spot < rows, part, tally).astype(LOW)
        for expert in range(experts):
            sent[group * experts + expert] = jnp.broadcast_to(part, sent.shape[1:])


def place_of(me, rows, piece, width):
    natural = (rows[0:1] ^ me) * piece + rows[1:2]
    return (lax.broadcasted_iota(jnp.int32, (width, width), 0) == natural).astype(LOW)


def terms_body(spot_at, where, got, weight, bias, shared, out, loads):
    me, expert = where[0], where[1]
    total, _, _ = got.shape
    piece, wide = weight.shape
    rows = got[:, 0, :]
    pick = (
        lax.broadcasted_iota(jnp.int32, (LANES, piece), 0)
        == lax.broadcasted_iota(jnp.int32, (LANES, piece), 1) + expert * piece
    ).astype(LOW)
    share = bias.shape[1]
    spot = (
        lax.broadcasted_iota(jnp.int32, (share, wide), 1)
        == lax.broadcasted_iota(jnp.int32, (share, wide), 0) + me * share
    ).astype(LOW)
    terms = dot(dot(rows, pick).astype(LOW), weight[...]) + dot(bias[...], spot)
    terms = terms.astype(LOW)
    first = up_to(piece, 8)
    for at in range(wide // LANES):
        out[:, first + at, :] = terms[:, at * LANES : (at + 1) * LANES]
    cols = shared.shape[1] // total
    for at in range(total):
        out[at, :piece, :cols] = shared[:, at * cols : (at + 1) * cols]
        out[at, :piece, cols:] = jnp.zeros((piece, LANES - cols), LOW)
    experts = loads.shape[1]
    tally = pltpu.roll(jnp.sum(rows.astype(WIDE), axis=0, keepdims=True), LANES - spot_at, 1)
    valid = jnp.sum(
        jnp.where(lax.broadcasted_iota(jnp.int32, tally.shape, 1) == experts, tally, 0.0), axis=1, keepdims=True
    )
    loads[...] = (tally * experts / (2.0 * valid))[:, :experts]


def shift_body(piece, terms, weight, modulation, lines, shared):
    total = modulation.shape[1] // LANES
    first = up_to(piece, 8)
    sums = jnp.sum(terms[:, first : first + total, :].astype(WIDE), axis=0)
    for at in range(total):
        modulation[:, at * LANES : (at + 1) * LANES] = sums[at : at + 1]
    for at in range(terms.shape[0]):
        shared[at * piece : (at + 1) * piece] = terms[at, :piece]
    gate = total // 6
    lines[:, :8] = jnp.zeros((lines.shape[0], 8, LANES), WIDE)
    lines[:, :gate] = jnp.broadcast_to(sums[5 * gate :], (lines.shape[0], gate, LANES))
    lines[:, 8:] = jnp.broadcast_to(weight[...], (lines.shape[0], 8, LANES))


def head_pair(values, pair):
    both = values[:, pair * LANES : (pair + 1) * LANES]
    lane = lax.broadcasted_iota(jnp.int32, both.shape, 1)
    zero = jnp.zeros_like(both)
    return jnp.concatenate(
        [jnp.where(lane < HEAD_DIM, both, zero), jnp.where(lane < HEAD_DIM, zero, both)], axis=0
    )


def scores_of(queries, stacked, pair, length):
    count = queries.shape[0]
    raw = dot_nt(queries[:, pair * LANES : (pair + 1) * LANES], stacked) * HEAD_DIM ** (-0.5)
    lane = lax.broadcasted_iota(jnp.int32, raw.shape, 1)
    return jnp.where((lane & (count - 1)) < length, raw, -1e30)


def times(left, low, high, cols):
    half = low.shape[0]
    return dot(left[:, :half], low[:, cols]) + dot(left[:, half:], high[:, cols])


def times_back(left, low, high, cols):
    return jnp.concatenate([dot_nt(left, low[:, cols]), dot_nt(left, high[:, cols])], axis=1)


def forward_body(
    piece, where, tokens, modulation, lengths, rows0, rows1, low0, high0, low1, high1,
    both, joined, totals, attn_out, middle_out, *parts,
):
    count, width = tokens.shape
    length = lengths[0]
    mod = modulation[...]
    tok = tokens[...].astype(WIDE)
    unit, _ = center_of(tok)
    first = (unit * (1.0 + mod[:, width : 2 * width]) + mod[:, :width]).astype(LOW)
    both[:, :width] = first
    start = 0
    for rows, low, high in ((rows0, low0, high0), (rows1, low1, high1)):
        moved = dot(first, place_of(where[0], rows, piece, width)).astype(LOW)
        size = min(low.shape[1], 3 * width - start)
        joined[:, start : start + size] = times(moved, low, high, slice(0, size)).astype(LOW)
        start += size
    queries, keys, values = joined[:, :width], joined[:, width : 2 * width], joined[:, 2 * width :]
    lane = lax.broadcasted_iota(jnp.int32, (count, LANES), 1)
    sums = jnp.zeros((count, LANES), WIDE)
    for pair in range(HEADS // 2):
        scores = scores_of(queries, head_pair(keys, pair), pair, length)
        probs = []
        for one in range(2):
            mine = scores[:, one * count : (one + 1) * count]
            top = jnp.max(mine, axis=-1, keepdims=True)
            total = top + jnp.log(jnp.sum(jnp.exp(mine - top), axis=-1, keepdims=True))
            sums = jnp.where(lane == 2 * pair + one, total, sums)
            probs.append(jnp.exp(mine - total).astype(LOW))
        both[:, width + pair * LANES : width + (pair + 1) * LANES] = dot(
            jnp.concatenate(probs, axis=1), head_pair(values, pair)
        ).astype(LOW)
    totals[...] = sums
    moved = dot(both[:, width:], place_of(where[0], rows1, piece, width)).astype(LOW)
    attn = times(moved, low1, high1, slice(width, 2 * width))
    attn_out[...] = attn
    middle = tok + mod[:, 2 * width : 3 * width] * attn
    middle_out[...] = middle
    unit, _ = center_of(middle)
    second = (unit * (1.0 + mod[:, 4 * width : 5 * width]) + mod[:, 3 * width : 4 * width]).astype(LOW)
    start = 0
    for part in parts:
        part[...] = second[:, start : start + part.shape[1]]
        start += part.shape[1]


def backward_body(
    piece, where, tokens, cotangent, modulation, lengths, rows0, rows1, low0, high0, low1, high1,
    joined, totals, attn_in, middle_in, near0, far0, near1, far1,
    grad_tokens, lines, *refs,
):
    sents, (sent, d_rows, d_cols, d_mod) = refs[:-4], refs[-4:]
    count, width = tokens.shape
    length = lengths[0]
    mod = modulation[...]
    start = 0
    for low, high in ((near0, far0), (near1, far1)):
        size = low.shape[1]
        total = low[...].astype(WIDE) + high[...].astype(WIDE)
        d_rows[:, start : start + size] = total[:count]
        d_mod[:, 5 * width + start : 5 * width + start + size] = total[count : count + 1]
        start += size
    d_second = d_rows[...]
    attn = attn_in[...]
    unit, scale = center_of(middle_in[...])
    d_mod[:, 3 * width : 4 * width] = jnp.sum(d_second, axis=0, keepdims=True)
    d_mod[:, 4 * width : 5 * width] = jnp.sum(d_second * unit, axis=0, keepdims=True)
    d_middle = cotangent[...].astype(WIDE) + norm_back(
        d_second * (1.0 + mod[:, 4 * width : 5 * width]), unit, scale
    )
    d_mod[:, 2 * width : 3 * width] = jnp.sum(d_middle * attn, axis=0, keepdims=True)
    d_attn = (mod[:, 2 * width : 3 * width] * d_middle).astype(LOW)
    d_cols[:, 3 * width :] = d_attn
    d_attended = dot_nt(
        times_back(d_attn, low1, high1, slice(width, 2 * width)).astype(LOW), place_of(where[0], rows1, piece, width)
    ).astype(LOW)
    queries, keys, values = joined[:, :width], joined[:, width : 2 * width], joined[:, 2 * width :]
    sums = totals[...]
    lane = lax.broadcasted_iota(jnp.int32, (count, LANES), 1)
    factor = HEAD_DIM ** (-0.5)
    for pair in range(HEADS // 2):
        at = slice(pair * LANES, (pair + 1) * LANES)
        k_pair, v_pair = head_pair(keys, pair), head_pair(values, pair)
        scores = scores_of(queries, k_pair, pair, length)
        d_probs = dot_nt(d_attended[:, at], v_pair)
        probs_low, d_scores_low = [], []
        for one in range(2):
            half = slice(one * count, (one + 1) * count)
            total = jnp.sum(jnp.where(lane == 2 * pair + one, sums, 0.0), axis=1, keepdims=True)
            probs = jnp.exp(scores[:, half] - total)
            back = d_probs[:, half]
            d_scores = probs * (back - jnp.sum(probs * back, axis=-1, keepdims=True))
            probs_low.append(probs.astype(LOW))
            d_scores_low.append(d_scores.astype(LOW))
        d_scores_both = jnp.concatenate(d_scores_low, axis=1)
        d_cols[:, at] = (dot(d_scores_both, k_pair) * factor).astype(LOW)
        q_pair, d_pair = queries[:, at], d_attended[:, at]
        d_k = dot_tn(d_scores_both, q_pair) * factor
        d_v = dot_tn(jnp.concatenate(probs_low, axis=1), d_pair)
        d_k = jnp.where(lane < HEAD_DIM, d_k[:count], d_k[count:])
        d_v = jnp.where(lane < HEAD_DIM, d_v[:count], d_v[count:])
        d_cols[:, width + pair * LANES : width + (pair + 1) * LANES] = d_k.astype(LOW)
        d_cols[:, 2 * width + pair * LANES : 2 * width + (pair + 1) * LANES] = d_v.astype(LOW)
    d_first = jnp.zeros((count, width), WIDE)
    start = 0
    for rows, low, high in ((rows0, low0, high0), (rows1, low1, high1)):
        size = min(low.shape[1], 3 * width - start)
        part = times_back(d_cols[:, start : start + size], low, high, slice(0, size))
        start += size
        place = place_of(where[0], rows, piece, width)
        top = part.astype(LOW)
        rest = (part - top.astype(WIDE)).astype(LOW)
        d_first += dot_nt(top, place) + dot_nt(rest, place)
    unit, scale = center_of(tokens[...].astype(WIDE))
    d_mod[:, :width] = jnp.sum(d_first, axis=0, keepdims=True)
    d_mod[:, width : 2 * width] = jnp.sum(d_first * unit, axis=0, keepdims=True)
    grad_tokens[...] = d_middle + norm_back(
        d_first * (1.0 + mod[:, width : 2 * width]), unit, scale
    )
    for at in range(lines.shape[1]):
        line = d_mod[:, at * LANES : (at + 1) * LANES].astype(LOW)
        lines[:, at, :] = jnp.broadcast_to(line, (lines.shape[0], LANES))
    experts = sent.shape[0]
    cols, out_cols = 3 * width // experts, width // experts
    for expert in range(experts):
        to = expert ^ where[1]
        sent[to, :, :cols] = d_cols[:, expert * cols : (expert + 1) * cols]
        sent[to, :, cols:] = d_cols[:, 3 * width + expert * out_cols : 3 * width + (expert + 1) * out_cols]
    for to, out in enumerate(sents):
        out[...] = sent[to]


def join_rows(lows, highs, rows):
    start = 0
    half = rows.shape[0] // 2
    for low, high in zip(lows, highs):
        share = low.shape[-1]
        for at, part in enumerate((low, high)):
            rows[at * half : (at + 1) * half, start : start + share] = part[...].reshape(half, share)
        start += share


def item_of(where, links, at, block):
    core, outer, inner = links
    item = where[0] ^ (core[0] * at) ^ (inner[0] * block)
    for bit, mask in enumerate(outer):
        item = item ^ ((pl.program_id(0) >> bit & 1) * mask)
    return item


def d_act_body(links, where, low, high, lines, down, d_act, rows):
    count, width = low.shape[-2:]
    for at, part in enumerate((low, high)):
        for block in range(2):
            item = item_of(where, links, at, block)
            here = slice((2 * at + block) * count, (2 * at + block + 1) * count)
            for line in range(width // LANES):
                cols = slice(line * LANES, (line + 1) * LANES)
                rows[0, here, cols] = (
                    part[block, :, cols].astype(WIDE) * lines[item, line : line + 1]
                ).astype(LOW)
    d_act[0] = dot_nt(rows[0], down[...]).astype(LOW)


def hidden_body(links, routed, where, *refs):
    lows, highs, cots, (lines, d_act, up, down) = refs[:2], refs[2:4], refs[4:6], refs[6:10]
    back_lows, back_highs, branches, (d_pre, act, rows) = refs[10:12], refs[12:14], refs[14:16], refs[16:]
    join_rows(lows, highs, rows)
    count = rows.shape[0] // 4
    width = up.shape[0]
    expert = where[1]
    flat = lax.broadcasted_iota(jnp.int32, (count, count), 0) == lax.broadcasted_iota(jnp.int32, (count, count), 1)
    spare = lax.broadcasted_iota(jnp.int32, (EXTRA, width), 0)
    blocks = [(at, block) for at in range(2) for block in range(2)]
    weights = []
    for at, block in blocks:
        line = lines[item_of(where, links, at, block), pl.ds(8 + expert, 1)]
        weights.append(jnp.sum(jnp.where(flat, line, 0.0), axis=1, keepdims=True))
    weight = jnp.concatenate(weights, axis=0)
    pre = dot(rows[...], up[...])
    square = pre * pre
    bend = jnp.tanh(pre * (CURVE + (CURVE * CUBIC) * square))
    gate = 0.5 + 0.5 * bend
    hidden = pre * gate
    slope = gate + hidden * (1.0 - bend) * (CURVE + (3.0 * CURVE * CUBIC) * square)
    d_hidden = d_act[0].astype(WIDE)
    d_full = d_hidden * slope
    d_low = jnp.concatenate([d_full[:, :routed] * weight, d_full[:, routed:]], axis=1).astype(LOW)
    d_pre[0] = d_low
    act_low = jnp.concatenate([hidden[:, :routed] * weight, hidden[:, routed:]], axis=1).astype(LOW)
    act[0] = act_low
    pair = jnp.sum(hidden[:, :routed] * d_hidden[:, :routed], axis=1, keepdims=True)
    back = dot_nt(d_low, up[...]).astype(LOW)
    out = dot(act_low, down[...])
    for number, (at, block) in enumerate(blocks):
        one = slice(number * count, (number + 1) * count)
        body, extra = slice(0, count), slice(count, count + EXTRA)
        d_gate = jnp.sum(out[one] * cots[at][block].astype(WIDE), axis=0, keepdims=True)
        d_gate = jnp.where(spare == 0, d_gate, 0.0).astype(LOW)
        start = 0
        for ref in (back_lows, back_highs)[at]:
            size = ref.shape[-1]
            ref[block, body] = back[one, start : start + size]
            ref[block, extra] = d_gate[:, start : start + size]
            start += size
        ref = branches[at]
        ref[block, body] = out[one].astype(LOW)
        line = jnp.sum(jnp.where(flat, pair[one], 0.0), axis=0, keepdims=True)
        ref[block, extra] = jnp.zeros((EXTRA, width), LOW)
        ref[block, extra, :count] = jnp.where(spare[:, :count] == expert, line, 0.0).astype(LOW)


def up_grads_body(write, where, *refs):
    second, d_pre, outs, (rows, up_sum) = refs[:4], refs[4], refs[5:-2], refs[-2:]
    step = pl.program_id(0)

    @pl.when(step == 0)
    def _():
        up_sum[...] = jnp.zeros(up_sum.shape, WIDE)

    join_rows(second[:2], second[2:], rows)
    up_sum[...] += dot_tn(rows[...], d_pre[0])

    @pl.when(step == pl.num_programs(0) - 1)
    def _():
        write(where, up_sum, outs)


def down_grads_body(write, where, d_mlp, act, *refs):
    outs, down_sum = refs[:-1], refs[-1]
    step = pl.program_id(0)

    @pl.when(step == 0)
    def _():
        down_sum[...] = jnp.zeros(down_sum.shape, WIDE)

    down_sum[...] += dot_tn(act[0], d_mlp[0])

    @pl.when(step == pl.num_programs(0) - 1)
    def _():
        write(where, down_sum, outs)


def write_whole(where, total, outs):
    outs[0][...] = total[...]


def place_and_twin(where):
    return where[2] // 2, where[2] % 2


def rows_at(number, size):
    return pl.ds(pl.multiple_of(number * size, 16), size)


def lanes_at(number, size):
    return pl.ds(pl.multiple_of(number * size, LANES), size)


def up_sent_body(where, weight, near, away):
    place, _ = place_and_twin(where)
    for at in range(4):
        (near if at < 2 else away)[at % 2] = weight[:, lanes_at(place ^ at, near.shape[2])]


def up_join_body(where, own, shared, other, shared_other, full):
    place, twin = place_and_twin(where)
    rows, cols = own.shape[1], own.shape[2]
    for at, mask in enumerate((0, 2, 1, 3)):
        full[rows_at(2 * (place ^ mask) + twin, rows), :cols] = own[at]
        full[rows_at(2 * (place ^ mask) + 1 - twin, rows), :cols] = other[at]
    for at, piece in enumerate((shared, shared_other)):
        full[:, cols + at * LANES : cols + (at + 1) * LANES] = piece[...]


def down_join_body(where, own, other, full):
    _, twin = place_and_twin(where)
    rows = (full.shape[0] - 2 * LANES) // 2
    size = own.shape[0] - rows
    blank = jnp.zeros((LANES - size, full.shape[1]), LOW)
    for at, piece in enumerate((own, other)):
        full[rows_at(twin if at == 0 else 1 - twin, rows)] = piece[:rows]
        start = 2 * rows + at * LANES
        full[start : start + size] = piece[rows:]
        full[start + size : start + LANES] = blank


def write_up_twins(where, up_sum, outs):
    keep_up, send_up0, send_up1 = outs
    place, twin = place_and_twin(where)
    rows, units = keep_up.shape[1], up_sum.shape[1] - 2 * LANES
    size = (keep_up.shape[2] - units) // 2
    mine, other = slice(units, units + size), slice(units + LANES, units + LANES + size)
    for out, first, at_twin, order_ in (
        (keep_up, 0, twin, (mine, other)),
        (send_up0, 0, 1 - twin, (other, mine)),
        (send_up1, 2, 1 - twin, (other, mine)),
    ):
        for at in range(out.shape[0]):
            here = rows_at(2 * (place ^ (first + at)) + at_twin, rows)
            out[at, :, :units] = up_sum[here, :units].astype(LOW)
            for number, cols in enumerate(order_):
                start = units + number * size
                out[at, :, start : start + size] = up_sum[here, cols].astype(LOW)


def write_down_twins(where, down_sum, outs):
    keep_down, send_down = outs
    _, twin = place_and_twin(where)
    half = (down_sum.shape[0] - 2 * LANES) // 2
    size = keep_down.shape[0] - half
    start = 2 * half
    for out, at_twin, first in ((keep_down, twin, start), (send_down, 1 - twin, start + LANES)):
        out[:half] = down_sum[rows_at(at_twin, half)].astype(out.dtype)
        out[half:] = down_sum[first : first + size].astype(out.dtype)


def twin_up_body(keep, got0, got1, *ups):
    for at, out in enumerate(ups):
        got = (got0, got1)[at // 2][at % 2]
        out[...] = (keep[at].astype(WIDE) + got.astype(WIDE)).astype(LOW)


def twin_down_body(keep, got, grad_down, shared_down):
    half = grad_down.shape[0]
    grad_down[...] = keep[:half] + got[:half].astype(WIDE)
    shared_down[...] = (keep[half:] + got[half:].astype(WIDE)).astype(LOW)


def up_rows_body(where, up0, up1, up2, up3, shared_down, grad_up, sent):
    place, twin = place_and_twin(where)
    expert = where[1]
    units = grad_up.shape[1] // 4
    size = (up0.shape[1] - units) // 2
    cols = sent.shape[2] - 2 * size
    for at, piece in enumerate((up0, up1, up2, up3)):
        grad_up[:, lanes_at(place ^ at, units)] = piece[:, :units].astype(WIDE)
        mine, other = piece[:, units : units + size], piece[:, units + size :]
        sent[(place ^ at) ^ expert, :, :size] = jnp.where(twin == 0, mine, other)
        sent[(place ^ at) ^ expert, :, size : 2 * size] = jnp.where(twin == 0, other, mine)
    for to in range(4):
        sent[to ^ expert, :, 2 * size :] = shared_down[:, to * cols : (to + 1) * cols]


def shared_rows_body(where, got0, got1, got2, got3, grad_up, grad_down, held):
    expert = where[1]
    for at, got in enumerate((got0, got1, got2, got3)):
        held[at ^ expert] = got[...]
    size = grad_up.shape[1] // 8
    for source in range(4):
        for twin in range(2):
            start = (4 * twin + source) * size
            grad_up[:, start : start + size] = held[source, :, twin * size : (twin + 1) * size].astype(WIDE)
        grad_down[source * size : (source + 1) * size] = held[source, :, 2 * size :].astype(WIDE)


def attn_terms_body(masks, where, both0, both1, both2, both3, cols0, cols1, cols2, cols3, low0, low1, high0, high1, term):
    group = where[2]
    width = both0.shape[1] // 2
    cut = 3 * width // 4
    rows = low0.shape[1]
    pairs = zip((both0, both1, both2, both3), (cols0, cols1, cols2, cols3))
    for at, (inputs, cols) in enumerate(pairs):
        parts = (dot_tn(inputs[:, :width], cols[:, :cut]), dot_tn(inputs[:, width:], cols[:, cut:]))
        for start, part in ((0, parts[0]), (cut, parts[1])):
            here = slice(start, start + part.shape[1])
            if at:
                term[:, here] += part
            else:
                term[:, here] = part
    half = width // 2
    for number, (low, high) in enumerate(((low0, high0), (low1, high1))):
        for at, mask in enumerate(masks[number]):
            ref = low if at < 4 else high
            ref[at % 4] = term[rows_at(group ^ mask, rows), number * half : (number + 1) * half].astype(LOW)


def attn_out_body(near0, far0, near1, far1, grad_qkv, grad_out, total):
    half = near0.shape[1]
    for at, (near, far) in enumerate(((near0, far0), (near1, far1))):
        total[:, at * half : (at + 1) * half] = near[...].astype(WIDE) + far[...].astype(WIDE)
    cut = grad_qkv.shape[1]
    grad_qkv[...] = total[:, :cut]
    grad_out[...] = total[:, cut:]


def finish_body(modulation, middle, kept, low, high, block_out, grad_gates, total):
    count, width = middle.shape
    total[...] = low[...].astype(WIDE) + high[...].astype(WIDE)
    block_out[...] = middle[...] + modulation[:, 5 * width :] * total[:count]
    pairs = total[count : count + 8, :count]
    for choice in range(2):
        grad_gates[choice : choice + 1] = jnp.sum(kept[choice] * pairs, axis=0, keepdims=True)


def ada_body(experts, where, got, cond, weight, grad_weight, grad_bias, sent, d_mod):
    expert = where[1]
    total, lines, _ = got.shape
    for at in range(lines):
        d_mod[:, at * LANES : (at + 1) * LANES] = got[:, at, :]
    grad_bias[...] = jnp.sum(d_mod[...].astype(WIDE), axis=0)
    cols = grad_weight.shape[1]
    mine = d_mod[:, pl.ds(pl.multiple_of(expert * cols, LANES), cols)]
    grad_weight[...] = dot_tn(cond[:, 0, :], mine)[: grad_weight.shape[0]]
    piece = weight.shape[0]
    back = dot_nt(d_mod[...], weight[...])
    sent[...] = jnp.zeros(sent.shape, WIDE)
    sent[:, 0, :piece] = back


def attn_grads_body(both, d_cols, out):
    experts, count, cols = d_cols.shape
    width = both.shape[2] // 2
    groups, rows, _ = out.shape
    flat = d_cols[...].reshape(experts * count, cols)
    inputs = both[...].reshape(experts * count, 2 * width)
    cut = 3 * cols // 4
    out[...] = jnp.concatenate(
        [dot_tn(inputs[:, :width], flat[:, :cut]), dot_tn(inputs[:, width:], flat[:, cut:])], axis=1
    ).astype(LOW).reshape(groups, rows, cols)


def attn_sum_body(got, grad_qkv, grad_out):
    total = jnp.sum(got[...].astype(WIDE), axis=0)
    cut = grad_qkv.shape[1]
    grad_qkv[...] = total[:, :cut]
    grad_out[...] = total[:, cut:]


def up_out_body(units, got, grad_up):
    for group in range(got.shape[0]):
        grad_up[:, group * units : (group + 1) * units] = got[group, :, :units].astype(WIDE)


def gather_far(pieces, masks):
    found = [pieces]
    for mask in masks:
        found = found + [[swap(piece, mask) for piece in held] for held in found]
    return found


def shards(
    tokens,
    cond,
    lengths,
    routes,
    gate_weights,
    ada_weight,
    ada_bias,
    qkv_weight,
    out_weight,
    shared_up,
    shared_down,
    expert_up,
    expert_down,
    cotangent,
):
    count, width = tokens.shape
    experts = lax.axis_size("expert")
    groups = lax.axis_size("batch")
    total = experts * groups
    me = lax.axis_index(AXES)
    my_expert = lax.axis_index("expert")
    my_group = lax.axis_index("batch")
    where = jnp.stack([me, my_expert, my_group]).astype(jnp.int32)
    capacity = 5 * 2 * count // (4 * experts)
    piece = ada_weight.shape[0]
    group_rows = width // groups
    shared_units = shared_down.shape[0]
    units = expert_down.shape[1]
    shares = [width // 2, width // 2]
    tall = (count, width)
    lines = 6 * width // LANES

    expert_masks = bits_of(experts)
    group_masks = [experts * step for step in bits_of(groups)]
    away = list(reversed(group_masks[1:3]))
    far = group_masks[:1] + group_masks[3:]
    core, across = expert_masks[:1], expert_masks[1:]
    team_links = [away + across, across + away]
    inner, outer = away[:1], across + away[1:]
    links = (core, outer, inner)
    steps = 2 ** len(outer)
    weight_links = [far[1:] + away + far[:1] + across, far[1:] + away + across + far[:1]]
    paired = groups == 8 and experts == 4
    room = 20 if paired else 48
    away_masks = order(sorted(away))

    pair_weight, kept, sent = call(
        functools.partial(route_body, experts, capacity, groups),
        [((8, count), WIDE), ((2, 8, count), WIDE), ((total, 16, LANES), LOW)],
        (routes.T, gate_weights.T, lengths, cond),
        smem=(2,),
    )
    cond_all = lax.all_to_all(sent, AXES, split_axis=0, concat_axis=0, tiled=True)

    attn_w = jnp.concatenate([qkv_weight, out_weight], axis=1)[None]
    cot = cotangent[None]
    down_own = jnp.concatenate([expert_down[0], shared_down], axis=0)
    down_other = swap(down_own, far[0])
    first_links = far[1:] + away
    cot_got = swap(cot, away[0])
    attn_w, cot_got = together(attn_w, cot_got)
    cot = grown(cot, cot_got)
    for at, mask in enumerate(first_links):
        attn_got = swap(attn_w, mask)
        if at == 0:
            attn_got, cond_all = together(attn_got, cond_all)
            terms, loads = call(
                functools.partial(terms_body, group_rows),
                [((total, up_to(up_to(piece, 8) + lines, 8), LANES), LOW), ((1, experts), WIDE)],
                (where, cond_all, ada_weight, ada_bias[None], shared_up),
                smem=(0,),
            )
            terms_got = lax.all_to_all(terms, AXES, split_axis=0, concat_axis=0, tiled=True)
        if at == len(first_links) - 1:
            attn_got, terms, down_other = together(attn_got, terms, down_other)
        attn_w = grown(attn_w, attn_got)
    cot_links = away + across
    attn_parts = [attn_w[:, :, : 2 * width], attn_w[:, :, 2 * width :]]
    last_links = [far[:1] + across, across + far[:1]]
    weight_links = [first_links + masks for masks in last_links]
    if paired:
        place_units = expert_up.shape[2] // 4
        up_near, up_away = call(
            up_sent_body, [((2, group_rows, place_units), LOW)] * 2, (where, expert_up[0]), smem=(0,)
        )
    for at in range(len(last_links[0])):
        got = [swap(part, masks[at]) for part, masks in zip(attn_parts, last_links)]
        if at == 0:
            if paired:
                up_got = swap(up_away, away[0])
        elif at == len(last_links[0]) - 1:
            cot_got = swap(cot, away[1])
            got, cot_got, terms_got = together(got, cot_got, terms_got)
            if paired:
                got, up_got = together(got, up_got)
            cot = grown(cot, cot_got)
        attn_parts = [grown(*pair) for pair in zip(attn_parts, got)]
    modulation, own_lines, part_shared_up = call(
        functools.partial(shift_body, piece),
        [((1, 6 * width), WIDE), ((total, 16, LANES), WIDE), ((width, LANES), LOW)],
        (terms_got, pair_weight),
    )
    attn_far = [swap(part, core[0]) for part in attn_parts]
    cot_got = swap(cot, across[0])
    if paired:
        up_mine = jnp.stack([up_near[0], up_got[0]])
        up_sent = jnp.stack([up_near[1], up_got[1]])
        up_last = swap(up_sent, away[1])
        shared_up_other = swap(part_shared_up, far[0])
    weights = []
    row_places = []
    for low, high, masks in zip(attn_parts, attn_far, weight_links):
        weights += [low.reshape(-1, 2 * width), high.reshape(-1, 2 * width)]
        found = np.repeat(np.array(order(masks + core), np.int32), piece)
        row_places.append(jnp.asarray(np.stack([found, np.tile(np.arange(piece, dtype=np.int32), total)])))

    both, joined, totals, attn, middle, *seconds = call(
        functools.partial(forward_body, piece),
        [
            ((count, 2 * width), LOW),
            ((count, 3 * width), LOW),
            ((count, LANES), WIDE),
            (tall, WIDE),
            (tall, WIDE),
            *[((count, share), LOW) for share in shares],
        ],
        (where, tokens, modulation, lengths, *row_places, *weights),
        smem=(0, 3),
    )

    shared_slot = up_to(shared_units, LANES)
    second_low = [part[None] for part in seconds]
    for at in range(len(away + across)):
        got = [swap(part, masks[at]) for part, masks in zip(second_low, team_links)]
        if at == 0:
            item_lines = lax.all_to_all(own_lines, AXES, split_axis=0, concat_axis=0, tiled=True)
            if paired:
                got, up_last, shared_up_other = together(got, up_last, shared_up_other)
                up_own = jnp.concatenate([up_mine, up_last], axis=0)
                up_other = swap(up_own, far[0])
        elif at == 1:
            if paired:
                got, up_other, cot_got, item_lines = together(got, up_other, cot_got, item_lines)
                routed, hidden = 2 * units, 2 * units + 2 * shared_slot
                (down_cat,) = call(
                    down_join_body, [((hidden, width), LOW)], (where, down_own, down_other), smem=(0,)
                )
        second_got = got
        if at < len(away + across) - 1:
            second_low = [grown(*pair) for pair in zip(second_low, got)]
    if paired:
        (up_cat,) = call(
            up_join_body,
            [((width, hidden), LOW)],
            (where, up_own, part_shared_up, up_other, shared_up_other),
            smem=(0,),
        )
    else:
        part_up = lax.all_to_all(expert_up[0], "batch", split_axis=1, concat_axis=0, tiled=True)
        held = gather_far([part_up, part_shared_up[:, :shared_units], expert_down[0], shared_down], far)
        slot = up_to(units, LANES)
        routed, hidden = len(held) * slot, len(held) * (slot + shared_slot)
        up_cat = jnp.concatenate(
            [pad_lanes(h[0], slot) for h in held] + [pad_lanes(h[1], shared_slot) for h in held], axis=1
        )
        down_cat = jnp.concatenate(
            [pad_lanes(h[2].T, slot).T for h in held] + [pad_lanes(h[3].T, shared_slot).T for h in held], axis=0
        )

    half = 2 * count

    def whole(array):
        return array, array.shape, lambda step: (0,) * array.ndim

    def block_at(masks, rows, lanes):
        bits = list(reversed(masks))
        block = tuple(2 if mask in inner else None for mask in bits) + (rows, lanes)

        def index(step):
            spot = {mask: step // 2**at % 2 for at, mask in enumerate(outer)}
            return tuple(spot.get(mask, 0) for mask in bits) + (0, 0)

        return block, index

    def block_in(array, masks):
        laid = array.reshape((2,) * len(masks) + array.shape[1:])
        return laid, *block_at(masks, *array.shape[1:])

    def block_out_of(rows, lanes, masks):
        return (2,) * len(masks) + (rows, lanes), LOW, *block_at(masks, rows, lanes)

    def rows_of(array):
        return array, (1,) + array.shape[1:], lambda step: (step, 0, 0)

    def rows_out(lanes):
        return (steps, 2 * half, lanes), LOW, (1, 2 * half, lanes), lambda step: (step, 0, 0)

    def sum_out(shape, kind):
        return shape, kind, shape, lambda step: (0,) * len(shape)

    def flat(part):
        return part.reshape((-1,) + part.shape[-2:])

    scalars = (where, None, None)

    cot_low = grown(cot, tie(cot_got, *second_low))
    for mask in across[1:]:
        cot_low = grown(cot_low, swap(cot_low, mask))
    cot_high = swap(cot_low, core[0])
    cots = [block_in(cot_low, cot_links), block_in(cot_high, cot_links)]
    d_act, d_mlp = sweep(
        functools.partial(d_act_body, links),
        steps,
        [scalars, *cots, whole(item_lines), whole(down_cat)],
        [rows_out(hidden), rows_out(width)],
        limit=room,
    )
    second_got, d_act, up_cat = together(second_got, d_act, up_cat)
    second_low = [grown(*pair) for pair in zip(second_low, second_got)]
    second_high = [swap(part, core[0]) for part in second_low]
    second_in = [block_in(part, masks) for parts in (second_low, second_high) for part, masks in zip(parts, team_links)]

    tall_rows = count + EXTRA
    back = [block_out_of(tall_rows, share, masks) for share, masks in zip(shares, team_links)]
    side = block_out_of(tall_rows, width, away + across)
    *parts, d_pre, act = sweep(
        functools.partial(hidden_body, links, routed),
        steps,
        [scalars, *second_in, *cots, whole(item_lines), rows_of(d_act), whole(up_cat), whole(down_cat)],
        [*back, *back, side, side, rows_out(hidden), rows_out(hidden)],
        scratch=[((2 * half, width), LOW)],
        limit=room,
    )
    parts = [flat(part) for part in parts]
    if paired:
        both_sent = tie(both, *second_high)
        both_group = [swap(both_sent, mask) for mask in range(1, 4)]
        parts, both_group = together(parts, both_group)
        both_group = [both] + both_group
    if paired:
        up_lanes = place_units + 2 * shared_units
        up_outs = [sum_out((blocks, group_rows, up_lanes), LOW) for blocks in (4, 2, 2)]
        down_outs = [sum_out((units + shared_units, width), kind) for kind in (WIDE, LOW)]
    else:
        up_outs, down_outs = [sum_out((width, hidden), WIDE)], [sum_out((hidden, width), WIDE)]
    up_grads = sweep(
        functools.partial(up_grads_body, write_up_twins if paired else write_whole),
        steps,
        [scalars, *second_in, rows_of(d_pre)],
        up_outs,
        scratch=[((2 * half, width), LOW), ((width, hidden), WIDE)],
        limit=room,
    )
    down_grads = sweep(
        functools.partial(down_grads_body, write_down_twins if paired else write_whole),
        steps,
        [scalars, rows_of(d_mlp), rows_of(act)],
        down_outs,
        scratch=[((hidden, width), WIDE)],
        limit=room,
    )

    lows, highs, orders = list(parts[:2]), list(parts[2:4]), [masks + core for masks in team_links]
    out_low, out_high, out_order = parts[4], parts[5], away + across + core
    sums_at = len(orders[0]) - 1
    out_got = swap(out_high, core[0])
    for at in range(sums_at + 1):
        got = [swap(high, masks[-1 - at]) for high, masks in zip(highs, orders)]
        if at == 0:
            got, up_grads = together(got, list(up_grads))
            if paired:
                keep_up, send_up0, send_up1 = up_grads
                twin_up0 = swap(send_up0, far[0])
        elif at == 1:
            got, down_grads, out_got = together(got, list(down_grads), out_got)
            if paired:
                keep_down, send_down = down_grads
                got, twin_up0 = together(got, twin_up0)
                twin_up1 = swap(send_up1, far[0])
        elif at == 2 and paired:
            out_got = swap(out_send0, across[0])
            got, out_got, twin_up1 = together(got, out_got, twin_up1)
            twin_down = swap(tie(send_down, twin_up1), far[0])
        elif at == sums_at and paired:
            out_got1 = swap(out_send1, across[0])
            got = list(together(*got))
        else:
            got = together(*got)
        if at < sums_at:
            pairs = [added(low, other) for low, other in zip(lows, got)]
            lows, highs = [pair[0] for pair in pairs], [pair[1] for pair in pairs]
        if at == 1 and paired:
            block = out_low.shape[1:]
            out_low, out_send0, out_send1 = call(
                add_split_body,
                [((4, *block), LOW), ((2, *block), LOW), ((2, *block), LOW)],
                (out_low, out_got),
            )
        elif at == 1:
            for mask in reversed((away + across)):
                out_low, out_high = added(out_low, out_got)
                out_got = swap(out_high, mask)
    folded = [half_[0] for pair in zip(lows, got) for half_ in pair]
    if paired:
        up_own = call(twin_up_body, [((group_rows, up_lanes), LOW)] * 4, (keep_up, twin_up0, twin_up1))
        folded, up_own = together(folded, up_own)
        up_got = [piece_ if not at else swap(piece_, away_masks[at]) for at, piece_ in enumerate(up_own)]

    sent_cols = (count, 4 * width // experts)
    grad_tokens, d_mod_sent, *d_cols = call(
        functools.partial(backward_body, piece),
        [(tall, WIDE), ((total, lines, LANES), LOW), *[(sent_cols, LOW)] * experts],
        (
            where, tokens, cotangent, modulation, lengths, *row_places, *weights,
            joined, totals, attn, middle, *folded,
        ),
        scratch=[((experts, *sent_cols), LOW), (tall, WIDE), ((count, 4 * width), LOW), ((1, 6 * width), WIDE)],
        smem=(0, 4),
    )

    if paired:
        d_cols, up_got[2], out_got1 = together(d_cols, up_got[2], out_got1)
        cols_got = [d_cols[at] if not at else swap(d_cols[at], at) for at in range(4)]
        out_low, out_high = call(
            add_join_body, [((2, *block), LOW), ((2, *block), LOW)], (out_low, out_got, out_got1)
        )
        out_got = swap(out_high, away[1])
        twin_down = tie(twin_down, cols_got[1], up_got[3])
        grad_expert_down, shared_own = call(
            twin_down_body, [((units, width), WIDE), ((shared_units, width), LOW)], (keep_down, twin_down)
        )
        d_mod_sent = tie(d_mod_sent, shared_own)
        after = tie(where, shared_own, *up_got)
        d_mod_all = lax.all_to_all(d_mod_sent, AXES, split_axis=0, concat_axis=0, tiled=True)
        grad_ada_weight, grad_ada_bias, sent = call(
            functools.partial(ada_body, experts),
            [((group_rows, 6 * width // experts), WIDE), ((6 * width,), WIDE), ((total, 8, LANES), WIDE)],
            (where, d_mod_all, cond_all, ada_weight),
            scratch=[((total, 6 * width), LOW)],
            smem=(0,),
        )
        sum_links = [away + far, away[:1] + far + away[1:]]
        sum_masks = [[mask // experts for mask in order(masks)] for masks in sum_links]
        term_half = ((4, group_rows, width // 2), LOW)
        attn_sent = call(
            functools.partial(attn_terms_body, sum_masks),
            [term_half] * 4,
            (after, *both_group, *cols_got),
            scratch=[((width, width), WIDE)],
            smem=(0,),
        )
        term_lows, term_highs = attn_sent[:2], attn_sent[2:]
        for at in range(3):
            got = [swap(high, masks[-1 - at]) for high, masks in zip(term_highs, sum_links)]
            if at == 0:
                got, out_got, up_got = together(got, out_got, up_got)
                out_low, out_high = added(out_low, out_got)
                out_got = swap(out_high, away[0])
            elif at == 1:
                got, sent = together(got, sent)
                grad_expert_up, crossed = call(
                    up_rows_body,
                    [
                        ((group_rows, groups * units), WIDE),
                        ((4, group_rows, 2 * shared_units + width // experts), LOW),
                    ],
                    (where, *up_got, shared_own),
                    smem=(0,),
                )
                got, crossed = together(got, crossed)
                crossed = [crossed[mask] if not mask else swap(crossed[mask], mask) for mask in range(4)]
            else:
                got, out_got, crossed = together(got, out_got, crossed)
            if at < 2:
                pairs = [added(low, other) for low, other in zip(term_lows, got)]
                term_lows, term_highs = [pair[0] for pair in pairs], [pair[1] for pair in pairs]
        grad_qkv, grad_out = call(
            attn_out_body,
            [((group_rows, 3 * width // experts), WIDE), ((group_rows, width // experts), WIDE)],
            [half_[0] for pair in zip(term_lows, got) for half_ in pair],
            scratch=[((group_rows, width), WIDE)],
        )
    else:
        d_mod_all = lax.all_to_all(d_mod_sent, AXES, split_axis=0, concat_axis=0, tiled=True)
        grad_ada_weight, grad_ada_bias, sent = call(
            functools.partial(ada_body, experts),
            [((group_rows, 6 * width // experts), WIDE), ((6 * width,), WIDE), ((total, 8, LANES), WIDE)],
            (where, d_mod_all, cond_all, ada_weight),
            scratch=[((total, 6 * width), LOW)],
            smem=(0,),
        )
        natural = jnp.arange(experts, dtype=jnp.int32) ^ my_expert
        both_group = lax.all_gather(both, "expert", axis=0)
        d_cols = jnp.take(jnp.stack(d_cols), natural, axis=0)
        d_cols = lax.all_to_all(d_cols, "expert", split_axis=0, concat_axis=0, tiled=True)
        (attn_terms,) = call(
            attn_grads_body, [((groups, group_rows, 4 * width // experts), LOW)], (both_group, d_cols)
        )
        attn_terms = lax.all_to_all(attn_terms, "batch", split_axis=0, concat_axis=0, tiled=True)
        grad_qkv, grad_out = call(
            attn_sum_body,
            [((group_rows, 3 * width // experts), WIDE), ((group_rows, width // experts), WIDE)],
            (attn_terms,),
        )

    block_out, grad_gate_weights = call(
        finish_body,
        [(tall, WIDE), ((2, count), WIDE)],
        (modulation, middle, kept, out_low[0], out_got[0]),
        scratch=[((tall_rows, width), WIDE)],
    )

    if paired:
        grad_shared_up, grad_shared_down = call(
            shared_rows_body,
            [((group_rows, width), WIDE), ((experts * shared_units, width // experts), WIDE)],
            (where, *crossed),
            scratch=[((4, group_rows, 2 * shared_units + width // experts), LOW)],
            smem=(0,),
        )
    else:
        (grad_up,), (grad_down,) = up_grads, down_grads
        replicas = hidden // (slot + shared_slot)
        sums = []
        for taken, size, first in ((grad_up.T, units, 0), (grad_up.T, shared_units, routed), (grad_down, units, 0), (grad_down, shared_units, routed)):
            room = up_to(size, LANES)
            held = [taken[first + at * room : first + at * room + size] for at in range(replicas)]
            for mask in reversed(far):
                some = len(held) // 2
                held = [
                    low + swap(high.astype(LOW), mask).astype(WIDE) for low, high in zip(held[:some], held[some:])
                ]
            sums.append(held[0])
        grad_expert_down = sums[2]
        up_rows = jnp.concatenate([sums[0].T, sums[1].T], axis=1).astype(LOW).reshape(groups, group_rows, -1)
        up_rows = lax.all_to_all(up_rows, "batch", split_axis=0, concat_axis=0, tiled=True)
        grad_shared_down = lax.all_to_all(
            sums[3].astype(LOW), "expert", split_axis=1, concat_axis=0, tiled=True
        ).astype(WIDE)
        (grad_expert_up,) = call(
            functools.partial(up_out_body, units), [((group_rows, groups * units), WIDE)], (up_rows,)
        )
        shared_rows = up_rows[:, :, units:].reshape(experts, groups // experts, group_rows, shared_units)
        shared_rows = lax.all_to_all(shared_rows, "expert", split_axis=0, concat_axis=0, tiled=True)
        grad_shared_up = shared_rows.transpose(2, 1, 0, 3).reshape(group_rows, groups * shared_units).astype(WIDE)

    d_cond_act = lax.all_to_all(sent, AXES, split_axis=0, concat_axis=0, tiled=True)
    d_cond_act = d_cond_act[:, 0, :piece].reshape(1, width)
    _, silu_back = jax.vjp(jax.nn.silu, cond.astype(WIDE))
    grad_cond = silu_back(d_cond_act)[0]

    return (
        block_out,
        grad_tokens,
        grad_cond,
        grad_gate_weights.T,
        grad_ada_weight,
        grad_ada_bias,
        grad_qkv,
        grad_out,
        grad_shared_up,
        grad_shared_down,
        grad_expert_up[None],
        grad_expert_down[None],
        loads.reshape(experts),
    )


def solution(mesh):
    rows = P(AXES, None)
    line = P(AXES)
    tiles = P("batch", "expert")
    split = P("expert", "batch", None)
    in_specs = (rows, rows, line, rows, rows, rows, line, rows, rows, rows, rows, split, split, rows)
    out_specs = (rows, rows, rows, rows, tiles, P(), tiles, tiles, tiles, tiles, split, split, P())
    return jax.shard_map(shards, mesh=mesh, in_specs=in_specs, out_specs=out_specs, check_vma=False)
```
